256 devices in a mesh: group: 4 (over x), brick: 64 (over z, y, core).
Axes of the slice: x: 4, y: 4, z: 8, core: 2. Of those that a mesh axis runs over, the one named last changes fastest.
Arguments:
- initial_field: float32 [128, 512, 512], P('group', 'brick'), may hold values from 0 to 3
- mass: float32 [128, 512, 512], P('group', 'brick'), may hold values from 0.02 to 0.6
- source: float32 [128, 512, 512], P('group', 'brick'), may hold values from -8 to 8
- sweeps: int32 [4], replicated, may hold values from 2 to 4, as said below
Outputs:
- fine_field: float32 [128, 512, 512], P('group', 'brick')
- mid_field: float32 [64, 256, 256], P('group', 'brick')
- coarse_field: float32 [32, 128, 128], P(None, 'brick')
- coarsest_field: float32 [16, 4096], replicated
The draws below stay inside these ranges and needn't reach their ends.
Inputs may be any that keep to these rules, and one draw needn't show every extreme that they name: One level takes exactly 4 sweeps and another exactly 2.
All inputs are finite; a program needn't handle non-finite values.
Results may differ from the reference program's by a relative error of at most 0.000027.
Values sent between devices are 32-bit elements; how exact they have to be, the bound alone decides.
No kernel may reach another device: no remote copies, remote signals or barrier semaphores. Data moves between devices by JAX's collectives and lax.ppermute only.
A program may use at most 128 MiB of HBM per device.

```python
import math
import jax
import jax.numpy as jnp
from jax import lax

SWEEPS = 4
LEVELS = 4
NX = 128
NY = 512
NZ = 512


def draw_sweeps(key, part):
    key = jax.random.fold_in(key, 7)
    counts = jax.random.randint(jax.random.fold_in(key, 1), (LEVELS,), 2, SWEEPS + 1)
    chosen = jax.random.randint(jax.random.fold_in(key, 2), (), 0, LEVELS)
    counts = counts.at[chosen].set(SWEEPS)
    counts = counts.at[(chosen + 1) % LEVELS].set(2)
    return counts.astype(jnp.int32)


def draw_initial_field(key, part):
    key = jax.random.fold_in(key, 11)
    shape = (NX, NY, NZ)
    values = 1.5 + 0.5 * jnp.clip(jax.random.normal(key, shape, jnp.float32), -3.0, 3.0)
    return values.astype(jnp.float32)


def levels(stream_key, dims, split, low, high):
    level, own = 1.0, jax.random.fold_in(stream_key, 6)
    for axis_at, parts in split:
        heights = jnp.exp(jax.random.uniform(jax.random.fold_in(own, axis_at), (parts,), jnp.float32, low / len(split), high / len(split)))
        level = level * jnp.repeat(heights, dims[axis_at] // parts).reshape([-1 if axis == axis_at else 1 for axis in range(len(dims))])
    return level


def bell_draw(stream_key, shape, deviation, bound, split=(), dtype=jnp.bfloat16):
    loudness = levels(stream_key, shape, split, -0.22, 0.18) if split else 1.0
    array = jax.random.normal(stream_key, shape, jnp.float32) * deviation * loudness
    return jnp.minimum(jnp.maximum(array, -bound), bound).astype(dtype)


def setup_inputs(seed: int = 0) -> dict:
    streams_of = jax.random.split(jax.random.key(seed), 5)
    initial_field = draw_initial_field(jax.random.fold_in(streams_of[4], 71), 0)
    mass = jnp.clip(jnp.exp(math.log(0.6) - 3.4011974 * jax.random.uniform(streams_of[1], (NX, NY, NZ), jnp.float32) ** levels(streams_of[1], (NX, NY, NZ), ((0, 4), (1, 64)), -0.2, 0.2)), 0.02, 0.6)
    source = bell_draw(streams_of[2], (NX, NY, NZ), 1.0, 8.0, ((0, 4), (1, 64)), jnp.float32)
    sweeps = draw_sweeps(jax.random.fold_in(streams_of[4], 71), 0)
    return {"initial_field": initial_field, "mass": mass, "source": source, "sweeps": sweeps}


def apply_operator(field, mass, source, inv_h2):
    beside_all = jnp.roll(field, -1, 0) + jnp.roll(field, 1, 0)
    beside_all = beside_all + jnp.roll(field, -1, 1) + jnp.roll(field, 1, 1)
    beside_all = beside_all + jnp.roll(field, -1, 2) + jnp.roll(field, 1, 2)
    return inv_h2 * (6.0 * field - beside_all) + mass * (field * field * field + field) - source


def parity_grid(shape):
    total = lax.broadcasted_iota(jnp.int32, shape, 0) + lax.broadcasted_iota(jnp.int32, shape, 1)
    total = total + lax.broadcasted_iota(jnp.int32, shape, 2)
    return total % 2


def relax(field, mass, source, inv_h2, parity, colour):
    value = apply_operator(field, mass, source, inv_h2)
    slope = 6.0 * inv_h2 + mass * (3.0 * field * field + 1.0)
    return jnp.where(parity == colour, field - value / slope, field)


def smooth(field, mass, source, inv_h2, count):
    parity = parity_grid(field.shape)

    def sweep(step, current):
        current = relax(current, mass, source, inv_h2, parity, 0)
        return relax(current, mass, source, inv_h2, parity, 1)

    return lax.fori_loop(0, count, sweep, field)


def restrict(field):
    rows, cols, depth = field.shape
    return field.reshape(rows // 2, 2, cols // 2, 2, depth // 2, 2).sum(axis=(1, 3, 5)) * 0.125


def descend(field, mass, source, inv_h2):
    defect = -apply_operator(field, mass, source, inv_h2)
    coarse_mass = restrict(mass)
    guess = restrict(field)
    coarse_source = restrict(defect) + apply_operator(guess, coarse_mass, 0.0, inv_h2 * 0.25)
    return guess, coarse_mass, coarse_source


def reference(initial_field, mass, source, sweeps):
    fine_field = smooth(initial_field, mass, source, 1.0, sweeps[0])
    guess, mass_one, source_one = descend(fine_field, mass, source, 1.0)
    mid_field = smooth(guess, mass_one, source_one, 0.25, sweeps[1])
    guess, mass_two, source_two = descend(mid_field, mass_one, source_one, 0.25)
    coarse_field = smooth(guess, mass_two, source_two, 0.0625, sweeps[2])
    guess, mass_three, source_three = descend(coarse_field, mass_two, source_two, 0.0625)
    coarsest = smooth(guess, mass_three, source_three, 0.015625, sweeps[3])
    return fine_field, mid_field, coarse_field, coarsest.reshape(coarsest.shape[0], -1)
```

```python
import functools

import jax
import jax.numpy as jnp
from jax import lax
from jax.experimental import pallas as pl
from jax.experimental.pallas import tpu as pltpu
from jax.sharding import PartitionSpec as P


INTERPRET = False
VMEM = 60 * 1024 * 1024
LANES = 128


def call(kernel, out_shapes, args, scratch=(), scalars=0):
    spec = pl.BlockSpec(memory_space=pltpu.VMEM)
    smem = pl.BlockSpec(memory_space=pltpu.SMEM)
    return pl.pallas_call(
        kernel,
        out_shape=[jax.ShapeDtypeStruct(shape, jnp.float32) for shape in out_shapes],
        in_specs=[smem] * scalars + [spec] * (len(args) - scalars),
        out_specs=[spec] * len(out_shapes),
        scratch_shapes=[pltpu.VMEM(shape, jnp.float32) for shape in scratch],
        compiler_params=pltpu.CompilerParams(vmem_limit_bytes=VMEM),
        interpret=INTERPRET,
    )(*args)


def iota(shape, axis):
    return lax.broadcasted_iota(jnp.int32, shape, axis)


def odd(shape, period=None):
    rows = iota(shape, 0)
    if period is not None:
        rows = rows % period
    return ((rows + iota(shape, 1)) & 1) == 1


def same_member(shape, quarter):
    rows = iota(shape, 0)
    return ((rows % quarter + rows // quarter + iota(shape, 1)) & 1) == 0


def roll(value, shift, axis):
    return pltpu.roll(value, shift % value.shape[axis], axis)


def both_ways(value, axis):
    return roll(value, 1, axis) + roll(value, -1, axis)


def newton(around, value, mass, source):
    curve = mass * (value * value)
    over = (around + source) + 2.0 * (curve * value)
    under = (6.0 + mass) + 3.0 * curve
    guess = pl.reciprocal(under, approx=True)
    guess = guess * (2.0 - under * guess)
    guess = guess * (2.0 - under * guess)
    return over * guess


def residual(around, value, mass, source):
    return (around - 6.0 * value) - mass * (value * value * value + value) + source


def pooled(rows, pool):
    high = rows.astype(jnp.bfloat16)
    rest = rows - high.astype(jnp.float32)
    middle = rest.astype(jnp.bfloat16)
    low = (rest - middle.astype(jnp.float32)).astype(jnp.bfloat16)
    dot = functools.partial(jnp.dot, preferred_element_type=jnp.float32)
    return dot(high, pool) + (dot(middle, pool) + dot(low, pool))


def pool_matrix(width, columns):
    half = width // 2
    shape = (width, columns)
    return jnp.where(iota(shape, 0) // 2 == iota(shape, 1) % half, 1.0, 0.0).astype(jnp.bfloat16)


def half_sweep(field, mass, source, colour, low, high):
    limit, rows, columns = field.shape[1:]
    is_odd = odd((rows, columns))

    def step(index, carry):
        before = jnp.maximum(index - 1, 0)
        after = jnp.minimum(index + 1, limit - 1)
        other = field[1 - colour, index]
        first, second = field[1 - colour, before], field[1 - colour, after]
        if colour == 1:
            first, second = second, first
        around = other + jnp.where(is_odd, second, first)
        around = around + both_ways(other, 0) + both_ways(other, 1)
        field[colour, index] = newton(around, field[colour, index], mass[colour, index], source[colour, index])
        return carry

    lax.fori_loop(low, high, step, 0)


def two_sweeps(count, field, mass, source):
    limit = field.shape[1]
    half_sweep(field, mass, source, 0, 0, limit)
    half_sweep(field, mass, source, 1, 1, limit - 1)

    @pl.when(count >= 2)
    def _():
        half_sweep(field, mass, source, 0, 1, limit - 1)
        half_sweep(field, mass, source, 1, 2, limit - 2)


def shifted(value, axis, by):
    count = lax.axis_size(axis)
    return lax.ppermute(value, axis, [(i, (i + by) % count) for i in range(count)])


def swapped_cores(value):
    count = lax.axis_size("brick")
    return lax.ppermute(value, "brick", [(i, i ^ 1) for i in range(count)])


def pack_kernel(count, *refs):
    blocks, (own, to_left, to_right, edge_left, edge_right) = refs[:count], refs[count:]
    pairs = own.shape[2]
    rows, columns = own.shape[3:]
    is_odd = odd((rows, columns))
    upper = iota((rows, columns), 0) < rows // 2
    for at, block in enumerate(blocks):

        def step(pair, carry, at=at, block=block):
            even, next_one = block[2 * pair], block[2 * pair + 1]
            red = jnp.where(is_odd, next_one, even)
            black = jnp.where(is_odd, even, next_one)
            own[at, 0, pair] = red
            own[at, 1, pair] = black
            turned = roll(black, rows // 2, 0)
            to_left[at, pair] = jnp.where(upper, red, turned)
            to_right[at, pair] = jnp.where(upper, turned, red)
            return carry

        lax.fori_loop(0, pairs, step, 0)
        for pair in range(2):
            for colour in range(2):
                edge_left[at, colour, pair] = own[at, colour, pair]
                edge_right[at, colour, pair] = own[at, colour, pairs - 2 + pair]


def first_exchange(blocks):
    count = len(blocks)
    rows, wide, columns = blocks[0].shape
    pairs = rows // 2
    own, to_left, to_right, edge_left, edge_right = call(
        functools.partial(pack_kernel, count),
        [(count, 2, pairs, wide, columns)]
        + [(count, pairs, wide, columns)] * 2
        + [(count, 2, 2, wide, columns)] * 2,
        list(blocks),
    )
    y_left = shifted(to_right, "brick", 1)
    y_right = shifted(to_left, "brick", -1)
    x_left = shifted(edge_right, "group", 1)
    x_right = shifted(edge_left, "group", -1)
    c_left = shifted(jnp.concatenate([y_left[:, -2:], y_right[:, -2:]], 1), "group", 1)
    c_right = shifted(jnp.concatenate([y_left[:, :2], y_right[:, :2]], 1), "group", -1)
    return own, x_left, x_right, y_left, y_right, c_left, c_right


def assemble_first(window, at, own, x_left, x_right, y_left, y_right, c_left, c_right):
    pairs, wide, columns = own.shape[2:]
    upper = iota((wide, columns), 0) < wide // 2

    def put(to, red, black, from_left, from_right):
        window[0, to, :wide] = red
        window[0, to, wide:] = jnp.where(upper, from_right, from_left)
        window[1, to, :wide] = black
        window[1, to, wide:] = roll(jnp.where(upper, from_left, from_right), wide // 2, 0)

    def step(pair, carry):
        put(pair + 2, own[at, 0, pair], own[at, 1, pair], y_left[at, pair], y_right[at, pair])
        return carry

    lax.fori_loop(0, pairs, step, 0)
    for k in range(2):
        put(k, x_left[at, 0, k], x_left[at, 1, k], c_left[at, k], c_left[at, 2 + k])
        put(pairs + 2 + k, x_right[at, 0, k], x_right[at, 1, k], c_right[at, k], c_right[at, 2 + k])


def first_kernel(sweeps, *refs):
    fresh, fixed = refs[:7], refs[7:14]
    fine, nxt, edge_left, edge_right, field, mass, source, tall = refs[14:]
    count = sweeps[0]
    assemble_first(field, 0, *fresh)
    assemble_first(mass, 1, *fixed)
    assemble_first(source, 2, *fixed)
    pairs, wide, columns = fresh[0].shape[2:]
    two_sweeps(count, field, mass, source)
    is_odd = odd((wide, columns))
    row = iota((wide, columns), 0)
    top, bottom = row == 0, row == wide - 1

    def unpack(pair, carry):
        red, black = field[0, pair + 2, :wide], field[1, pair + 2, :wide]
        fine[2 * pair] = jnp.where(is_odd, black, red)
        fine[2 * pair + 1] = jnp.where(is_odd, red, black)
        return carry

    lax.fori_loop(0, pairs, unpack, 0)

    def keep(index, value):
        for c in range(columns // LANES):
            tall[c, index] = value[:, c * LANES : (c + 1) * LANES]

    @pl.when(count <= 2)
    def _():
        def step(pair, carry):
            total = jnp.zeros((wide, columns), jnp.float32)
            for colour in range(2):
                other = field[1 - colour, pair + 2, :wide]
                first = jnp.where(pair == 0, 0.0, field[1 - colour, pair + 1, :wide])
                second = jnp.where(pair == pairs - 1, 0.0, field[1 - colour, pair + 3, :wide])
                if colour == 1:
                    first, second = second, first
                around = other + jnp.where(is_odd, second, first) + both_ways(other, 1)
                around = around + jnp.where(bottom, 0.0, roll(other, -1, 0))
                around = around + jnp.where(top, 0.0, roll(other, 1, 0))
                at = (colour, pair + 2, slice(0, wide))
                total = total + residual(around, field[at], mass[at], source[at])
            own = (pair + 2, slice(0, wide))
            keep(pair, field[(0, *own)] + field[(1, *own)])
            keep(pairs + pair, total)
            keep(2 * pairs + pair, mass[(0, *own)] + mass[(1, *own)])
            return carry

        lax.fori_loop(0, pairs, step, 0)
        low = jnp.where(is_odd, field[1, 2, :wide], field[0, 2, :wide])
        high = jnp.where(is_odd, field[0, pairs + 1, :wide], field[1, pairs + 1, :wide])
        half, tiles, quarter = columns // 2, pairs // 2, wide // 2
        keep(3 * pairs, high)
        keep(3 * pairs + 1, low)
        lines = (3 * pairs + 2) * wide // 2
        flat = tall.reshape(columns // LANES, 2 * lines, LANES)

        def every_other(start):
            parts = [flat[c, pl.ds(start, lines, stride=2)] for c in range(columns // LANES)]
            return jnp.concatenate(parts, 1)

        firsts, seconds = every_other(0), every_other(1)
        whole = (iota((wide, columns), 0)) % quarter
        y_faces = []
        for t in range(tiles):
            last, head = seconds[t * wide : (t + 1) * wide], firsts[t * wide : (t + 1) * wide]
            y_faces.append(
                jnp.where(
                    whole == 0,
                    roll(last, quarter + 1, 0),
                    jnp.where(whole == quarter - 1, roll(head, quarter - 1, 0), 0.0),
                )
            )
        narrow = pooled(jnp.concatenate([firsts + seconds] + y_faces, 0), pool_matrix(columns, half))
        is_odd_half = odd((wide, half), quarter)
        is_even = same_member((wide, half), quarter)

        def packed(index, factor):
            tile = narrow[index * wide : (index + 1) * wide] * factor
            return jnp.where(is_odd_half, roll(tile, quarter, 0), tile)

        face_x = packed(3 * tiles, 0.5)
        for t in range(tiles):
            values = [
                packed(t, 0.125),
                packed(tiles + t, 0.5),
                packed(2 * tiles + t, 0.5),
                packed(3 * tiles + 1 + t, 0.5),
            ]
            for at, value in enumerate(values):
                nxt[at, t] = value
                if t < 2:
                    if at == 1 and t == 1:
                        value = jnp.where(is_even, value, face_x)
                    edge_left[at, t] = value
                if t >= tiles - 2:
                    if at == 1 and t == tiles - 2:
                        value = jnp.where(is_even, face_x, value)
                    edge_right[at, t - tiles + 2] = value
        nxt[4, 0] = face_x
        for t in range(1, tiles):
            nxt[4, t] = jnp.zeros((wide, half), jnp.float32)


def first_level(field, mass, source, count):
    rows, wide, columns = field.shape
    pairs = rows // 2
    half, tiles = columns // 2, pairs // 2
    window = (2, pairs + 4, 2 * wide, columns)
    outs = [
        (rows, wide, columns),
        (5, tiles, wide, half),
        (4, 2, wide, half),
        (4, 2, wide, half),
    ]

    def run(fresh, fixed, left):
        return call(
            first_kernel, outs, [left, *fresh, *fixed], [window] * 3 + [(columns // LANES, 3 * pairs + 2, wide, LANES)], 1
        )

    parts = first_exchange([field, mass, source])
    once = run(parts, parts, count)
    return lax.cond(
        count[0] > 2,
        lambda given: run(first_exchange([given[0]]), parts, count - 2),
        lambda given: given,
        once,
    )


def second_prepare_kernel(own, x_left, x_right, extended, to_left, to_right, faces):
    tiles, wide, columns = own.shape[1:]
    quarter = wide // 2
    row_of = iota((wide, columns), 0) % quarter
    is_even = same_member((wide, columns), quarter)
    face_x = own[4, 0]
    for t in range(tiles + 4):
        if t < 2:
            source, k = x_left, t
        elif t < tiles + 2:
            source, k = own, t - 2
        else:
            source, k = x_right, t - tiles - 2
        defect = source[1, k]
        if t == 1:
            defect = defect + jnp.where(is_even, 0.0, face_x)
        if t == 2:
            defect = defect + jnp.where(is_even, x_left[1, 0], 0.0)
        if t == tiles + 1:
            defect = defect + jnp.where(is_even, 0.0, x_right[1, 1])
        if t == tiles + 2:
            defect = defect + jnp.where(is_even, face_x, 0.0)
        face_y = source[3, k]
        faces[t] = face_y
        for at in range(3):
            value = defect if at == 1 else source[at, k]
            extended[at, t] = value
            to_left[at, t] = jnp.where(row_of == quarter - 1, face_y, value) if at == 1 else value
            to_right[at, t] = jnp.where(row_of == 0, face_y, value) if at == 1 else value


def assemble_second(window, to, tile, left, right):
    wide = tile.shape[0]
    quarter = wide // 2
    upper = iota(tile.shape, 0) < quarter
    window[0, to, :wide] = jnp.where(upper, tile, roll(right, quarter, 0))
    window[0, to, wide:] = roll(left, quarter, 0)
    window[1, to, :wide] = jnp.where(upper, roll(tile, quarter, 0), right)
    window[1, to, wide:] = left


def second_finish(count, field, mass, source, middle, packed, nxt, tall):
    limit, columns = field.shape[1], field.shape[3]
    pairs = limit - 4
    wide = field.shape[2] // 2
    quarter = wide // 2
    two_sweeps(count, field, mass, source)
    is_odd = odd((wide, columns), quarter)
    row = iota((wide, columns), 0)
    upper = row < quarter
    top, bottom = row == 0, row == quarter - 1
    for pair in range(pairs):
        red, black = field[0, pair + 2, :wide], field[1, pair + 2, :wide]
        tile = jnp.where(upper, red, roll(black, quarter, 0))
        packed[pair] = tile
        middle[pair] = jnp.where(is_odd, roll(tile, quarter, 0), tile)

    @pl.when(count <= 2)
    def _():
        for pair in range(pairs):
            total = jnp.zeros((wide, columns), jnp.float32)
            for colour in range(2):
                other = field[1 - colour, pair + 2, :wide]
                around = other + both_ways(other, 1)
                around = around + jnp.where(bottom, 0.0, roll(other, -1, 0))
                around = around + jnp.where(top, 0.0, roll(other, 1, 0))
                first = field[1 - colour, pair + 1, :wide] if pair else 0.0
                second = field[1 - colour, pair + 3, :wide] if pair < pairs - 1 else 0.0
                if colour == 1:
                    first, second = second, first
                around = around + jnp.where(is_odd, second, first)
                at = (colour, pair + 2, slice(0, wide))
                total = total + residual(around, field[at], mass[at], source[at])
            own = (pair + 2, slice(0, wide))
            for at, value in enumerate(
                [field[(0, *own)] + field[(1, *own)], total, mass[(0, *own)] + mass[(1, *own)]]
            ):
                for r in range(quarter):
                    tall[at, r, pair : pair + 1] = value[r : r + 1]
        low = jnp.where(is_odd, field[1, 2, :wide], field[0, 2, :wide])
        high = jnp.where(is_odd, field[0, pairs + 1, :wide], field[1, pairs + 1, :wide])
        pieces = []
        for at in range(3):
            for r in range(0, quarter, 2):
                pieces.append((tall[at, r] + tall[at, r + 1]) * (0.125 if at == 0 else 0.5))
        pieces.append(tall[0, 0] * 0.5)
        pieces.append(tall[0, quarter - 1] * 0.5)
        face = jnp.where(upper, high, roll(low, quarter, 0))
        pieces.append((face + roll(face, -1, 0)) * 0.5)
        wide_rows = jnp.concatenate(pieces, 0)
        nxt[...] = pooled(wide_rows, pool_matrix(columns, columns // 2)).reshape(nxt.shape)


def second_kernel(sweeps, extended, left, right, faces, middle, packed, nxt, mass, source, field, tall):
    limit, wide, columns = extended.shape[1:]
    quarter = wide // 2
    row_of = iota((wide, columns), 0) % quarter
    top, bottom = row_of == 0, row_of == quarter - 1
    for t in range(limit):
        assemble_second(field, t, extended[0, t], left[0, t], right[0, t])
        assemble_second(mass, t, extended[2, t], left[2, t], right[2, t])
        one, two, face = left[1, t], right[1, t], faces[t]
        tile = extended[1, t] + jnp.where(top, one, 0.0) + jnp.where(bottom, two, 0.0)
        one = one + jnp.where(bottom, face, 0.0)
        two = two + jnp.where(top, face, 0.0)
        assemble_second(source, t, tile, one, two)
    is_odd = odd((2 * wide, columns))

    def step(index, carry):
        before, after = jnp.maximum(index - 1, 0), jnp.minimum(index + 1, limit - 1)
        for colour in range(2):
            other = field[1 - colour, index]
            first, second = field[1 - colour, before], field[1 - colour, after]
            if colour == 1:
                first, second = second, first
            around = other + jnp.where(is_odd, second, first) + both_ways(other, 0) + both_ways(other, 1)
            source[colour, index] = source[colour, index] - residual(
                around, field[colour, index], mass[colour, index], 0.0
            )
        return carry

    lax.fori_loop(0, limit, step, 0)
    second_finish(sweeps[0], field, mass, source, middle, packed, nxt, tall)


def second_again_kernel(sweeps, extended, left, right, mass, source, middle, packed, nxt, field, tall):
    for t in range(extended.shape[0]):
        assemble_second(field, t, extended[t], left[t], right[t])
    second_finish(sweeps[0], field, mass, source, middle, packed, nxt, tall)


def second_level(parts, edge_left, edge_right, count):
    tiles, wide, columns = parts.shape[1:]
    limit = tiles + 4
    x_left = shifted(edge_right, "group", 1)
    x_right = shifted(edge_left, "group", -1)
    three = (3, limit, wide, columns)
    extended, to_left, to_right, faces = call(
        second_prepare_kernel, [three, three, three, (limit, wide, columns)], [parts, x_left, x_right]
    )
    left = shifted(to_right, "brick", 1)
    right = shifted(to_left, "brick", -1)
    window = (2, limit, 2 * wide, columns)
    outs = [(tiles, wide, columns), (tiles, wide, columns), (9, tiles, columns // 2)]
    scratch = [window, (3, wide // 2, tiles, columns)]
    middle, packed, nxt, mass, source = call(
        second_kernel, outs + [window, window], [count, extended, left, right, faces], scratch, 1
    )

    def again(given):
        packed = given[1]
        x_left = shifted(packed[-2:], "group", 1)
        x_right = shifted(packed[:2], "group", -1)
        extended = jnp.concatenate([x_left, packed, x_right], 0)
        left = shifted(extended, "brick", 1)
        right = shifted(extended, "brick", -1)
        return list(call(second_again_kernel, outs, [count - 2, extended, left, right, mass, source], scratch, 1))

    done = lax.cond(count[0] > 2, again, lambda given: given, [middle, packed, nxt])
    return done[0], done[2]


def third_prepare_kernel(*refs):
    blocks, out = refs[:-1], refs[-1]
    count = len(blocks)
    rows, columns = blocks[0].shape[1:]
    row = iota((rows, columns), 0)
    for b in range(count):
        span = pl.ds(b * rows, rows)
        before, after = blocks[b - 1][8], blocks[(b + 1) % count][8]
        for at in range(8):
            value = blocks[b][at]
            if at in (2, 3):
                high = before[2 * (at - 2) : 2 * (at - 2) + 1]
                low = after[rows // 2 + 2 * (at - 2) : rows // 2 + 2 * (at - 2) + 1]
                value = value + jnp.where(row == 0, high, 0.0) + jnp.where(row == rows - 1, low, 0.0)
            out[at, span] = value


def third_finish(sweeps, turn, field, mass, source, coarse, packed, nxt, double, tall):
    rows, columns = field.shape[2:]
    is_odd = odd((rows, columns))
    count = sweeps[0]
    two_sweeps(count, field, mass, source)
    red, black = field[0, 2], field[1, 2]
    even = jnp.where(is_odd, black, red)
    next_one = jnp.where(is_odd, red, black)
    packed[0] = red
    packed[1] = black

    def straight(value):
        double[:rows] = value
        double[rows:] = value
        return double[pl.ds(pl.multiple_of(rows - turn[0], 8), rows)]

    even, next_one = straight(even), straight(next_one)
    for r in range(rows):
        coarse[2 * r : 2 * r + 1] = even[r : r + 1]
        coarse[2 * r + 1 : 2 * r + 2] = next_one[r : r + 1]

    @pl.when(count <= 2)
    def _():
        total = jnp.zeros((rows, columns), jnp.float32)
        for colour in range(2):
            other = field[1 - colour, 2]
            around = other + both_ways(other, 0) + both_ways(other, 1)
            total = total + residual(around, field[colour, 2], mass[colour, 2], source[colour, 2])
        total = straight(total)
        coefficient = straight(mass[0, 2] + mass[1, 2])
        pieces = [(even + next_one) * 0.125, total * 0.5, coefficient * 0.5, next_one * 0.5, even * 0.5]
        narrow = pooled(jnp.concatenate(pieces, 0), pool_matrix(columns, columns))
        tall[...] = narrow
        total_rows = 5 * rows
        nxt[...] = (
            tall[pl.ds(0, total_rows // 2, stride=2)] + tall[pl.ds(1, total_rows // 2, stride=2)]
        ).reshape(nxt.shape)


def pack_pair(window, at, even, next_one, is_odd):
    window[0, at] = jnp.where(is_odd, next_one, even)
    window[1, at] = jnp.where(is_odd, even, next_one)


def third_kernel(sweeps, turn, own, left2, left1, right1, right2, coarse, packed, nxt, mass, source, field, double, tall):
    rows, columns = own.shape[1:]
    is_odd = odd((rows, columns))
    order = (left2, left1, own, right1, right2)
    for q, part in enumerate(order):
        pack_pair(field, q, part[0], part[1], is_odd)
        pack_pair(mass, q, part[4], part[5], is_odd)
        first, second = part[2], part[3]
        if q > 0:
            first = first + order[q - 1][7]
        if q < 4:
            second = second + order[q + 1][6]
        pack_pair(source, q, first, second, is_odd)
    for q in range(5):
        for colour in range(2):
            other = field[1 - colour, q]
            first, second = field[1 - colour, max(q - 1, 0)], field[1 - colour, min(q + 1, 4)]
            if colour == 1:
                first, second = second, first
            around = other + jnp.where(is_odd, second, first) + both_ways(other, 0) + both_ways(other, 1)
            source[colour, q] = source[colour, q] - residual(around, field[colour, q], mass[colour, q], 0.0)
    third_finish(sweeps, turn, field, mass, source, coarse, packed, nxt, double, tall)


def third_again_kernel(sweeps, turn, own, left2, left1, right1, right2, mass, source, coarse, packed, nxt, field, double, tall):
    for q, part in enumerate((left2, left1, own, right1, right2)):
        for colour in range(2):
            field[colour, q] = part[colour]
    third_finish(sweeps, turn, field, mass, source, coarse, packed, nxt, double, tall)


def third_level(part, count):
    groups = lax.axis_size("group")
    tile_rows, columns = part.shape[1:]
    rows = groups * tile_rows
    blocks = [part] + [shifted(part, "group", -d) for d in range(1, groups)]
    (own,) = call(third_prepare_kernel, [(8, rows, columns)], blocks)
    turn = (lax.axis_index("group") * tile_rows).astype(jnp.int32).reshape(1)

    def neighbours(value):
        return [shifted(value, "brick", by) for by in (2, 1, -1, -2)]

    window = (2, 5, rows, columns)
    outs = [(2 * rows, columns), (2, rows, columns), (5, rows // 2, columns)]
    scratch = [window, (2 * rows, columns), (5 * rows, columns)]
    coarse, packed, nxt, mass, source = call(
        third_kernel, outs + [window, window], [count, turn, own, *neighbours(own)], scratch, 2
    )

    def again(given):
        packed = given[1]
        args = [count - 2, turn, packed, *neighbours(packed), mass, source]
        return list(call(third_again_kernel, outs, args, scratch, 2))

    done = lax.cond(count[0] > 2, again, lambda given: given, [coarse, packed, nxt])
    return done[0].reshape(rows, 2, columns), done[2]


def chip_kernel(core, own, other, out):
    rows, columns = own.shape[1:]
    low = iota((rows, columns), 1) < columns // 2

    def send(values):
        for c in range(out.shape[0]):
            for at, value in enumerate(values):
                out[c, at] = value

    @pl.when(core[0] == 0)
    def _():
        send(
            [
                jnp.where(low, own[0], other[0]),
                jnp.where(low, own[1] + other[4], other[1] + own[3]),
            ]
        )

    @pl.when(core[0] == 1)
    def _():
        send([jnp.where(low, other[2], own[2]), jnp.where(low, other[4], own[3])])


def fourth_kernel(sweeps, core, own, other, out, field, mass, source):
    chips, rows, columns = field.shape
    lane = iota((rows, columns), 1)
    low = lane < columns // 2
    half = columns // 2
    first, last = lane % half == 0, lane % half == half - 1
    is_odd = ((iota((rows, columns), 0) + lane // half + lane) & 1) == 1

    def sides(ref, t):
        before, after = (t + chips - 1) % chips, (t + 1) % chips
        return jnp.where(low, ref[after], ref[before])

    def around_of(t):
        value = field[t]
        total = roll(value + sides(field, t), half, 1) + both_ways(value, 0)
        total = total + jnp.where(last, roll(value, half - 1, 1), roll(value, -1, 1))
        return total + jnp.where(first, roll(value, 1 - half, 1), roll(value, 1, 1))

    def load(one, two):
        def step(t, carry):
            field[t] = one[t, 0]
            mass[t] = two[t, 0]
            before, after = (t + chips - 1) % chips, (t + 1) % chips
            face = jnp.where(low, two[after, 1], two[before, 1])
            source[t] = one[t, 1] + roll(face, half, 1)
            return carry

        lax.fori_loop(0, chips, step, 0)

    @pl.when(core[0] == 0)
    def _():
        load(own, other)

    @pl.when(core[0] == 1)
    def _():
        load(other, own)

    def start(t, carry):
        source[t] = source[t] - residual(around_of(t), field[t], mass[t], 0.0)
        return carry

    lax.fori_loop(0, chips, start, 0)

    def one_sweep(step, carry):
        for colour in range(2):

            def update(t, inner):
                value = field[t]
                fresh = newton(around_of(t), value, mass[t], source[t])
                field[t] = jnp.where(is_odd, fresh, value) if colour else jnp.where(is_odd, value, fresh)
                return inner

            lax.fori_loop(0, chips, update, 0)
        return carry

    lax.fori_loop(0, sweeps[0], one_sweep, 0)
    for t in range(chips):
        out[:, t * columns : (t + 1) * columns] = field[t]


def fourth_level(part, count):
    bricks = lax.axis_size("brick")
    chips = bricks // 2
    rows, columns = part.shape[1:]
    core = (lax.axis_index("brick") % 2).astype(jnp.int32).reshape(1)
    (message,) = call(chip_kernel, [(chips, 2, rows, columns)], [core, part, swapped_cores(part)], (), 1)
    cores = [[2 * chip + c for chip in range(chips)] for c in range(2)]
    own = lax.all_to_all(message, "brick", 0, 0, axis_index_groups=cores)
    other = swapped_cores(own)
    (out,) = call(
        fourth_kernel, [(rows, chips * columns)], [count, core, own, other], [(chips, rows, columns)] * 3, 2
    )
    return out


def on_device(initial_field, mass, source, sweeps):
    fine, parts, edge_left, edge_right = first_level(initial_field, mass, source, sweeps[0:1])
    middle, part = second_level(parts, edge_left, edge_right, sweeps[1:2])
    coarse, part = third_level(part, sweeps[2:3])
    coarsest = fourth_level(part, sweeps[3:4])
    tiles, wide, columns = middle.shape
    middle = middle.reshape(2 * tiles, wide // 2, columns)
    return fine, middle, coarse, coarsest


def solution(mesh):
    return jax.shard_map(
        on_device,
        mesh=mesh,
        in_specs=(
            P("group", "brick", None),
            P("group", "brick", None),
            P("group", "brick", None),
            P(),
        ),
        out_specs=(
            P("group", "brick", None),
            P("group", "brick", None),
            P(None, "brick", None),
            P(),
        ),
        check_vma=False,
    )
```

```python
import functools

import jax
import jax.numpy as jnp
from jax import lax
from jax.experimental import pallas as pl
from jax.experimental.pallas import tpu as pltpu
from jax.sharding import PartitionSpec as P


INTERPRET = False
MIB = 1024 * 1024
LANES = 128


def call(kernel, out_shapes, args, scratch=(), scalars=0, results=0, limit=12 * MIB):
    spec = pl.BlockSpec(memory_space=pltpu.VMEM)
    smem = pl.BlockSpec(memory_space=pltpu.SMEM)
    return pl.pallas_call(
        kernel,
        out_shape=[
            jax.ShapeDtypeStruct(shape, jnp.float32) if at < results else pltpu.VMEM(shape, jnp.float32)
            for at, shape in enumerate(out_shapes)
        ],
        in_specs=[smem] * scalars + [spec] * (len(args) - scalars),
        out_specs=[spec] * len(out_shapes),
        scratch_shapes=[pltpu.VMEM(shape, jnp.float32) for shape in scratch],
        compiler_params=pltpu.CompilerParams(vmem_limit_bytes=limit),
        interpret=INTERPRET,
    )(*args)


def iota(shape, axis):
    return lax.broadcasted_iota(jnp.int32, shape, axis)


def odd(shape, period=None):
    rows = iota(shape, 0)
    if period is not None:
        rows = rows % period
    return ((rows + iota(shape, 1)) & 1) == 1


def same_member(shape, quarter):
    rows = iota(shape, 0)
    return ((rows % quarter + rows // quarter + iota(shape, 1)) & 1) == 0


def roll(value, shift, axis):
    return pltpu.roll(value, shift % value.shape[axis], axis)


def both_ways(value, axis):
    return roll(value, 1, axis) + roll(value, -1, axis)


def newton(around, value, mass, source):
    curve = mass * (value * value)
    over = (around + source) + 2.0 * (curve * value)
    under = (6.0 + mass) + 3.0 * curve
    guess = pl.reciprocal(under, approx=True)
    guess = guess * (2.0 - under * guess)
    return over * guess


def residual(around, value, mass, source):
    return (around - 6.0 * value) - mass * (value * value * value + value) + source


def pooled(rows, pool):
    high = rows.astype(jnp.bfloat16)
    rest = rows - high.astype(jnp.float32)
    middle = rest.astype(jnp.bfloat16)
    low = (rest - middle.astype(jnp.float32)).astype(jnp.bfloat16)
    dot = functools.partial(jnp.dot, preferred_element_type=jnp.float32)
    return dot(high, pool) + (dot(middle, pool) + dot(low, pool))


def pool_matrix(width, columns):
    half = width // 2
    shape = (width, columns)
    return jnp.where(iota(shape, 0) // 2 == iota(shape, 1) % half, 1.0, 0.0).astype(jnp.bfloat16)


def half_sweep(field, mass, source, colour, low, high, most, beside=None):
    mine, other = field[colour], field[1 - colour]
    limit, rows, columns = mine.shape
    is_odd = odd((rows, columns))
    beside = beside or (lambda value: both_ways(value, 1))
    together = max(k for k in range(1, most + 1) if (high - low) % k == 0)

    def step(turn, carry):
        start = low + turn * together
        near = [other[jnp.clip(start + k, 0, limit - 1)] for k in range(-1, together + 1)]
        fresh = []
        for k in range(together):
            first, second = (near[k], near[k + 2]) if colour == 0 else (near[k + 2], near[k])
            around = near[k + 1] + jnp.where(is_odd, second, first)
            around = around + both_ways(near[k + 1], 0) + beside(near[k + 1])
            fresh.append(newton(around, mine[start + k], mass[colour][start + k], source[colour][start + k]))
        for k in range(together):
            mine[start + k] = fresh[k]
        return carry

    turns = (high - low) // together
    if turns == 1:
        step(0, 0)
    else:
        lax.fori_loop(0, turns, step, 0)


def two_sweeps(count, field, mass, source, most):
    limit = field[0].shape[0]
    half_sweep(field, mass, source, 0, 0, limit, most)
    half_sweep(field, mass, source, 1, 1, limit - 1, most)

    @pl.when(count >= 2)
    def _():
        half_sweep(field, mass, source, 0, 1, limit - 1, most)
        half_sweep(field, mass, source, 1, 2, limit - 2, most)


def source_from_defect(field, mass, source, beside=None, inner=None):
    limit, rows, columns = field[0].shape
    is_odd = odd((rows, columns))
    beside = beside or (lambda value: both_ways(value, 1))
    for index in inner or range(limit):
        for colour in range(2):
            other = field[1 - colour]
            first, second = other[max(index - 1, 0)], other[min(index + 1, limit - 1)]
            if colour == 1:
                first, second = second, first
            around = other[index] + jnp.where(is_odd, second, first)
            around = around + both_ways(other[index], 0) + beside(other[index])
            source[colour][index] = source[colour][index] - residual(
                around, field[colour][index], mass[colour][index], 0.0
            )


def shifted(value, axis, by):
    count = lax.axis_size(axis)
    return lax.ppermute(value, axis, [(i, (i + by) % count) for i in range(count)])


def swapped_cores(value):
    count = lax.axis_size("brick")
    return lax.ppermute(value, "brick", [(i, i ^ 1) for i in range(count)])


def pack_kernel(count, *refs):
    blocks, (own, to_left, to_right, tip_left, tip_right, edge_left, edge_right) = refs[:count], refs[count:]
    pairs = own.shape[2]
    rows, columns = own.shape[3:]
    is_odd = odd((rows, columns))
    upper = iota((rows, columns), 0) < rows // 2
    for at, block in enumerate(blocks):

        def step(pair, carry, at=at, block=block, tip=None):
            even, next_one = block[2 * pair], block[2 * pair + 1]
            red = jnp.where(is_odd, next_one, even)
            black = jnp.where(is_odd, even, next_one)
            own[at, 0, pair] = red
            own[at, 1, pair] = black
            turned = roll(black, rows // 2, 0)
            one, two = jnp.where(upper, red, turned), jnp.where(upper, turned, red)
            if tip is None:
                to_left[at, pair - 2] = one
                to_right[at, pair - 2] = two
            else:
                tip_left[at, tip] = one
                tip_right[at, tip] = two
            return carry

        for tip, pair in enumerate((0, 1, pairs - 2, pairs - 1)):
            step(pair, 0, tip=tip)
        lax.fori_loop(2, pairs - 2, step, 0, unroll=4)
        for pair in range(2):
            for colour in range(2):
                edge_left[at, colour, pair] = own[at, colour, pair]
                edge_right[at, colour, pair] = own[at, colour, pairs - 2 + pair]


def first_exchange(blocks):
    count = len(blocks)
    rows, wide, columns = blocks[0].shape
    pairs = rows // 2
    own, to_left, to_right, tip_left, tip_right, edge_left, edge_right = call(
        functools.partial(pack_kernel, count),
        [(count, 2, pairs, wide, columns)]
        + [(count, pairs - 4, wide, columns)] * 2
        + [(count, 4, wide, columns)] * 2
        + [(count, 2, 2, wide, columns)] * 2,
        list(blocks),
    )
    t_left = shifted(tip_right, "brick", 1)
    t_right = shifted(tip_left, "brick", -1)
    y_left = shifted(to_right, "brick", 1)
    y_right = shifted(to_left, "brick", -1)
    x_left = shifted(edge_right, "group", 1)
    x_right = shifted(edge_left, "group", -1)
    far = [t_left[0, 2:], t_right[0, 2:]] + [t[1:, 3] for t in (t_left, t_right) if count > 1]
    c_left = shifted(jnp.concatenate(far, 0), "group", 1)
    far = [t_left[0, :2], t_right[0, :2]] + [t[1:, 0] for t in (t_left, t_right) if count > 1]
    c_right = shifted(jnp.concatenate(far, 0), "group", -1)
    return own, x_left, x_right, t_left, t_right, y_left, y_right, c_left, c_right


def assemble_first(window, at, own, x_left, x_right, t_left, t_right, y_left, y_right, c_left, c_right):
    pairs, wide, columns = own.shape[2:]
    upper = iota((wide, columns), 0) < wide // 2

    def put(to, red, black, from_left, from_right):
        window[0][to, :wide] = red
        window[0][to, wide:] = jnp.where(upper, from_right, from_left)
        window[1][to, :wide] = black
        window[1][to, wide:] = roll(jnp.where(upper, from_left, from_right), wide // 2, 0)

    def step(pair, carry):
        put(pair + 2, own[at, 0, pair], own[at, 1, pair], y_left[at, pair - 2], y_right[at, pair - 2])
        return carry

    lax.fori_loop(2, pairs - 2, step, 0, unroll=4)
    for tip, pair in enumerate((0, 1, pairs - 2, pairs - 1)):
        put(pair + 2, own[at, 0, pair], own[at, 1, pair], t_left[at, tip], t_right[at, tip])
    for k in range(2):
        if at == 0:
            left, right = (c_left[k], c_left[2 + k]), (c_right[k], c_right[2 + k])
        else:
            left, right = (c_left[3 + at], c_left[5 + at]), (c_right[3 + at], c_right[5 + at])
        put(k, x_left[at, 0, k], x_left[at, 1, k], *left)
        put(pairs + 2 + k, x_right[at, 0, k], x_right[at, 1, k], *right)


def first_kernel(sweeps, *refs):
    fresh, fixed = refs[:9], refs[9:18]
    fine, nxt, edge_left, edge_right, *windows, tall = refs[18:]
    field, mass, source = windows[0:2], windows[2:4], windows[4:6]
    count = sweeps[0]
    assemble_first(field, 0, *fresh)
    assemble_first(mass, 1, *fixed)
    assemble_first(source, 2, *fixed)
    pairs, wide, columns = fresh[0].shape[2:]
    two_sweeps(count, field, mass, source, 2)
    is_odd = odd((wide, columns))
    row = iota((wide, columns), 0)
    top, bottom = row == 0, row == wide - 1

    def unpack(pair, carry):
        red, black = field[0][pair + 2, :wide], field[1][pair + 2, :wide]
        fine[2 * pair] = jnp.where(is_odd, black, red)
        fine[2 * pair + 1] = jnp.where(is_odd, red, black)
        return carry

    lax.fori_loop(0, pairs, unpack, 0, unroll=4)

    def keep(index, value):
        for c in range(columns // LANES):
            tall[c, index] = value[:, c * LANES : (c + 1) * LANES]

    @pl.when(count <= 2)
    def _():
        def step(pair, carry):
            total = jnp.zeros((wide, columns), jnp.float32)
            for colour in range(2):
                other = field[1 - colour][pair + 2, :wide]
                first = jnp.where(pair == 0, 0.0, field[1 - colour][pair + 1, :wide])
                second = jnp.where(pair == pairs - 1, 0.0, field[1 - colour][pair + 3, :wide])
                if colour == 1:
                    first, second = second, first
                around = other + jnp.where(is_odd, second, first) + both_ways(other, 1)
                around = around + jnp.where(bottom, 0.0, roll(other, -1, 0))
                around = around + jnp.where(top, 0.0, roll(other, 1, 0))
                at = (pair + 2, slice(0, wide))
                total = total + residual(around, field[colour][at], mass[colour][at], source[colour][at])
            keep(pair, field[0][at] + field[1][at])
            keep(pairs + pair, total)
            keep(2 * pairs + pair, mass[0][at] + mass[1][at])
            return carry

        lax.fori_loop(0, pairs, step, 0, unroll=2)
        low = jnp.where(is_odd, field[1][2, :wide], field[0][2, :wide])
        high = jnp.where(is_odd, field[0][pairs + 1, :wide], field[1][pairs + 1, :wide])
        half, tiles, quarter = columns // 2, pairs // 2, wide // 2
        keep(3 * pairs, high)
        keep(3 * pairs + 1, low)
        lines = (3 * pairs + 2) * wide // 2
        flat = tall.reshape(columns // LANES, 2 * lines, LANES)

        def every_other(start):
            parts = [flat[c, pl.ds(start, lines, stride=2)] for c in range(columns // LANES)]
            return jnp.concatenate(parts, 1)

        firsts, seconds = every_other(0), every_other(1)
        whole = (iota((wide, columns), 0)) % quarter
        y_faces = []
        for t in range(tiles):
            last, head = seconds[t * wide : (t + 1) * wide], firsts[t * wide : (t + 1) * wide]
            y_faces.append(
                jnp.where(
                    whole == 0,
                    roll(last, quarter + 1, 0),
                    jnp.where(whole == quarter - 1, roll(head, quarter - 1, 0), 0.0),
                )
            )
        narrow = pooled(jnp.concatenate([firsts + seconds] + y_faces, 0), pool_matrix(columns, half))
        is_odd_half = odd((wide, half), quarter)
        is_even = same_member((wide, half), quarter)

        def packed(index, factor):
            tile = narrow[index * wide : (index + 1) * wide] * factor
            return jnp.where(is_odd_half, roll(tile, quarter, 0), tile)

        face_x = packed(3 * tiles, 0.5)
        for t in range(tiles):
            values = [
                packed(t, 0.125),
                packed(tiles + t, 0.5),
                packed(2 * tiles + t, 0.5),
                packed(3 * tiles + 1 + t, 0.5),
            ]
            for at, value in enumerate(values):
                nxt[at, t] = value
                if t < 2:
                    if at == 1 and t == 1:
                        value = jnp.where(is_even, value, face_x)
                    edge_left[at, t] = value
                if t >= tiles - 2:
                    if at == 1 and t == tiles - 2:
                        value = jnp.where(is_even, face_x, value)
                    edge_right[at, t - tiles + 2] = value
        nxt[4, 0] = face_x
        for t in range(1, tiles):
            nxt[4, t] = jnp.zeros((wide, half), jnp.float32)


def first_level(field, mass, source, count):
    rows, wide, columns = field.shape
    pairs = rows // 2
    half, tiles = columns // 2, pairs // 2
    window = (pairs + 4, 2 * wide, columns)
    outs = [
        (rows, wide, columns),
        (5, tiles, wide, half),
        (4, 2, wide, half),
        (4, 2, wide, half),
    ]

    def run(fresh, fixed, left):
        scratch = [window] * 6 + [(columns // LANES, 3 * pairs + 2, wide, LANES)]
        return call(first_kernel, outs, [left, *fresh, *fixed], scratch, 1, 1, 24 * MIB)

    parts = first_exchange([field, mass, source])
    once = run(parts, parts, count)
    return lax.cond(
        count[0] > 2,
        lambda given: run(first_exchange([given[0]]), parts, count - 2),
        lambda given: given,
        once,
    )


def second_prepare_kernel(own, x_left, x_right, extended, to_left, to_right, faces):
    tiles, wide, columns = own.shape[1:]
    quarter = wide // 2
    row_of = iota((wide, columns), 0) % quarter
    is_even = same_member((wide, columns), quarter)
    face_x = own[4, 0]
    for t in range(tiles + 4):
        if t < 2:
            source, k = x_left, t
        elif t < tiles + 2:
            source, k = own, t - 2
        else:
            source, k = x_right, t - tiles - 2
        defect = source[1, k]
        if t == 1:
            defect = defect + jnp.where(is_even, 0.0, face_x)
        if t == 2:
            defect = defect + jnp.where(is_even, x_left[1, 0], 0.0)
        if t == tiles + 1:
            defect = defect + jnp.where(is_even, 0.0, x_right[1, 1])
        if t == tiles + 2:
            defect = defect + jnp.where(is_even, face_x, 0.0)
        face_y = source[3, k]
        faces[t] = face_y
        for at in range(3):
            value = defect if at == 1 else source[at, k]
            extended[at, t] = value
            to_left[at, t] = jnp.where(row_of == quarter - 1, face_y, value) if at == 1 else value
            to_right[at, t] = jnp.where(row_of == 0, face_y, value) if at == 1 else value


def assemble_second(window, to, tile, left, right):
    wide = tile.shape[0]
    quarter = wide // 2
    upper = iota(tile.shape, 0) < quarter
    window[0][to, :wide] = jnp.where(upper, tile, roll(right, quarter, 0))
    window[0][to, wide:] = roll(left, quarter, 0)
    window[1][to, :wide] = jnp.where(upper, roll(tile, quarter, 0), right)
    window[1][to, wide:] = left


def second_finish(count, field, mass, source, middle, packed, nxt, tall):
    limit, rows, columns = field[0].shape
    pairs = limit - 4
    wide = rows // 2
    quarter = wide // 2
    two_sweeps(count, field, mass, source, 4)
    is_odd = odd((wide, columns), quarter)
    row = iota((wide, columns), 0)
    upper = row < quarter
    top, bottom = row == 0, row == quarter - 1
    for pair in range(pairs):
        red, black = field[0][pair + 2, :wide], field[1][pair + 2, :wide]
        tile = jnp.where(upper, red, roll(black, quarter, 0))
        packed[pair] = tile
        middle[pair] = jnp.where(is_odd, roll(tile, quarter, 0), tile)

    @pl.when(count <= 2)
    def _():
        for pair in range(pairs):
            total = jnp.zeros((wide, columns), jnp.float32)
            for colour in range(2):
                other = field[1 - colour][pair + 2, :wide]
                around = other + both_ways(other, 1)
                around = around + jnp.where(bottom, 0.0, roll(other, -1, 0))
                around = around + jnp.where(top, 0.0, roll(other, 1, 0))
                first = field[1 - colour][pair + 1, :wide] if pair else 0.0
                second = field[1 - colour][pair + 3, :wide] if pair < pairs - 1 else 0.0
                if colour == 1:
                    first, second = second, first
                around = around + jnp.where(is_odd, second, first)
                at = (pair + 2, slice(0, wide))
                total = total + residual(around, field[colour][at], mass[colour][at], source[colour][at])
            values = [field[0][at] + field[1][at], total, mass[0][at] + mass[1][at]]
            for at, value in enumerate(values):
                for r in range(quarter):
                    tall[at, r, pair : pair + 1] = value[r : r + 1]
        low = jnp.where(is_odd, field[1][2, :wide], field[0][2, :wide])
        high = jnp.where(is_odd, field[0][pairs + 1, :wide], field[1][pairs + 1, :wide])
        pieces = []
        for at in range(3):
            for r in range(0, quarter, 2):
                pieces.append((tall[at, r] + tall[at, r + 1]) * (0.125 if at == 0 else 0.5))
        pieces.append(tall[0, 0] * 0.5)
        pieces.append(tall[0, quarter - 1] * 0.5)
        face = jnp.where(upper, high, roll(low, quarter, 0))
        pieces.append((face + roll(face, -1, 0)) * 0.5)
        wide_rows = jnp.concatenate(pieces, 0)
        nxt[...] = pooled(wide_rows, pool_matrix(columns, columns // 2)).reshape(nxt.shape)


def second_kernel(sweeps, extended, left, right, faces, middle, packed, nxt, *rest):
    mass, source, field, tall = rest[0:2], rest[2:4], rest[4:6], rest[6]
    limit, wide, columns = extended.shape[1:]
    quarter = wide // 2
    row_of = iota((wide, columns), 0) % quarter
    top, bottom = row_of == 0, row_of == quarter - 1
    for t in range(limit):
        assemble_second(field, t, extended[0, t], left[0, t], right[0, t])
        assemble_second(mass, t, extended[2, t], left[2, t], right[2, t])
        one, two, face = left[1, t], right[1, t], faces[t]
        tile = extended[1, t] + jnp.where(top, one, 0.0) + jnp.where(bottom, two, 0.0)
        one = one + jnp.where(bottom, face, 0.0)
        two = two + jnp.where(top, face, 0.0)
        assemble_second(source, t, tile, one, two)
    source_from_defect(field, mass, source)
    second_finish(sweeps[0], field, mass, source, middle, packed, nxt, tall)


def second_again_kernel(sweeps, extended, left, right, *rest):
    mass, source = rest[0:2], rest[2:4]
    middle, packed, nxt, *field, tall = rest[4:]
    for t in range(extended.shape[0]):
        assemble_second(field, t, extended[t], left[t], right[t])
    second_finish(sweeps[0], field, mass, source, middle, packed, nxt, tall)


def second_level(parts, edge_left, edge_right, count):
    tiles, wide, columns = parts.shape[1:]
    limit = tiles + 4
    x_left = shifted(edge_right, "group", 1)
    x_right = shifted(edge_left, "group", -1)
    three = (3, limit, wide, columns)
    extended, to_left, to_right, faces = call(
        second_prepare_kernel, [three, three, three, (limit, wide, columns)], [parts, x_left, x_right]
    )
    left = shifted(to_right, "brick", 1)
    right = shifted(to_left, "brick", -1)
    window = (limit, 2 * wide, columns)
    outs = [(tiles, wide, columns), (tiles, wide, columns), (9, tiles, columns // 2)]
    scratch = [window, window, (3, wide // 2, tiles, columns)]
    args = [count, extended, left, right, faces]
    middle, packed, nxt, *fixed = call(second_kernel, outs + [window] * 4, args, scratch, 1, 1)

    def again(given):
        packed = given[1]
        x_left = shifted(packed[-2:], "group", 1)
        x_right = shifted(packed[:2], "group", -1)
        extended = jnp.concatenate([x_left, packed, x_right], 0)
        left = shifted(extended, "brick", 1)
        right = shifted(extended, "brick", -1)
        return list(call(second_again_kernel, outs, [count - 2, extended, left, right, *fixed], scratch, 1, 1))

    done = lax.cond(count[0] > 2, again, lambda given: given, [middle, packed, nxt])
    return done[0], done[2]


def third_prepare_kernel(*refs):
    blocks, out = refs[:-1], refs[-1]
    count = len(blocks)
    rows, columns = blocks[0].shape[1:]
    row = iota((rows, columns), 0)
    for b in range(count):
        span = pl.ds(b * rows, rows)
        before, after = blocks[b - 1][8], blocks[(b + 1) % count][8]
        for at in range(8):
            value = blocks[b][at]
            if at in (2, 3):
                high = before[2 * (at - 2) : 2 * (at - 2) + 1]
                low = after[rows // 2 + 2 * (at - 2) : rows // 2 + 2 * (at - 2) + 1]
                value = value + jnp.where(row == 0, high, 0.0) + jnp.where(row == rows - 1, low, 0.0)
            out[at, span] = value


def third_finish(sweeps, turn, field, mass, source, coarse, packed, nxt, double, tall):
    rows, columns = field[0].shape[1:]
    is_odd = odd((rows, columns))
    count = sweeps[0]
    two_sweeps(count, field, mass, source, 5)
    red, black = field[0][2], field[1][2]
    even = jnp.where(is_odd, black, red)
    next_one = jnp.where(is_odd, red, black)
    packed[0] = red
    packed[1] = black

    def straight(value):
        double[:rows] = value
        double[rows:] = value
        return double[pl.ds(pl.multiple_of(rows - turn[0], 8), rows)]

    even, next_one = straight(even), straight(next_one)
    for r in range(rows):
        coarse[2 * r : 2 * r + 1] = even[r : r + 1]
        coarse[2 * r + 1 : 2 * r + 2] = next_one[r : r + 1]

    @pl.when(count <= 2)
    def _():
        total = jnp.zeros((rows, columns), jnp.float32)
        for colour in range(2):
            other = field[1 - colour][2]
            around = other + both_ways(other, 0) + both_ways(other, 1)
            total = total + residual(around, field[colour][2], mass[colour][2], source[colour][2])
        total = straight(total)
        coefficient = straight(mass[0][2] + mass[1][2])
        pieces = [(even + next_one) * 0.125, total * 0.5, coefficient * 0.5, next_one * 0.5, even * 0.5]
        narrow = pooled(jnp.concatenate(pieces, 0), pool_matrix(columns, columns))
        tall[...] = narrow
        total_rows = 5 * rows
        nxt[...] = (
            tall[pl.ds(0, total_rows // 2, stride=2)] + tall[pl.ds(1, total_rows // 2, stride=2)]
        ).reshape(nxt.shape)


def pack_pair(window, at, even, next_one, is_odd):
    window[0][at] = jnp.where(is_odd, next_one, even)
    window[1][at] = jnp.where(is_odd, even, next_one)


def third_kernel(sweeps, turn, own, left2, left1, right1, right2, coarse, packed, nxt, *rest):
    mass, source, field, double, tall = rest[0:2], rest[2:4], rest[4:6], rest[6], rest[7]
    rows, columns = own.shape[1:]
    is_odd = odd((rows, columns))
    order = (left2, left1, own, right1, right2)
    for q, part in enumerate(order):
        pack_pair(field, q, part[0], part[1], is_odd)
        pack_pair(mass, q, part[4], part[5], is_odd)
        first, second = part[2], part[3]
        if q > 0:
            first = first + order[q - 1][7]
        if q < 4:
            second = second + order[q + 1][6]
        pack_pair(source, q, first, second, is_odd)
    source_from_defect(field, mass, source)
    third_finish(sweeps, turn, field, mass, source, coarse, packed, nxt, double, tall)


def third_again_kernel(sweeps, turn, own, left2, left1, right1, right2, *rest):
    mass, source = rest[0:2], rest[2:4]
    coarse, packed, nxt, *field, double, tall = rest[4:]
    for q, part in enumerate((left2, left1, own, right1, right2)):
        for colour in range(2):
            field[colour][q] = part[colour]
    third_finish(sweeps, turn, field, mass, source, coarse, packed, nxt, double, tall)


def third_level(part, count):
    groups = lax.axis_size("group")
    tile_rows, columns = part.shape[1:]
    rows = groups * tile_rows
    blocks = [part] + [shifted(part, "group", -d) for d in range(1, groups)]
    (own,) = call(third_prepare_kernel, [(8, rows, columns)], blocks)
    turn = (lax.axis_index("group") * tile_rows).astype(jnp.int32).reshape(1)

    def neighbours(value):
        return [shifted(value, "brick", by) for by in (2, 1, -1, -2)]

    window = (5, rows, columns)
    outs = [(2 * rows, columns), (2, rows, columns), (5, rows // 2, columns)]
    scratch = [window, window, (2 * rows, columns), (5 * rows, columns)]
    args = [count, turn, own, *neighbours(own)]
    coarse, packed, nxt, *fixed = call(third_kernel, outs + [window] * 4, args, scratch, 2, 1)

    def again(given):
        packed = given[1]
        args = [count - 2, turn, packed, *neighbours(packed), *fixed]
        return list(call(third_again_kernel, outs, args, scratch, 2, 1))

    done = lax.cond(count[0] > 2, again, lambda given: given, [coarse, packed, nxt])
    return done[0].reshape(rows, 2, columns), done[2]


def chip_kernel(core, own, other, out):
    rows, columns = own.shape[1:]
    low = iota((rows, columns), 1) < columns // 2

    def send(values):
        for c in range(out.shape[0]):
            for at, value in enumerate(values):
                out[c, at] = value

    @pl.when(core[0] == 0)
    def _():
        send(
            [
                jnp.where(low, own[0], other[0]),
                jnp.where(low, own[1] + other[4], other[1] + own[3]),
            ]
        )

    @pl.when(core[0] == 1)
    def _():
        send([jnp.where(low, other[2], own[2]), jnp.where(low, other[4], own[3])])


def fourth_kernel(sweeps, core, own, other, out, *windows):
    field, mass, source = windows[0:2], windows[2:4], windows[4:6]
    chips, _, rows, columns = own.shape
    tiles, half = chips // 2, columns // 2
    lane = iota((rows, columns), 1)
    low = lane < half
    is_odd = odd((rows, columns))
    first, last = lane % half == 0, lane % half == half - 1

    def turned(value):
        return roll(value, half, 1)

    def beside(value):
        after = jnp.where(last, roll(value, half - 1, 1), roll(value, -1, 1))
        return after + jnp.where(first, roll(value, 1 - half, 1), roll(value, 1, 1))

    def put(window, t, one, two):
        one, two = jnp.where(is_odd, turned(one), one), jnp.where(is_odd, turned(two), two)
        window[0][t + 1] = jnp.where(low, one, turned(two))
        window[1][t + 1] = jnp.where(low, turned(one), two)

    def repeat(window, colour):
        window[colour][0] = turned(window[colour][tiles])
        window[colour][tiles + 1] = turned(window[colour][1])

    def load(one, two):
        def defect(t):
            before, after = (t + chips - 1) % chips, (t + 1) % chips
            return one[t, 1] + turned(jnp.where(low, two[after, 1], two[before, 1]))

        for t in range(tiles):
            put(field, t, one[t, 0], one[t + tiles, 0])
            put(mass, t, two[t, 0], two[t + tiles, 0])
            put(source, t, defect(t), defect(t + tiles))

    @pl.when(core[0] == 0)
    def _():
        load(own, other)

    @pl.when(core[0] == 1)
    def _():
        load(other, own)

    for colour in range(2):
        repeat(field, colour)
    source_from_defect(field, mass, source, beside, range(1, tiles + 1))

    def one_sweep(step, carry):
        for colour in range(2):
            half_sweep(field, mass, source, colour, 1, tiles + 1, 8, beside)
            repeat(field, colour)
        return carry

    lax.fori_loop(0, sweeps[0], one_sweep, 0)
    for t in range(tiles):
        red, black = field[0][t + 1], field[1][t + 1]
        one, two = jnp.where(low, red, turned(black)), jnp.where(low, turned(red), black)
        for at, value in ((t, one), (t + tiles, two)):
            out[:, at * columns : (at + 1) * columns] = jnp.where(is_odd, turned(value), value)


def fourth_level(part, count):
    bricks = lax.axis_size("brick")
    chips = bricks // 2
    rows, columns = part.shape[1:]
    core = (lax.axis_index("brick") % 2).astype(jnp.int32).reshape(1)
    (message,) = call(chip_kernel, [(chips, 2, rows, columns)], [core, part, swapped_cores(part)], (), 1)
    cores = [[2 * chip + c for chip in range(chips)] for c in range(2)]
    own = lax.all_to_all(message, "brick", 0, 0, axis_index_groups=cores)
    other = swapped_cores(own)
    scratch = [(chips // 2 + 2, rows, columns)] * 6
    (out,) = call(fourth_kernel, [(rows, chips * columns)], [count, core, own, other], scratch, 2, 1)
    return out


def on_device(initial_field, mass, source, sweeps):
    fine, parts, edge_left, edge_right = first_level(initial_field, mass, source, sweeps[0:1])
    middle, part = second_level(parts, edge_left, edge_right, sweeps[1:2])
    coarse, part = third_level(part, sweeps[2:3])
    coarsest = fourth_level(part, sweeps[3:4])
    tiles, wide, columns = middle.shape
    middle = middle.reshape(2 * tiles, wide // 2, columns)
    return fine, middle, coarse, coarsest


def solution(mesh):
    return jax.shard_map(
        on_device,
        mesh=mesh,
        in_specs=(
            P("group", "brick", None),
            P("group", "brick", None),
            P("group", "brick", None),
            P(),
        ),
        out_specs=(
            P("group", "brick", None),
            P("group", "brick", None),
            P(None, "brick", None),
            P(),
        ),
        check_vma=False,
    )
```

```python
import functools

import jax
import jax.numpy as jnp
from jax import lax
from jax.experimental import pallas as pl
from jax.experimental.pallas import tpu as pltpu
from jax.sharding import PartitionSpec as P


INTERPRET = False
MIB = 1024 * 1024
LANES = 128


def call(kernel, out_shapes, args, scratch=(), scalars=0, results=0, limit=12 * MIB):
    spec = pl.BlockSpec(memory_space=pltpu.VMEM)
    smem = pl.BlockSpec(memory_space=pltpu.SMEM)
    return pl.pallas_call(
        kernel,
        out_shape=[
            jax.ShapeDtypeStruct(shape, jnp.float32) if at < results else pltpu.VMEM(shape, jnp.float32)
            for at, shape in enumerate(out_shapes)
        ],
        in_specs=[smem] * scalars + [spec] * (len(args) - scalars),
        out_specs=[spec] * len(out_shapes),
        scratch_shapes=[pltpu.VMEM(shape, jnp.float32) for shape in scratch],
        compiler_params=pltpu.CompilerParams(vmem_limit_bytes=limit),
        interpret=INTERPRET,
    )(*args)


def iota(shape, axis):
    return lax.broadcasted_iota(jnp.int32, shape, axis)


def odd(shape, period=None, plus=0):
    rows = iota(shape, 0)
    if period is not None:
        rows = rows % period
    return ((rows + iota(shape, 1) + plus) & 1) == 1


def same_member(shape, quarter):
    rows = iota(shape, 0)
    return ((rows % quarter + rows // quarter + iota(shape, 1)) & 1) == 0


def roll(value, shift, axis):
    return pltpu.roll(value, shift % value.shape[axis], axis)


def both_ways(value, axis):
    return roll(value, 1, axis) + roll(value, -1, axis)


def newton(around, value, mass, source):
    curve = mass * (value * value)
    over = (around + source) + 2.0 * (curve * value)
    under = (6.0 + mass) + 3.0 * curve
    guess = pl.reciprocal(under, approx=True)
    guess = guess * (2.0 - under * guess)
    return over * guess


def residual(around, value, mass, source):
    return (around - 6.0 * value) - mass * (value * value * value + value) + source


def pooled(rows, pool):
    high = rows.astype(jnp.bfloat16)
    rest = rows - high.astype(jnp.float32)
    middle = rest.astype(jnp.bfloat16)
    low = (rest - middle.astype(jnp.float32)).astype(jnp.bfloat16)
    dot = functools.partial(jnp.dot, preferred_element_type=jnp.float32)
    return dot(high, pool) + (dot(middle, pool) + dot(low, pool))


def pool_matrix(width, columns):
    half = width // 2
    shape = (width, columns)
    return jnp.where(iota(shape, 0) // 2 == iota(shape, 1) % half, 1.0, 0.0).astype(jnp.bfloat16)


def half_sweep(field, mass, source, colour, low, high, most, beside=None, plus=0):
    mine, other = field[colour], field[1 - colour]
    limit, rows, columns = mine.shape
    is_odd = odd((rows, columns), plus=plus)
    beside = beside or (lambda value: both_ways(value, 1))
    together = max(k for k in range(1, most + 1) if (high - low) % k == 0)

    def step(turn, carry):
        start = low + turn * together
        near = [other[jnp.clip(start + k, 0, limit - 1)] for k in range(-1, together + 1)]
        fresh = []
        for k in range(together):
            first, second = (near[k], near[k + 2]) if colour == 0 else (near[k + 2], near[k])
            around = near[k + 1] + jnp.where(is_odd, second, first)
            around = around + both_ways(near[k + 1], 0) + beside(near[k + 1])
            fresh.append(newton(around, mine[start + k], mass[colour][start + k], source[colour][start + k]))
        for k in range(together):
            mine[start + k] = fresh[k]
        return carry

    turns = (high - low) // together
    if turns == 1:
        step(0, 0)
    else:
        lax.fori_loop(0, turns, step, 0)


def two_sweeps(count, field, mass, source, most, plus=0):
    limit = field[0].shape[0]
    half_sweep(field, mass, source, 0, 0, limit, most, plus=plus)
    half_sweep(field, mass, source, 1, 1, limit - 1, most, plus=plus)

    @pl.when(count >= 2)
    def _():
        half_sweep(field, mass, source, 0, 1, limit - 1, most, plus=plus)
        half_sweep(field, mass, source, 1, 2, limit - 2, most, plus=plus)


def source_from_defect(field, mass, source, beside=None, inner=None, plus=0):
    limit, rows, columns = field[0].shape
    is_odd = odd((rows, columns), plus=plus)
    beside = beside or (lambda value: both_ways(value, 1))
    for index in inner or range(limit):
        for colour in range(2):
            other = field[1 - colour]
            first, second = other[max(index - 1, 0)], other[min(index + 1, limit - 1)]
            if colour == 1:
                first, second = second, first
            around = other[index] + jnp.where(is_odd, second, first)
            around = around + both_ways(other[index], 0) + beside(other[index])
            source[colour][index] = source[colour][index] - residual(
                around, field[colour][index], mass[colour][index], 0.0
            )


def shifted(value, axis, by):
    count = lax.axis_size(axis)
    return lax.ppermute(value, axis, [(i, (i + by) % count) for i in range(count)])


def swapped_cores(value):
    count = lax.axis_size("brick")
    return lax.ppermute(value, "brick", [(i, i ^ 1) for i in range(count)])


def swapped_chips(value):
    count = lax.axis_size("brick")
    return lax.ppermute(value, "brick", [(i, (i + 1 if i % 2 else i - 1) % count) for i in range(count)])


def place_of(axis, modulus=None):
    place = lax.axis_index(axis)
    return (place if modulus is None else place & (modulus - 1)).astype(jnp.int32).reshape(1)


def kept_pairs(pairs):
    quarter = pairs // 4
    kept = list(range(quarter)) + list(range(pairs - quarter, pairs))
    return kept, list(range(quarter, pairs - quarter))


def ride_right(row, mass, source, rider):
    mass = jnp.where(row < 2, roll(rider, -2, 0), jnp.where(row == 4, roll(rider, -1, 0), mass))
    return mass, jnp.where(row < 2, roll(rider, 2, 0), source)


def ride_left(row, mass, source, rider):
    mass = jnp.where(row > 5, roll(rider, 2, 0), jnp.where(row == 3, roll(rider, 1, 0), mass))
    return mass, jnp.where(row > 5, roll(rider, -2, 0), source)


def rider_from_left(row, mass, source):
    return jnp.where(row < 4, roll(mass, 2, 0), jnp.where(row == 5, roll(mass, 1, 0), roll(source, -2, 0)))


def rider_from_right(row, mass, source):
    return jnp.where(row < 2, roll(source, 2, 0), jnp.where(row == 2, roll(mass, -1, 0), roll(mass, -2, 0)))


def pack_kernel(count, *refs):
    blocks, (own, to_left, to_right, edge_left, edge_right, held, arrived) = refs[:count], refs[count:]
    pairs = own.shape[2]
    rows, columns = own.shape[3:]
    is_odd = odd((rows, columns))
    row = iota((rows, columns), 0)
    upper = row < rows // 2
    parts = arrived.shape[1]
    some = 2 * pairs // parts

    def part_of(at, part):
        span = pl.ds(some * part, some)
        return pltpu.make_async_copy(blocks[at].at[span], held.at[at, span], arrived.at[at, part])

    def packed(at, pair):
        even, next_one = held[at, 2 * pair], held[at, 2 * pair + 1]
        red = jnp.where(is_odd, next_one, even)
        black = jnp.where(is_odd, even, next_one)
        own[at, 0, pair] = red
        own[at, 1, pair] = black
        if pair < 2:
            edge_left[at, 0, pair] = red
            edge_left[at, 1, pair] = black
        if pair >= pairs - 2:
            edge_right[at, 0, pair - pairs + 2] = red
            edge_right[at, 1, pair - pairs + 2] = black
        turned = roll(black, rows // 2, 0)
        return jnp.where(upper, red, turned), jnp.where(upper, turned, red)

    for at in range(count):
        for part in range(parts):
            part_of(at, part).start()
    for part in range(parts):
        part_of(0, part).wait()
        for pair in range(some // 2 * part, some // 2 * (part + 1)):
            to_left[pair], to_right[pair] = packed(0, pair)
    if count > 1:
        for at in (1, 2):
            for part in range(parts):
                part_of(at, part).wait()
        kept, riders = kept_pairs(pairs)
        half = pairs // 2
        for k, (pair, other) in enumerate(zip(kept, riders)):
            mass, source = packed(1, pair), packed(2, pair)
            other_mass, rider = packed(1, other), packed(2, other)
            for side, (message, ride) in enumerate(((to_left, ride_left), (to_right, ride_right))):
                one, two = ride(row, mass[side], source[side], rider[side])
                message[pairs + k] = one
                message[pairs + half + k] = two
                message[2 * pairs + k] = other_mass[side]


def corner_kernel(y_left, y_right, to_left, to_right):
    tiles, rows, columns = y_left.shape
    pairs = tiles if to_left.shape[0] == 3 else tiles * 2 // 5
    from_right = iota((rows, columns), 0) % (rows // 2) < rows // 4
    for out, near, far, kept in ((to_left, 0, 1, 0), (to_right, pairs - 1, pairs - 2, pairs // 2 - 1)):
        out[0] = y_left[near]
        out[1] = y_right[near]
        both = [far] if out.shape[0] == 3 else [far, pairs + kept, pairs + pairs // 2 + kept]
        for k, at in enumerate(both):
            out[2 + k] = jnp.where(from_right, y_right[at], y_left[at])


def first_exchange(blocks):
    count = len(blocks)
    rows, wide, columns = blocks[0].shape
    pairs = rows // 2
    tile = (wide, columns)
    shapes = [(count, 2, pairs, *tile)] + [(pairs if count == 1 else pairs * 5 // 2, *tile)] * 2
    shapes += [(count, 2, 2, *tile)] * 2
    own, to_left, to_right, edge_left, edge_right = pl.pallas_call(
        functools.partial(pack_kernel, count),
        out_shape=[pltpu.VMEM(shape, jnp.float32) for shape in shapes],
        in_specs=[pl.BlockSpec(memory_space=pltpu.HBM)] * count,
        out_specs=[pl.BlockSpec(memory_space=pltpu.VMEM)] * len(shapes),
        scratch_shapes=[
            pltpu.VMEM((count, rows, *tile), jnp.float32),
            pltpu.SemaphoreType.DMA((count, 4)),
        ],
        compiler_params=pltpu.CompilerParams(vmem_limit_bytes=12 * MIB),
    )(*[pltpu.with_memory_space_constraint(block, pltpu.HBM) for block in blocks])
    y_left = shifted(to_right, "brick", 1)
    y_right = shifted(to_left, "brick", -1)
    x_left = shifted(edge_right, "group", 1)
    x_right = shifted(edge_left, "group", -1)
    corners = call(corner_kernel, [(3 if count == 1 else 5, *tile)] * 2, [y_left, y_right])
    c_left = shifted(corners[1], "group", 1)
    c_right = shifted(corners[0], "group", -1)
    return own, x_left, x_right, y_left, y_right, c_left, c_right


def assemble_first(window, at, own, x_left, x_right, y_left, y_right, c_left, c_right):
    pairs, wide, columns = own.shape[2:]
    row = iota((wide, columns), 0)
    upper = row < wide // 2
    kept, riders = kept_pairs(pairs)

    def put(to, red, black, from_left, from_right):
        window[0][to, :wide] = red
        window[0][to, wide:] = jnp.where(upper, from_right, from_left)
        window[1][to, :wide] = black
        window[1][to, wide:] = roll(jnp.where(upper, from_left, from_right), wide // 2, 0)

    for pair in range(pairs):
        if at == 0:
            left, right = y_left[pair], y_right[pair]
        elif pair in kept:
            place = pairs + (at - 1) * (pairs // 2) + kept.index(pair)
            left, right = y_left[place], y_right[place]
        elif at == 1:
            place = 2 * pairs + riders.index(pair)
            left, right = y_left[place], y_right[place]
        else:
            place = pairs + riders.index(pair)
            left = rider_from_left(row, y_left[place], y_left[place + pairs // 2])
            right = rider_from_right(row, y_right[place], y_right[place + pairs // 2])
        put(pair + 2, own[at, 0, pair], own[at, 1, pair], left, right)
    for k in range(2):
        for to, near, x_side, corner in ((k, k == 1, x_left, c_left), (pairs + 2 + k, k == 0, x_right, c_right)):
            if at == 0:
                left, right = (corner[0], corner[1]) if near else (corner[2], corner[2])
            else:
                left = right = corner[2 + at]
            put(to, x_side[at, 0, k], x_side[at, 1, k], left, right)


def first_kernel(sweeps, *refs):
    fresh, fixed = refs[:7], refs[7:14]
    fine, nxt, edge_left, edge_right, *windows, tall = refs[14:]
    field, mass, source = windows[0:2], windows[2:4], windows[4:6]
    count = sweeps[0]
    assemble_first(field, 0, *fresh)
    assemble_first(mass, 1, *fixed)
    assemble_first(source, 2, *fixed)
    pairs, wide, columns = fresh[0].shape[2:]
    two_sweeps(count, field, mass, source, 2)
    is_odd = odd((wide, columns))
    row = iota((wide, columns), 0)
    top, bottom = row == 0, row == wide - 1

    def unpack(pair, carry):
        red, black = field[0][pair + 2, :wide], field[1][pair + 2, :wide]
        fine[2 * pair] = jnp.where(is_odd, black, red)
        fine[2 * pair + 1] = jnp.where(is_odd, red, black)
        return carry

    lax.fori_loop(0, pairs, unpack, 0, unroll=4)

    def keep(index, value):
        for c in range(columns // LANES):
            tall[c, index] = value[:, c * LANES : (c + 1) * LANES]

    @pl.when(count <= 2)
    def _():
        def step(pair, carry):
            total = jnp.zeros((wide, columns), jnp.float32)
            for colour in range(2):
                other = field[1 - colour][pair + 2, :wide]
                first = jnp.where(pair == 0, 0.0, field[1 - colour][pair + 1, :wide])
                second = jnp.where(pair == pairs - 1, 0.0, field[1 - colour][pair + 3, :wide])
                if colour == 1:
                    first, second = second, first
                around = other + jnp.where(is_odd, second, first) + both_ways(other, 1)
                around = around + jnp.where(bottom, 0.0, roll(other, -1, 0))
                around = around + jnp.where(top, 0.0, roll(other, 1, 0))
                at = (pair + 2, slice(0, wide))
                total = total + residual(around, field[colour][at], mass[colour][at], source[colour][at])
            keep(pair, field[0][at] + field[1][at])
            keep(pairs + pair, total)
            keep(2 * pairs + pair, mass[0][at] + mass[1][at])
            return carry

        lax.fori_loop(0, pairs, step, 0, unroll=2)
        low = jnp.where(is_odd, field[1][2, :wide], field[0][2, :wide])
        high = jnp.where(is_odd, field[0][pairs + 1, :wide], field[1][pairs + 1, :wide])
        half, tiles, quarter = columns // 2, pairs // 2, wide // 2
        keep(3 * pairs, high)
        keep(3 * pairs + 1, low)
        lines = (3 * pairs + 2) * wide // 2
        flat = tall.reshape(columns // LANES, 2 * lines, LANES)

        def every_other(start):
            parts = [flat[c, pl.ds(start, lines, stride=2)] for c in range(columns // LANES)]
            return jnp.concatenate(parts, 1)

        firsts, seconds = every_other(0), every_other(1)
        whole = (iota((wide, columns), 0)) % quarter
        y_faces = []
        for t in range(tiles):
            last, head = seconds[t * wide : (t + 1) * wide], firsts[t * wide : (t + 1) * wide]
            y_faces.append(
                jnp.where(
                    whole == 0,
                    roll(last, quarter + 1, 0),
                    jnp.where(whole == quarter - 1, roll(head, quarter - 1, 0), 0.0),
                )
            )
        narrow = pooled(jnp.concatenate([firsts + seconds] + y_faces, 0), pool_matrix(columns, half))
        is_odd_half = odd((wide, half), quarter)
        is_even = same_member((wide, half), quarter)

        def packed(index, factor):
            tile = narrow[index * wide : (index + 1) * wide] * factor
            return jnp.where(is_odd_half, roll(tile, quarter, 0), tile)

        face_x = packed(3 * tiles, 0.5)
        for t in range(tiles):
            values = [
                packed(t, 0.125),
                packed(tiles + t, 0.5),
                packed(2 * tiles + t, 0.5),
                packed(3 * tiles + 1 + t, 0.5),
            ]
            for at, value in enumerate(values):
                nxt[at, t] = value
                if t < 2:
                    if at == 1 and t == 1:
                        value = jnp.where(is_even, value, face_x)
                    edge_left[at, t] = value
                if t >= tiles - 2:
                    if at == 1 and t == tiles - 2:
                        value = jnp.where(is_even, face_x, value)
                    edge_right[at, t - tiles + 2] = value
        nxt[4, 0] = face_x
        for t in range(1, tiles):
            nxt[4, t] = jnp.zeros((wide, half), jnp.float32)


def first_level(field, mass, source, count):
    rows, wide, columns = field.shape
    pairs = rows // 2
    half, tiles = columns // 2, pairs // 2
    window = (pairs + 4, 2 * wide, columns)
    outs = [
        (rows, wide, columns),
        (5, tiles, wide, half),
        (4, 2, wide, half),
        (4, 2, wide, half),
    ]

    def run(fresh, fixed, left):
        scratch = [window] * 6 + [(columns // LANES, 3 * pairs + 2, wide, LANES)]
        return call(first_kernel, outs, [left, *fresh, *fixed], scratch, 1, 1, 24 * MIB)

    parts = first_exchange([field, mass, source])
    once = run(parts, parts, count)
    return lax.cond(
        count[0] > 2,
        lambda given: run(first_exchange([given[0]]), parts, count - 2),
        lambda given: given,
        once,
    )


def second_prepare_kernel(own, x_left, x_right, extended, to_left, to_right, faces):
    tiles, wide, columns = own.shape[1:]
    quarter = wide // 2
    row_of = iota((wide, columns), 0) % quarter
    is_even = same_member((wide, columns), quarter)
    face_x = own[4, 0]
    for t in range(tiles + 4):
        if t < 2:
            source, k = x_left, t
        elif t < tiles + 2:
            source, k = own, t - 2
        else:
            source, k = x_right, t - tiles - 2
        defect = source[1, k]
        if t == 1:
            defect = defect + jnp.where(is_even, 0.0, face_x)
        if t == 2:
            defect = defect + jnp.where(is_even, x_left[1, 0], 0.0)
        if t == tiles + 1:
            defect = defect + jnp.where(is_even, 0.0, x_right[1, 1])
        if t == tiles + 2:
            defect = defect + jnp.where(is_even, face_x, 0.0)
        face_y = source[3, k]
        faces[t] = face_y
        for at in range(3):
            value = defect if at == 1 else source[at, k]
            extended[at, t] = value
            to_left[at, t] = jnp.where(row_of == quarter - 1, face_y, value) if at == 1 else value
            to_right[at, t] = jnp.where(row_of == 0, face_y, value) if at == 1 else value


def assemble_second(window, to, tile, left, right):
    wide = tile.shape[0]
    quarter = wide // 2
    upper = iota(tile.shape, 0) < quarter
    window[0][to, :wide] = jnp.where(upper, tile, roll(right, quarter, 0))
    window[0][to, wide:] = roll(left, quarter, 0)
    window[1][to, :wide] = jnp.where(upper, roll(tile, quarter, 0), right)
    window[1][to, wide:] = left


def second_finish(count, field, mass, source, middle, packed, nxt, tall):
    limit, rows, columns = field[0].shape
    pairs = limit - 4
    wide = rows // 2
    quarter = wide // 2
    two_sweeps(count, field, mass, source, 4)
    is_odd = odd((wide, columns), quarter)
    row = iota((wide, columns), 0)
    upper = row < quarter
    top, bottom = row == 0, row == quarter - 1
    for pair in range(pairs):
        red, black = field[0][pair + 2, :wide], field[1][pair + 2, :wide]
        tile = jnp.where(upper, red, roll(black, quarter, 0))
        packed[pair] = tile
        plain = jnp.where(is_odd, roll(tile, quarter, 0), tile)
        middle[2 * pair] = plain[:quarter]
        middle[2 * pair + 1] = plain[quarter:]

    @pl.when(count <= 2)
    def _():
        for pair in range(pairs):
            total = jnp.zeros((wide, columns), jnp.float32)
            for colour in range(2):
                other = field[1 - colour][pair + 2, :wide]
                around = other + both_ways(other, 1)
                around = around + jnp.where(bottom, 0.0, roll(other, -1, 0))
                around = around + jnp.where(top, 0.0, roll(other, 1, 0))
                first = field[1 - colour][pair + 1, :wide] if pair else 0.0
                second = field[1 - colour][pair + 3, :wide] if pair < pairs - 1 else 0.0
                if colour == 1:
                    first, second = second, first
                around = around + jnp.where(is_odd, second, first)
                at = (pair + 2, slice(0, wide))
                total = total + residual(around, field[colour][at], mass[colour][at], source[colour][at])
            values = [field[0][at] + field[1][at], total, mass[0][at] + mass[1][at]]
            for at, value in enumerate(values):
                for r in range(quarter):
                    tall[at, r, pair : pair + 1] = value[r : r + 1]
        low = jnp.where(is_odd, field[1][2, :wide], field[0][2, :wide])
        high = jnp.where(is_odd, field[0][pairs + 1, :wide], field[1][pairs + 1, :wide])
        pieces = []
        for at in range(3):
            for r in range(0, quarter, 2):
                pieces.append((tall[at, r] + tall[at, r + 1]) * (0.125 if at == 0 else 0.5))
        pieces.append(tall[0, 0] * 0.5)
        pieces.append(tall[0, quarter - 1] * 0.5)
        face = jnp.where(upper, high, roll(low, quarter, 0))
        pieces.append((face + roll(face, -1, 0)) * 0.5)
        wide_rows = jnp.concatenate(pieces, 0)
        nxt[...] = pooled(wide_rows, pool_matrix(columns, columns // 2)).reshape(nxt.shape)


def second_kernel(sweeps, extended, left, right, faces, middle, packed, nxt, *rest):
    mass, source, field, tall = rest[0:2], rest[2:4], rest[4:6], rest[6]
    limit, wide, columns = extended.shape[1:]
    quarter = wide // 2
    row_of = iota((wide, columns), 0) % quarter
    top, bottom = row_of == 0, row_of == quarter - 1
    for t in range(limit):
        assemble_second(field, t, extended[0, t], left[0, t], right[0, t])
        assemble_second(mass, t, extended[2, t], left[2, t], right[2, t])
        one, two, face = left[1, t], right[1, t], faces[t]
        tile = extended[1, t] + jnp.where(top, one, 0.0) + jnp.where(bottom, two, 0.0)
        one = one + jnp.where(bottom, face, 0.0)
        two = two + jnp.where(top, face, 0.0)
        assemble_second(source, t, tile, one, two)
    source_from_defect(field, mass, source)
    second_finish(sweeps[0], field, mass, source, middle, packed, nxt, tall)


def second_again_kernel(sweeps, extended, left, right, *rest):
    mass, source = rest[0:2], rest[2:4]
    middle, packed, nxt, *field, tall = rest[4:]
    for t in range(extended.shape[0]):
        assemble_second(field, t, extended[t], left[t], right[t])
    second_finish(sweeps[0], field, mass, source, middle, packed, nxt, tall)


def second_level(parts, edge_left, edge_right, count):
    tiles, wide, columns = parts.shape[1:]
    limit = tiles + 4
    x_left = shifted(edge_right, "group", 1)
    x_right = shifted(edge_left, "group", -1)
    three = (3, limit, wide, columns)
    extended, to_left, to_right, faces = call(
        second_prepare_kernel, [three, three, three, (limit, wide, columns)], [parts, x_left, x_right]
    )
    left = shifted(to_right, "brick", 1)
    right = shifted(to_left, "brick", -1)
    window = (limit, 2 * wide, columns)
    outs = [(2 * tiles, wide // 2, columns), (tiles, wide, columns), (9, tiles, columns // 2)]
    scratch = [window, window, (3, wide // 2, tiles, columns)]
    args = [count, extended, left, right, faces]
    middle, packed, nxt, *fixed = call(second_kernel, outs + [window] * 4, args, scratch, 1, 1)

    def again(given):
        packed = given[1]
        x_left = shifted(packed[-2:], "group", 1)
        x_right = shifted(packed[:2], "group", -1)
        extended = jnp.concatenate([x_left, packed, x_right], 0)
        left = shifted(extended, "brick", 1)
        right = shifted(extended, "brick", -1)
        return list(call(second_again_kernel, outs, [count - 2, extended, left, right, *fixed], scratch, 1, 1))

    done = lax.cond(count[0] > 2, again, lambda given: given, [middle, packed, nxt])
    return done[0], done[2]


def third_prepare_kernel(group, *refs):
    blocks, out = refs[:-1], refs[-1]
    count = len(blocks)
    rows, columns = blocks[0].shape[1:]
    row = iota((rows, columns), 0)
    for b in range(count):
        span = pl.ds(pl.multiple_of(((group[0] + b) % count) * rows, rows), rows)
        before, after = blocks[b - 1][8], blocks[(b + 1) % count][8]
        for at in range(8):
            value = blocks[b][at]
            if at in (2, 3):
                high = before[2 * (at - 2) : 2 * (at - 2) + 1]
                low = after[rows // 2 + 2 * (at - 2) : rows // 2 + 2 * (at - 2) + 1]
                value = value + jnp.where(row == 0, high, 0.0) + jnp.where(row == rows - 1, low, 0.0)
            out[at, span] = value


def third_chip_kernel(core, own, other, chip, face):
    edge = core[0]
    for at in range(3):
        values = [own[2 * at + edge], own[2 * at + 1 - edge], other[2 * at + edge], other[2 * at + 1 - edge]]
        if at == 1:
            values[1] = values[1] + other[6 + edge]
            values[2] = values[2] + own[7 - edge]
        for k in range(4):
            chip[4 * at + k] = values[k]
    chip[12] = own[6 + edge]
    face[0] = other[7 - edge]


def third_finish(sweeps, core, field, mass, source, coarse, packed, message, tall):
    rows, columns = field[0].shape[1:]
    is_odd = odd((rows, columns), plus=core[0])
    count = sweeps[0]
    two_sweeps(count, field, mass, source, 6, core[0])
    red, black = field[0][2], field[1][2]
    one, two = jnp.where(is_odd, black, red), jnp.where(is_odd, red, black)
    for colour in range(2):
        for k in range(2):
            packed[2 * colour + k] = field[colour][2 + k]
    tall[:rows] = jnp.where(core[0] == 0, one, two)
    tall[rows : 2 * rows] = jnp.where(core[0] == 0, two, one)
    for r in range(rows):
        coarse[2 * r : 2 * r + 1] = tall[r : r + 1]
        coarse[2 * r + 1 : 2 * r + 2] = tall[rows + r : rows + r + 1]

    @pl.when(count <= 2)
    def _():
        totals = []
        for q in (2, 3):
            total = jnp.zeros((rows, columns), jnp.float32)
            for colour in range(2):
                other = field[1 - colour]
                beyond = inner_only(is_odd, other[5 - q], q, colour)
                around = other[q] + beyond + both_ways(other[q], 0) + both_ways(other[q], 1)
                total = total + residual(around, field[colour][q], mass[colour][q], source[colour][q])
            totals.append(total * 0.5)
        red, black = field[0][3], field[1][3]
        last = jnp.where(is_odd, red, black)
        pieces = [(field[0][q] + field[1][q]) * 0.125 for q in (2, 3)] + totals
        pieces += [(mass[0][q] + mass[1][q]) * 0.5 for q in (2, 3)] + [one * 0.5, last * 0.5]
        tall[...] = pooled(jnp.concatenate(pieces, 0), pool_matrix(columns, columns))
        half = rows // 2
        narrow = tall[pl.ds(0, 8 * half, stride=2)] + tall[pl.ds(1, 8 * half, stride=2)]
        lower = (iota((half, columns), 1) // (columns // 2)) == core[0]
        tiles = []
        for at in range(4):
            first, second = narrow[2 * at * half : (2 * at + 1) * half], narrow[(2 * at + 1) * half : (2 * at + 2) * half]
            tiles.append(jnp.where(lower, first, second))
        for at in range(2):
            tile = jnp.where(core[0] == 0, tiles[at], tiles[2 + at])
            for c in range(message.shape[0]):
                message[c, at] = tile


def inner_only(is_odd, inner, q, colour):
    above = is_odd if colour == 0 else jnp.logical_not(is_odd)
    return jnp.where(above, inner, 0.0) if q == 2 else jnp.where(above, 0.0, inner)


def pack_pair(window, at, even, next_one, is_odd):
    window[0][at] = jnp.where(is_odd, next_one, even)
    window[1][at] = jnp.where(is_odd, even, next_one)


def third_kernel(sweeps, core, chip, face, near, far, coarse, packed, message, *rest):
    mass, source, field, tall = rest[0:2], rest[2:4], rest[4:6], rest[6]
    rows, columns = chip.shape[1:]
    is_odd = odd((rows, columns), plus=core[0])
    for at, window in enumerate((field, source, mass)):
        side = [near[4 * at + k] for k in range(4)]
        own = [chip[4 * at + k] for k in range(4)]
        beyond = [far[4 * at + k] for k in range(4)]
        if at == 1:
            side[0] = side[0] + chip[12]
            own[0] = own[0] + near[12]
            own[3] = own[3] + far[12]
            beyond[0] = beyond[0] + face[0]
        line = side[::-1] + own + beyond
        for q in range(6):
            pack_pair(window, q, line[2 * q], line[2 * q + 1], is_odd)
    source_from_defect(field, mass, source, plus=core[0])
    third_finish(sweeps, core, field, mass, source, coarse, packed, message, tall)


def third_again_kernel(sweeps, core, chip, near, far, *rest):
    mass, source = rest[0:2], rest[2:4]
    coarse, packed, message, *field, tall = rest[4:]
    for colour in range(2):
        for k in range(2):
            field[colour][1 - k] = near[2 * colour + k]
            field[colour][2 + k] = chip[2 * colour + k]
            field[colour][4 + k] = far[2 * colour + k]
    third_finish(sweeps, core, field, mass, source, coarse, packed, message, tall)


def third_level(part, count, core):
    groups, chips = lax.axis_size("group"), lax.axis_size("brick") // 2
    tile_rows, columns = part.shape[1:]
    rows = groups * tile_rows
    blocks = [part] + [shifted(part, "group", -d) for d in range(1, groups)]
    (own,) = call(third_prepare_kernel, [(8, rows, columns)], [place_of("group"), *blocks], (), 1)
    chip, face = call(
        third_chip_kernel, [(13, rows, columns), (1, rows, columns)], [core, own, swapped_cores(own)], (), 1
    )
    near = swapped_chips(chip)
    far = swapped_cores(near)
    window = (6, rows, columns)
    outs = [(2 * rows, columns), (4, rows, columns), (chips, 2, rows // 2, columns)]
    scratch = [window, window, (8 * rows, columns)]
    args = [count, core, chip, face, near, far]
    coarse, packed, message, *fixed = call(third_kernel, outs + [window] * 4, args, scratch, 2, 1)

    def again(given):
        packed = given[1]
        near = swapped_chips(packed)
        args = [count - 2, core, packed, near, swapped_cores(near), *fixed]
        return list(call(third_again_kernel, outs, args, scratch, 2, 1))

    done = lax.cond(count[0] > 2, again, lambda given: given, [coarse, packed, message])
    return done[0].reshape(rows, 2, columns), done[2]


def fourth_kernel(sweeps, core, own, other, out, *windows):
    field, mass, source = windows[0:2], windows[2:4], windows[4:6]
    chips, _, rows, columns = own.shape
    tiles, half = chips // 2, columns // 2
    lane = iota((rows, columns), 1)
    low = lane < half
    is_odd = odd((rows, columns))
    first, last = lane % half == 0, lane % half == half - 1

    def turned(value):
        return roll(value, half, 1)

    def beside(value):
        after = jnp.where(last, roll(value, half - 1, 1), roll(value, -1, 1))
        return after + jnp.where(first, roll(value, 1 - half, 1), roll(value, 1, 1))

    def put(window, t, one, two):
        one, two = jnp.where(is_odd, turned(one), one), jnp.where(is_odd, turned(two), two)
        window[0][t + 1] = jnp.where(low, one, turned(two))
        window[1][t + 1] = jnp.where(low, turned(one), two)

    def repeat(window, colour):
        window[colour][0] = turned(window[colour][tiles])
        window[colour][tiles + 1] = turned(window[colour][1])

    def load(one, two):
        def defect(t):
            before, after = (t + chips - 1) % chips, (t + 1) % chips
            return one[t, 1] + turned(jnp.where(low, two[after, 1], two[before, 1]))

        for t in range(tiles):
            put(field, t, one[t, 0], one[t + tiles, 0])
            put(mass, t, two[t, 0], two[t + tiles, 0])
            put(source, t, defect(t), defect(t + tiles))

    @pl.when(core[0] == 0)
    def _():
        load(own, other)

    @pl.when(core[0] == 1)
    def _():
        load(other, own)

    for colour in range(2):
        repeat(field, colour)
    source_from_defect(field, mass, source, beside, range(1, tiles + 1))

    def one_sweep(step, carry):
        for colour in range(2):
            half_sweep(field, mass, source, colour, 1, tiles + 1, 8, beside)
            repeat(field, colour)
        return carry

    lax.fori_loop(0, sweeps[0], one_sweep, 0)
    for t in range(tiles):
        red, black = field[0][t + 1], field[1][t + 1]
        one, two = jnp.where(low, red, turned(black)), jnp.where(low, turned(red), black)
        for at, value in ((t, one), (t + tiles, two)):
            out[:, at * columns : (at + 1) * columns] = jnp.where(is_odd, turned(value), value)


def fourth_level(message, count, core):
    chips, _, rows, columns = message.shape
    cores = [[2 * chip + c for chip in range(chips)] for c in range(2)]
    own = lax.all_to_all(message, "brick", 0, 0, axis_index_groups=cores)
    other = swapped_cores(own)
    scratch = [(chips // 2 + 2, rows, columns)] * 6
    (out,) = call(fourth_kernel, [(rows, chips * columns)], [count, core, own, other], scratch, 2, 1)
    return out


def on_device(initial_field, mass, source, sweeps):
    fine, parts, edge_left, edge_right = first_level(initial_field, mass, source, sweeps[0:1])
    middle, part = second_level(parts, edge_left, edge_right, sweeps[1:2])
    core = place_of("brick", 2)
    coarse, message = third_level(part, sweeps[2:3], core)
    coarsest = fourth_level(message, sweeps[3:4], core)
    return fine, middle, coarse, coarsest


def solution(mesh):
    return jax.shard_map(
        on_device,
        mesh=mesh,
        in_specs=(
            P("group", "brick", None),
            P("group", "brick", None),
            P("group", "brick", None),
            P(),
        ),
        out_specs=(
            P("group", "brick", None),
            P("group", "brick", None),
            P(None, "brick", None),
            P(),
        ),
        check_vma=False,
    )
```

```python
import functools

import jax
import jax.numpy as jnp
from jax import lax
from jax.experimental import pallas as pl
from jax.experimental.pallas import tpu as pltpu
from jax.sharding import PartitionSpec as P


INTERPRET = False
MIB = 1024 * 1024
LANES = 128


def call(kernel, out_shapes, args, scratch=(), scalars=0, results=0, limit=12 * MIB):
    spec = pl.BlockSpec(memory_space=pltpu.VMEM)
    smem = pl.BlockSpec(memory_space=pltpu.SMEM)
    return pl.pallas_call(
        kernel,
        out_shape=[
            (pltpu.HBM if at < results else pltpu.VMEM)(shape, jnp.float32) for at, shape in enumerate(out_shapes)
        ],
        in_specs=[smem] * scalars + [spec] * (len(args) - scalars),
        out_specs=[pl.BlockSpec(memory_space=pltpu.HBM)] * results + [spec] * (len(out_shapes) - results),
        scratch_shapes=[pltpu.VMEM(shape, jnp.float32) for shape in [*scratch, *out_shapes[:results]]]
        + [pltpu.SemaphoreType.DMA] * results,
        compiler_params=pltpu.CompilerParams(vmem_limit_bytes=limit),
        interpret=INTERPRET,
    )(*args)


def iota(shape, axis):
    return lax.broadcasted_iota(jnp.int32, shape, axis)


def odd(shape, period=None, plus=0):
    rows = iota(shape, 0)
    if period is not None:
        rows = rows % period
    return ((rows + iota(shape, 1) + plus) & 1) == 1


def same_member(shape, quarter):
    rows = iota(shape, 0)
    return ((rows % quarter + rows // quarter + iota(shape, 1)) & 1) == 0


def roll(value, shift, axis):
    return pltpu.roll(value, shift % value.shape[axis], axis)


def both_ways(value, axis):
    return roll(value, 1, axis) + roll(value, -1, axis)


def newton(around, value, mass, source):
    curve = mass * (value * value)
    over = (around + source) + 2.0 * (curve * value)
    under = (6.0 + mass) + 3.0 * curve
    guess = pl.reciprocal(under, approx=True)
    guess = guess * (2.0 - under * guess)
    return over * guess


def residual(around, value, mass, source):
    return (around - 6.0 * value) - mass * (value * value * value + value) + source


def pooled(rows, pool):
    high = rows.astype(jnp.bfloat16)
    rest = rows - high.astype(jnp.float32)
    middle = rest.astype(jnp.bfloat16)
    low = (rest - middle.astype(jnp.float32)).astype(jnp.bfloat16)
    dot = functools.partial(jnp.dot, preferred_element_type=jnp.float32)
    return dot(high, pool) + (dot(middle, pool) + dot(low, pool))


def pool_matrix(width, columns):
    half = width // 2
    shape = (width, columns)
    return jnp.where(iota(shape, 0) // 2 == iota(shape, 1) % half, 1.0, 0.0).astype(jnp.bfloat16)


def half_sweep(field, mass, source, colour, low, high, most, beside=None, plus=0):
    mine, other = field[colour], field[1 - colour]
    limit, rows, columns = mine.shape
    is_odd = odd((rows, columns), plus=plus)
    beside = beside or (lambda value: both_ways(value, 1))
    together = max(k for k in range(1, most + 1) if (high - low) % k == 0)

    def step(turn, carry):
        start = low + turn * together
        near = [other[jnp.clip(start + k, 0, limit - 1)] for k in range(-1, together + 1)]
        fresh = []
        for k in range(together):
            first, second = (near[k], near[k + 2]) if colour == 0 else (near[k + 2], near[k])
            around = near[k + 1] + jnp.where(is_odd, second, first)
            around = around + both_ways(near[k + 1], 0) + beside(near[k + 1])
            fresh.append(newton(around, mine[start + k], mass[colour][start + k], source[colour][start + k]))
        for k in range(together):
            mine[start + k] = fresh[k]
        return carry

    turns = (high - low) // together
    if turns == 1:
        step(0, 0)
    else:
        lax.fori_loop(0, turns, step, 0)


def two_sweeps(count, field, mass, source, most, plus=0):
    limit = field[0].shape[0]
    half_sweep(field, mass, source, 0, 0, limit, most, plus=plus)
    half_sweep(field, mass, source, 1, 1, limit - 1, most, plus=plus)

    @pl.when(count >= 2)
    def _():
        half_sweep(field, mass, source, 0, 1, limit - 1, most, plus=plus)
        half_sweep(field, mass, source, 1, 2, limit - 2, most, plus=plus)


def source_from_defect(field, mass, source, beside=None, inner=None, plus=0):
    limit, rows, columns = field[0].shape
    is_odd = odd((rows, columns), plus=plus)
    beside = beside or (lambda value: both_ways(value, 1))
    for index in inner or range(limit):
        for colour in range(2):
            other = field[1 - colour]
            first, second = other[max(index - 1, 0)], other[min(index + 1, limit - 1)]
            if colour == 1:
                first, second = second, first
            around = other[index] + jnp.where(is_odd, second, first)
            around = around + both_ways(other[index], 0) + beside(other[index])
            source[colour][index] = source[colour][index] - residual(
                around, field[colour][index], mass[colour][index], 0.0
            )


def shifted(value, axis, by):
    count = lax.axis_size(axis)
    return lax.ppermute(value, axis, [(i, (i + by) % count) for i in range(count)])


def swapped_cores(value):
    count = lax.axis_size("brick")
    return lax.ppermute(value, "brick", [(i, i ^ 1) for i in range(count)])


def swapped_chips(value):
    count = lax.axis_size("brick")
    return lax.ppermute(value, "brick", [(i, (i + 1 if i % 2 else i - 1) % count) for i in range(count)])


def place_of(axis, modulus=None):
    place = lax.axis_index(axis)
    return (place if modulus is None else place & (modulus - 1)).astype(jnp.int32).reshape(1)


def kept_pairs(pairs):
    quarter = pairs // 4
    kept = list(range(quarter)) + list(range(pairs - quarter, pairs))
    return kept, list(range(quarter, pairs - quarter))


def ride_right(row, mass, source, rider):
    mass = jnp.where(row < 2, roll(rider, -2, 0), jnp.where(row == 4, roll(rider, -1, 0), mass))
    return mass, jnp.where(row < 2, roll(rider, 2, 0), source)


def ride_left(row, mass, source, rider):
    mass = jnp.where(row > 5, roll(rider, 2, 0), jnp.where(row == 3, roll(rider, 1, 0), mass))
    return mass, jnp.where(row > 5, roll(rider, -2, 0), source)


def rider_from_left(row, mass, source):
    return jnp.where(row < 4, roll(mass, 2, 0), jnp.where(row == 5, roll(mass, 1, 0), roll(source, -2, 0)))


def rider_from_right(row, mass, source):
    return jnp.where(row < 2, roll(source, 2, 0), jnp.where(row == 2, roll(mass, -1, 0), roll(mass, -2, 0)))


def pack_kernel(count, *refs):
    blocks, (own, to_left, to_right, edge_left, edge_right, held, arrived) = refs[:count], refs[count:]
    pairs = own.shape[2]
    rows, columns = own.shape[3:]
    is_odd = odd((rows, columns))
    row = iota((rows, columns), 0)
    upper = row < rows // 2
    parts = arrived.shape[1]
    some = 2 * pairs // parts

    def part_of(at, part):
        span = pl.ds(some * part, some)
        return pltpu.make_async_copy(blocks[at].at[span], held.at[at, span], arrived.at[at, part])

    def packed(at, pair):
        even, next_one = held[at, 2 * pair], held[at, 2 * pair + 1]
        red = jnp.where(is_odd, next_one, even)
        black = jnp.where(is_odd, even, next_one)
        own[at, 0, pair] = red
        own[at, 1, pair] = black
        if pair < 2:
            edge_left[at, 0, pair] = red
            edge_left[at, 1, pair] = black
        if pair >= pairs - 2:
            edge_right[at, 0, pair - pairs + 2] = red
            edge_right[at, 1, pair - pairs + 2] = black
        turned = roll(black, rows // 2, 0)
        return jnp.where(upper, red, turned), jnp.where(upper, turned, red)

    for at in range(count):
        for part in range(parts):
            part_of(at, part).start()
    for part in range(parts):
        part_of(0, part).wait()
        for pair in range(some // 2 * part, some // 2 * (part + 1)):
            to_left[pair], to_right[pair] = packed(0, pair)
    if count > 1:
        for at in (1, 2):
            for part in range(parts):
                part_of(at, part).wait()
        kept, riders = kept_pairs(pairs)
        half = pairs // 2
        for k, (pair, other) in enumerate(zip(kept, riders)):
            mass, source = packed(1, pair), packed(2, pair)
            other_mass, rider = packed(1, other), packed(2, other)
            for side, (message, ride) in enumerate(((to_left, ride_left), (to_right, ride_right))):
                one, two = ride(row, mass[side], source[side], rider[side])
                message[pairs + k] = one
                message[pairs + half + k] = two
                message[2 * pairs + k] = other_mass[side]


def corner_kernel(y_left, y_right, to_left, to_right):
    tiles, rows, columns = y_left.shape
    pairs = tiles if to_left.shape[0] == 3 else tiles * 2 // 5
    from_right = iota((rows, columns), 0) % (rows // 2) < rows // 4
    for out, near, far, kept in ((to_left, 0, 1, 0), (to_right, pairs - 1, pairs - 2, pairs // 2 - 1)):
        out[0] = y_left[near]
        out[1] = y_right[near]
        both = [far] if out.shape[0] == 3 else [far, pairs + kept, pairs + pairs // 2 + kept]
        for k, at in enumerate(both):
            out[2 + k] = jnp.where(from_right, y_right[at], y_left[at])


def pack_shapes(count, pairs, tile):
    shapes = [(count, 2, pairs, *tile)] + [(pairs if count == 1 else pairs * 5 // 2, *tile)] * 2
    return shapes + [(count, 2, 2, *tile)] * 2


def packed_blocks(blocks):
    count = len(blocks)
    rows, *tile = blocks[0].shape
    shapes = pack_shapes(count, rows // 2, tile)
    return pl.pallas_call(
        functools.partial(pack_kernel, count),
        out_shape=[pltpu.VMEM(shape, jnp.float32) for shape in shapes],
        in_specs=[pl.BlockSpec(memory_space=pltpu.HBM)] * count,
        out_specs=[pl.BlockSpec(memory_space=pltpu.VMEM)] * len(shapes),
        scratch_shapes=[
            pltpu.VMEM((count, rows, *tile), jnp.float32),
            pltpu.SemaphoreType.DMA((count, 4)),
        ],
        compiler_params=pltpu.CompilerParams(vmem_limit_bytes=12 * MIB),
    )(*[pltpu.with_memory_space_constraint(block, pltpu.HBM) for block in blocks])


def first_exchange(own, to_left, to_right, edge_left, edge_right):
    count, tile = own.shape[0], own.shape[3:]
    y_left = shifted(to_right, "brick", 1)
    y_right = shifted(to_left, "brick", -1)
    x_left = shifted(edge_right, "group", 1)
    x_right = shifted(edge_left, "group", -1)
    corners = call(corner_kernel, [(3 if count == 1 else 5, *tile)] * 2, [y_left, y_right])
    c_left = shifted(corners[1], "group", 1)
    c_right = shifted(corners[0], "group", -1)
    return own, x_left, x_right, y_left, y_right, c_left, c_right


def assemble_first(window, at, own, x_left, x_right, y_left, y_right, c_left, c_right):
    pairs, wide, columns = own.shape[2:]
    row = iota((wide, columns), 0)
    upper = row < wide // 2
    kept, riders = kept_pairs(pairs)

    def put(to, red, black, from_left, from_right):
        window[0][to, :wide] = red
        window[0][to, wide:] = jnp.where(upper, from_right, from_left)
        window[1][to, :wide] = black
        window[1][to, wide:] = roll(jnp.where(upper, from_left, from_right), wide // 2, 0)

    for pair in range(pairs):
        if at == 0:
            left, right = y_left[pair], y_right[pair]
        elif pair in kept:
            place = pairs + (at - 1) * (pairs // 2) + kept.index(pair)
            left, right = y_left[place], y_right[place]
        elif at == 1:
            place = 2 * pairs + riders.index(pair)
            left, right = y_left[place], y_right[place]
        else:
            place = pairs + riders.index(pair)
            left = rider_from_left(row, y_left[place], y_left[place + pairs // 2])
            right = rider_from_right(row, y_right[place], y_right[place + pairs // 2])
        put(pair + 2, own[at, 0, pair], own[at, 1, pair], left, right)
    for k in range(2):
        for to, near, x_side, corner in ((k, k == 1, x_left, c_left), (pairs + 2 + k, k == 0, x_right, c_right)):
            if at == 0:
                left, right = (corner[0], corner[1]) if near else (corner[2], corner[2])
            else:
                left = right = corner[2 + at]
            put(to, x_side[at, 0, k], x_side[at, 1, k], left, right)


def first_kernel(sweeps, *refs):
    halo, refs = refs[:7], refs[7:]
    fine, nxt, edge_left, edge_right, *refs = refs
    again, windows, field, rest = refs[:5], refs[5:9], refs[9:11], refs[11:]
    mass, source = windows[:2], windows[2:]
    for at, window in enumerate((field, mass, source)):
        assemble_first(window, at, *halo)
    first_finish(sweeps[0], field, mass, source, (fine, nxt, edge_left, edge_right), again, *rest)


def first_again_kernel(sweeps, *refs):
    halo, mass, source, outs, field, rest = refs[:7], refs[7:9], refs[9:11], refs[11:15], refs[15:17], refs[17:]
    assemble_first(field, 0, *halo)
    first_finish(sweeps[0] - 2, field, mass, source, outs, None, *rest)


def first_finish(count, field, mass, source, outs, again, tall, held, sent):
    fine, nxt, edge_left, edge_right = outs
    limit, rows, columns = field[0].shape
    pairs, wide = limit - 4, rows // 2
    two_sweeps(count, field, mass, source, 4)
    is_odd = odd((wide, columns))
    row = iota((wide, columns), 0)
    top, bottom = row == 0, row == wide - 1
    copy = pltpu.make_async_copy(held, fine, sent)

    if again is not None:

        @pl.when(count > 2)
        def _():
            own, to_left, to_right, *edges = again
            upper = row < wide // 2
            for pair in range(pairs):
                red, black = field[0][pair + 2, :wide], field[1][pair + 2, :wide]
                own[0, 0, pair] = red
                own[0, 1, pair] = black
                turned = roll(black, wide // 2, 0)
                to_left[pair] = jnp.where(upper, red, turned)
                to_right[pair] = jnp.where(upper, turned, red)
                for edge, first in zip(edges, (0, pairs - 2)):
                    if first <= pair < first + 2:
                        edge[0, 0, pair - first] = red
                        edge[0, 1, pair - first] = black

    def keep(index, value):
        for c in range(columns // LANES):
            tall[c, index] = value[:, c * LANES : (c + 1) * LANES]

    @pl.when(count <= 2)
    def _():
        for pair in range(pairs):
            red, black = field[0][pair + 2, :wide], field[1][pair + 2, :wide]
            held[2 * pair] = jnp.where(is_odd, black, red)
            held[2 * pair + 1] = jnp.where(is_odd, red, black)
        copy.start()

        def step(pair, carry):
            total = jnp.zeros((wide, columns), jnp.float32)
            for colour in range(2):
                other = field[1 - colour][pair + 2, :wide]
                first = jnp.where(pair == 0, 0.0, field[1 - colour][pair + 1, :wide])
                second = jnp.where(pair == pairs - 1, 0.0, field[1 - colour][pair + 3, :wide])
                if colour == 1:
                    first, second = second, first
                around = other + jnp.where(is_odd, second, first) + both_ways(other, 1)
                around = around + jnp.where(bottom, 0.0, roll(other, -1, 0))
                around = around + jnp.where(top, 0.0, roll(other, 1, 0))
                at = (pair + 2, slice(0, wide))
                total = total + residual(around, field[colour][at], mass[colour][at], source[colour][at])
            keep(pair, field[0][at] + field[1][at])
            keep(pairs + pair, total)
            keep(2 * pairs + pair, mass[0][at] + mass[1][at])
            return carry

        lax.fori_loop(0, pairs, step, 0, unroll=2)
        low = jnp.where(is_odd, field[1][2, :wide], field[0][2, :wide])
        high = jnp.where(is_odd, field[0][pairs + 1, :wide], field[1][pairs + 1, :wide])
        half, tiles, quarter = columns // 2, pairs // 2, wide // 2
        keep(3 * pairs, high)
        keep(3 * pairs + 1, low)
        lines = (3 * pairs + 2) * wide // 2
        flat = tall.reshape(columns // LANES, 2 * lines, LANES)

        def every_other(start):
            parts = [flat[c, pl.ds(start, lines, stride=2)] for c in range(columns // LANES)]
            return jnp.concatenate(parts, 1)

        firsts, seconds = every_other(0), every_other(1)
        whole = (iota((wide, columns), 0)) % quarter
        y_faces = []
        for t in range(tiles):
            last, head = seconds[t * wide : (t + 1) * wide], firsts[t * wide : (t + 1) * wide]
            y_faces.append(
                jnp.where(
                    whole == 0,
                    roll(last, quarter + 1, 0),
                    jnp.where(whole == quarter - 1, roll(head, quarter - 1, 0), 0.0),
                )
            )
        narrow = pooled(jnp.concatenate([firsts + seconds] + y_faces, 0), pool_matrix(columns, half))
        is_odd_half = odd((wide, half), quarter)
        is_even = same_member((wide, half), quarter)

        def packed(index, factor):
            tile = narrow[index * wide : (index + 1) * wide] * factor
            return jnp.where(is_odd_half, roll(tile, quarter, 0), tile)

        face_x = packed(3 * tiles, 0.5)
        for t in range(tiles):
            values = [
                packed(t, 0.125),
                packed(tiles + t, 0.5),
                packed(2 * tiles + t, 0.5),
                packed(3 * tiles + 1 + t, 0.5),
            ]
            for at, value in enumerate(values):
                nxt[at, t] = value
                if t < 2:
                    if at == 1 and t == 1:
                        value = jnp.where(is_even, value, face_x)
                    edge_left[at, t] = value
                if t >= tiles - 2:
                    if at == 1 and t == tiles - 2:
                        value = jnp.where(is_even, face_x, value)
                    edge_right[at, t - tiles + 2] = value
        nxt[4, 0] = face_x
        for t in range(1, tiles):
            nxt[4, t] = jnp.zeros((wide, half), jnp.float32)
        copy.wait()


def first_level(field, mass, source, count):
    rows, wide, columns = field.shape
    pairs = rows // 2
    half, tiles = columns // 2, pairs // 2
    window = (pairs + 4, 2 * wide, columns)
    outs = [
        (rows, wide, columns),
        (5, tiles, wide, half),
        (4, 2, wide, half),
        (4, 2, wide, half),
    ]

    tall = (columns // LANES, 3 * pairs + 2, wide, LANES)
    halo = first_exchange(*packed_blocks([field, mass, source]))
    every = outs + pack_shapes(1, pairs, (wide, columns)) + [window] * 4
    results = call(first_kernel, every, [count, *halo], [window, window, tall], 1, 1, 24 * MIB)
    once, more, fixed = results[:4], results[4:9], results[9:]

    def again(given):
        args = [count, *first_exchange(*more), *fixed]
        return list(call(first_again_kernel, outs, args, [window, window, tall], 1, 1, 24 * MIB))

    return lax.cond(count[0] > 2, again, lambda given: given, list(once))


def second_prepare_kernel(own, x_left, x_right, extended, to_left, to_right, faces):
    tiles, wide, columns = own.shape[1:]
    quarter = wide // 2
    row_of = iota((wide, columns), 0) % quarter
    is_even = same_member((wide, columns), quarter)
    face_x = own[4, 0]
    for t in range(tiles + 4):
        if t < 2:
            source, k = x_left, t
        elif t < tiles + 2:
            source, k = own, t - 2
        else:
            source, k = x_right, t - tiles - 2
        defect = source[1, k]
        if t == 1:
            defect = defect + jnp.where(is_even, 0.0, face_x)
        if t == 2:
            defect = defect + jnp.where(is_even, x_left[1, 0], 0.0)
        if t == tiles + 1:
            defect = defect + jnp.where(is_even, 0.0, x_right[1, 1])
        if t == tiles + 2:
            defect = defect + jnp.where(is_even, face_x, 0.0)
        face_y = source[3, k]
        faces[t] = face_y
        for at in range(3):
            value = defect if at == 1 else source[at, k]
            extended[at, t] = value
            to_left[at, t] = jnp.where(row_of == quarter - 1, face_y, value) if at == 1 else value
            to_right[at, t] = jnp.where(row_of == 0, face_y, value) if at == 1 else value


def assemble_second(window, to, tile, left, right):
    wide = tile.shape[0]
    quarter = wide // 2
    upper = iota(tile.shape, 0) < quarter
    window[0][to, :wide] = jnp.where(upper, tile, roll(right, quarter, 0))
    window[0][to, wide:] = roll(left, quarter, 0)
    window[1][to, :wide] = jnp.where(upper, roll(tile, quarter, 0), right)
    window[1][to, wide:] = left


def second_finish(count, field, mass, source, middle, packed, nxt, tall, held, sent):
    limit, rows, columns = field[0].shape
    pairs = limit - 4
    wide = rows // 2
    quarter = wide // 2
    two_sweeps(count, field, mass, source, 4)
    is_odd = odd((wide, columns), quarter)
    row = iota((wide, columns), 0)
    upper = row < quarter
    top, bottom = row == 0, row == quarter - 1
    for pair in range(pairs):
        red, black = field[0][pair + 2, :wide], field[1][pair + 2, :wide]
        tile = jnp.where(upper, red, roll(black, quarter, 0))
        packed[pair] = tile
        plain = jnp.where(is_odd, roll(tile, quarter, 0), tile)
        held[2 * pair] = plain[:quarter]
        held[2 * pair + 1] = plain[quarter:]
    copy = pltpu.make_async_copy(held, middle, sent)

    @pl.when(count <= 2)
    def _():
        copy.start()
        for pair in range(pairs):
            total = jnp.zeros((wide, columns), jnp.float32)
            for colour in range(2):
                other = field[1 - colour][pair + 2, :wide]
                around = other + both_ways(other, 1)
                around = around + jnp.where(bottom, 0.0, roll(other, -1, 0))
                around = around + jnp.where(top, 0.0, roll(other, 1, 0))
                first = field[1 - colour][pair + 1, :wide] if pair else 0.0
                second = field[1 - colour][pair + 3, :wide] if pair < pairs - 1 else 0.0
                if colour == 1:
                    first, second = second, first
                around = around + jnp.where(is_odd, second, first)
                at = (pair + 2, slice(0, wide))
                total = total + residual(around, field[colour][at], mass[colour][at], source[colour][at])
            values = [field[0][at] + field[1][at], total, mass[0][at] + mass[1][at]]
            for at, value in enumerate(values):
                for r in range(quarter):
                    tall[at, r, pair : pair + 1] = value[r : r + 1]
        low = jnp.where(is_odd, field[1][2, :wide], field[0][2, :wide])
        high = jnp.where(is_odd, field[0][pairs + 1, :wide], field[1][pairs + 1, :wide])
        pieces = []
        for at in range(3):
            for r in range(0, quarter, 2):
                pieces.append((tall[at, r] + tall[at, r + 1]) * (0.125 if at == 0 else 0.5))
        pieces.append(tall[0, 0] * 0.5)
        pieces.append(tall[0, quarter - 1] * 0.5)
        face = jnp.where(upper, high, roll(low, quarter, 0))
        pieces.append((face + roll(face, -1, 0)) * 0.5)
        wide_rows = jnp.concatenate(pieces, 0)
        nxt[...] = pooled(wide_rows, pool_matrix(columns, columns // 2)).reshape(nxt.shape)
        copy.wait()


def second_kernel(sweeps, extended, left, right, faces, middle, packed, nxt, *rest):
    mass, source, field, rest = rest[0:2], rest[2:4], rest[4:6], rest[6:]
    limit, wide, columns = extended.shape[1:]
    quarter = wide // 2
    row_of = iota((wide, columns), 0) % quarter
    top, bottom = row_of == 0, row_of == quarter - 1
    for t in range(limit):
        assemble_second(field, t, extended[0, t], left[0, t], right[0, t])
        assemble_second(mass, t, extended[2, t], left[2, t], right[2, t])
        one, two, face = left[1, t], right[1, t], faces[t]
        tile = extended[1, t] + jnp.where(top, one, 0.0) + jnp.where(bottom, two, 0.0)
        one = one + jnp.where(bottom, face, 0.0)
        two = two + jnp.where(top, face, 0.0)
        assemble_second(source, t, tile, one, two)
    source_from_defect(field, mass, source)
    second_finish(sweeps[0], field, mass, source, middle, packed, nxt, *rest)


def second_again_kernel(sweeps, extended, left, right, *rest):
    mass, source = rest[0:2], rest[2:4]
    middle, packed, nxt, *rest = rest[4:]
    field, rest = rest[:2], rest[2:]
    for t in range(extended.shape[0]):
        assemble_second(field, t, extended[t], left[t], right[t])
    second_finish(sweeps[0], field, mass, source, middle, packed, nxt, *rest)


def second_level(parts, edge_left, edge_right, count):
    tiles, wide, columns = parts.shape[1:]
    limit = tiles + 4
    x_left = shifted(edge_right, "group", 1)
    x_right = shifted(edge_left, "group", -1)
    three = (3, limit, wide, columns)
    extended, to_left, to_right, faces = call(
        second_prepare_kernel, [three, three, three, (limit, wide, columns)], [parts, x_left, x_right]
    )
    left = shifted(to_right, "brick", 1)
    right = shifted(to_left, "brick", -1)
    window = (limit, 2 * wide, columns)
    outs = [(2 * tiles, wide // 2, columns), (tiles, wide, columns), (9, tiles, columns // 2)]
    scratch = [window, window, (3, wide // 2, tiles, columns)]
    args = [count, extended, left, right, faces]
    middle, packed, nxt, *fixed = call(second_kernel, outs + [window] * 4, args, scratch, 1, 1)

    def again(given):
        packed = given[1]
        x_left = shifted(packed[-2:], "group", 1)
        x_right = shifted(packed[:2], "group", -1)
        extended = jnp.concatenate([x_left, packed, x_right], 0)
        left = shifted(extended, "brick", 1)
        right = shifted(extended, "brick", -1)
        return list(call(second_again_kernel, outs, [count - 2, extended, left, right, *fixed], scratch, 1, 1))

    done = lax.cond(count[0] > 2, again, lambda given: given, [middle, packed, nxt])
    return done[0], done[2]


def third_prepare_kernel(group, *refs):
    blocks, out = refs[:-1], refs[-1]
    count = len(blocks)
    rows, columns = blocks[0].shape[1:]
    row = iota((rows, columns), 0)
    for b in range(count):
        span = pl.ds(pl.multiple_of(((group[0] + b) % count) * rows, rows), rows)
        before, after = blocks[b - 1][8], blocks[(b + 1) % count][8]
        for at in range(8):
            value = blocks[b][at]
            if at in (2, 3):
                high = before[2 * (at - 2) : 2 * (at - 2) + 1]
                low = after[rows // 2 + 2 * (at - 2) : rows // 2 + 2 * (at - 2) + 1]
                value = value + jnp.where(row == 0, high, 0.0) + jnp.where(row == rows - 1, low, 0.0)
            out[at, span] = value


def third_chip_kernel(core, own, other, chip, face):
    edge = core[0]
    for at in range(3):
        values = [own[2 * at + edge], own[2 * at + 1 - edge], other[2 * at + edge], other[2 * at + 1 - edge]]
        if at == 1:
            values[1] = values[1] + other[6 + edge]
            values[2] = values[2] + own[7 - edge]
        for k in range(4):
            chip[4 * at + k] = values[k]
    chip[12] = own[6 + edge]
    face[0] = other[7 - edge]


def third_finish(sweeps, core, field, mass, source, coarse, packed, message, tall, held, sent):
    rows, columns = field[0].shape[1:]
    is_odd = odd((rows, columns), plus=core[0])
    count = sweeps[0]
    two_sweeps(count, field, mass, source, 6, core[0])
    red, black = field[0][2], field[1][2]
    one, two = jnp.where(is_odd, black, red), jnp.where(is_odd, red, black)
    for colour in range(2):
        for k in range(2):
            packed[2 * colour + k] = field[colour][2 + k]
    tall[:rows] = jnp.where(core[0] == 0, one, two)
    tall[rows : 2 * rows] = jnp.where(core[0] == 0, two, one)
    for r in range(rows):
        held[2 * r : 2 * r + 1] = tall[r : r + 1]
        held[2 * r + 1 : 2 * r + 2] = tall[rows + r : rows + r + 1]
    copy = pltpu.make_async_copy(held, coarse, sent)

    @pl.when(count <= 2)
    def _():
        copy.start()
        totals = []
        for q in (2, 3):
            total = jnp.zeros((rows, columns), jnp.float32)
            for colour in range(2):
                other = field[1 - colour]
                beyond = inner_only(is_odd, other[5 - q], q, colour)
                around = other[q] + beyond + both_ways(other[q], 0) + both_ways(other[q], 1)
                total = total + residual(around, field[colour][q], mass[colour][q], source[colour][q])
            totals.append(total * 0.5)
        red, black = field[0][3], field[1][3]
        last = jnp.where(is_odd, red, black)
        pieces = [(field[0][q] + field[1][q]) * 0.125 for q in (2, 3)] + totals
        pieces += [(mass[0][q] + mass[1][q]) * 0.5 for q in (2, 3)] + [one * 0.5, last * 0.5]
        tall[...] = pooled(jnp.concatenate(pieces, 0), pool_matrix(columns, columns))
        half = rows // 2
        narrow = tall[pl.ds(0, 8 * half, stride=2)] + tall[pl.ds(1, 8 * half, stride=2)]
        lane = iota((half, columns), 1) // (columns // 2)
        lower = lane == core[0]
        is_odd_half = odd((half, columns))
        even_row = same_row((half, columns))

        def narrow_of(k):
            return narrow[k * half : (k + 1) * half]

        tiles = []
        for at in range(3):
            tile = jnp.where(lower, narrow_of(2 * at), narrow_of(2 * at + 1))
            tiles.append(jnp.where(is_odd_half, roll(tile, columns // 2, 1), tile))
        low_face = jnp.where(core[0] == 0, narrow_of(6), narrow_of(7))
        high_face = jnp.where(core[0] == 0, narrow_of(7), narrow_of(6))
        tiles.append(jnp.where(even_row, high_face, low_face))
        for at in range(2):
            tile = jnp.where(core[0] == 0, tiles[at], tiles[2 + at])
            tile = jnp.where(core[1] == 0, tile, roll(tile, columns // 2, 1))
            for c in range(message.shape[0]):
                message[c, at] = tile
        copy.wait()


def same_row(shape):
    half = shape[1] // 2
    lane = iota(shape, 1)
    return ((iota(shape, 0) + lane + lane // half) & 1) == 0


def inner_only(is_odd, inner, q, colour):
    above = is_odd if colour == 0 else jnp.logical_not(is_odd)
    return jnp.where(above, inner, 0.0) if q == 2 else jnp.where(above, 0.0, inner)


def pack_pair(window, at, even, next_one, is_odd):
    window[0][at] = jnp.where(is_odd, next_one, even)
    window[1][at] = jnp.where(is_odd, even, next_one)


def third_kernel(sweeps, core, chip, face, near, far, coarse, packed, message, *rest):
    mass, source, field, rest = rest[0:2], rest[2:4], rest[4:6], rest[6:]
    rows, columns = chip.shape[1:]
    is_odd = odd((rows, columns), plus=core[0])
    for at, window in enumerate((field, source, mass)):
        side = [near[4 * at + k] for k in range(4)]
        own = [chip[4 * at + k] for k in range(4)]
        beyond = [far[4 * at + k] for k in range(4)]
        if at == 1:
            side[0] = side[0] + chip[12]
            own[0] = own[0] + near[12]
            own[3] = own[3] + far[12]
            beyond[0] = beyond[0] + face[0]
        line = side[::-1] + own + beyond
        for q in range(6):
            pack_pair(window, q, line[2 * q], line[2 * q + 1], is_odd)
    source_from_defect(field, mass, source, plus=core[0])
    third_finish(sweeps, core, field, mass, source, coarse, packed, message, *rest)


def third_again_kernel(sweeps, core, chip, near, far, *rest):
    mass, source = rest[0:2], rest[2:4]
    coarse, packed, message, *rest = rest[4:]
    field, rest = rest[:2], rest[2:]
    for colour in range(2):
        for k in range(2):
            field[colour][1 - k] = near[2 * colour + k]
            field[colour][2 + k] = chip[2 * colour + k]
            field[colour][4 + k] = far[2 * colour + k]
    third_finish(sweeps, core, field, mass, source, coarse, packed, message, *rest)


def third_level(part, count, core):
    groups, chips = lax.axis_size("group"), lax.axis_size("brick") // 2
    tile_rows, columns = part.shape[1:]
    rows = groups * tile_rows
    blocks = [part] + [shifted(part, "group", -d) for d in range(1, groups)]
    (own,) = call(third_prepare_kernel, [(8, rows, columns)], [place_of("group"), *blocks], (), 1)
    chip, face = call(
        third_chip_kernel, [(13, rows, columns), (1, rows, columns)], [core, own, swapped_cores(own)], (), 1
    )
    near = swapped_chips(chip)
    far = swapped_cores(near)
    window = (6, rows, columns)
    outs = [(2 * rows, columns), (4, rows, columns), (chips, 2, rows // 2, columns)]
    scratch = [window, window, (8 * rows, columns)]
    args = [count, core, chip, face, near, far]
    coarse, packed, message, *fixed = call(third_kernel, outs + [window] * 4, args, scratch, 2, 1)

    def again(given):
        packed = given[1]
        near = swapped_chips(packed)
        args = [count - 2, core, packed, near, swapped_cores(near), *fixed]
        return list(call(third_again_kernel, outs, args, scratch, 2, 1))

    done = lax.cond(count[0] > 2, again, lambda given: given, [coarse, packed, message])
    return done[0].reshape(rows, 2, columns), done[2]


def fourth_kernel(sweeps, core, own, other, out, *windows):
    field, mass, source, (held, sent) = windows[0:2], windows[2:4], windows[4:6], windows[6:]
    chips, _, rows, columns = own.shape
    tiles, half = chips // 2, columns // 2
    lane = iota((rows, columns), 1)
    low = lane < half
    is_odd = odd((rows, columns))
    first, last = lane % half == 0, lane % half == half - 1

    def turned(value):
        return roll(value, half, 1)

    def beside(value):
        after = jnp.where(last, roll(value, half - 1, 1), roll(value, -1, 1))
        return after + jnp.where(first, roll(value, 1 - half, 1), roll(value, 1, 1))

    def put(window, t, one, two):
        window[0][t + 1] = jnp.where(low, one, two)
        window[1][t + 1] = turned(jnp.where(low, two, one))

    def repeat(window, colour):
        window[colour][0] = turned(window[colour][tiles])
        window[colour][tiles + 1] = turned(window[colour][1])

    def load(one, two):
        even_row = same_row((rows, columns))

        def defect(t):
            before, after = two[(t - 1) % chips, 1], two[(t + 1) % chips, 1]
            before = turned(before) if t in (0, tiles) else before
            after = turned(after) if t in (tiles - 1, chips - 1) else after
            if t < tiles:
                return one[t, 1] + jnp.where(even_row, before, after)
            return one[t, 1] + jnp.where(even_row, after, before)

        for t in range(tiles):
            put(field, t, one[t, 0], one[t + tiles, 0])
            put(mass, t, two[t, 0], two[t + tiles, 0])
            put(source, t, defect(t), defect(t + tiles))

    @pl.when(core[0] == 0)
    def _():
        load(own, other)

    @pl.when(core[0] == 1)
    def _():
        load(other, own)

    for colour in range(2):
        repeat(field, colour)
    source_from_defect(field, mass, source, beside, range(1, tiles + 1))

    def one_sweep(step, carry):
        for colour in range(2):
            half_sweep(field, mass, source, colour, 1, tiles + 1, 8, beside)
            repeat(field, colour)
        return carry

    lax.fori_loop(0, sweeps[0], one_sweep, 0)
    for t in range(tiles):
        red, black = field[0][t + 1], field[1][t + 1]
        red_too, black_too = turned(red), turned(black)
        one = jnp.where(low, jnp.where(is_odd, black, red), jnp.where(is_odd, red_too, black_too))
        two = jnp.where(low, jnp.where(is_odd, black_too, red_too), jnp.where(is_odd, red, black))
        for at, value in ((t, one), (t + tiles, two)):
            held[:, at * columns : (at + 1) * columns] = value
    copy = pltpu.make_async_copy(held, out, sent)
    copy.start()
    copy.wait()


def fourth_level(message, count, core):
    chips, _, rows, columns = message.shape
    cores = [[2 * chip + c for chip in range(chips)] for c in range(2)]
    own = lax.all_to_all(message, "brick", 0, 0, axis_index_groups=cores)
    other = swapped_cores(own)
    scratch = [(chips // 2 + 2, rows, columns)] * 6
    (out,) = call(fourth_kernel, [(rows, chips * columns)], [count, core, own, other], scratch, 2, 1)
    return out


def on_device(initial_field, mass, source, sweeps):
    fine, parts, edge_left, edge_right = first_level(initial_field, mass, source, sweeps[0:1])
    middle, part = second_level(parts, edge_left, edge_right, sweeps[1:2])
    bricks = lax.axis_size("brick")
    place = lax.axis_index("brick")
    core = jnp.stack([place % 2, (place >= bricks // 2).astype(place.dtype)]).astype(jnp.int32)
    coarse, message = third_level(part, sweeps[2:3], core)
    coarsest = fourth_level(message, sweeps[3:4], core)
    return fine, middle, coarse, coarsest


def solution(mesh):
    return jax.shard_map(
        on_device,
        mesh=mesh,
        in_specs=(
            P("group", "brick", None),
            P("group", "brick", None),
            P("group", "brick", None),
            P(),
        ),
        out_specs=(
            P("group", "brick", None),
            P("group", "brick", None),
            P(None, "brick", None),
            P(),
        ),
        check_vma=False,
    )
```

```python
import functools

import jax
import jax.numpy as jnp
from jax import lax
from jax.experimental import pallas as pl
from jax.experimental.pallas import tpu as pltpu
from jax.sharding import PartitionSpec as P


INTERPRET = False
MIB = 1024 * 1024
LANES = 128


def call(kernel, out_shapes, args, scratch=(), results=0, limit=12 * MIB):
    spec = pl.BlockSpec(memory_space=pltpu.VMEM)
    return pl.pallas_call(
        kernel,
        out_shape=[
            (pltpu.HBM if at < results else pltpu.VMEM)(shape, jnp.float32) for at, shape in enumerate(out_shapes)
        ],
        in_specs=[spec] * len(args),
        out_specs=[pl.BlockSpec(memory_space=pltpu.HBM)] * results + [spec] * (len(out_shapes) - results),
        scratch_shapes=[pltpu.VMEM(shape, jnp.float32) for shape in [*scratch, *out_shapes[:results]]]
        + [pltpu.SemaphoreType.DMA] * results,
        compiler_params=pltpu.CompilerParams(vmem_limit_bytes=limit),
        interpret=INTERPRET,
    )(*args)


def iota(shape, axis):
    return lax.broadcasted_iota(jnp.int32, shape, axis)


def odd(shape, period=None, plus=0):
    rows = iota(shape, 0)
    if period is not None:
        rows = rows % period
    return ((rows + iota(shape, 1) + plus) & 1) == 1


def same_member(shape, quarter):
    rows = iota(shape, 0)
    return ((rows % quarter + rows // quarter + iota(shape, 1)) & 1) == 0


def roll(value, shift, axis):
    return pltpu.roll(value, shift % value.shape[axis], axis)


def both_ways(value, axis):
    return roll(value, 1, axis) + roll(value, -1, axis)


def newton(around, value, mass, source):
    curve = mass * (value * value)
    over = (around + source) + 2.0 * (curve * value)
    under = (6.0 + mass) + 3.0 * curve
    guess = pl.reciprocal(under, approx=True)
    guess = guess * (2.0 - under * guess)
    return over * guess


def residual(around, value, mass, source):
    return (around - 6.0 * value) - mass * (value * value * value + value) + source


def pooled(rows, pool):
    high = rows.astype(jnp.bfloat16)
    rest = rows - high.astype(jnp.float32)
    middle = rest.astype(jnp.bfloat16)
    low = (rest - middle.astype(jnp.float32)).astype(jnp.bfloat16)
    dot = functools.partial(jnp.dot, preferred_element_type=jnp.float32)
    return dot(high, pool) + (dot(middle, pool) + dot(low, pool))


def pool_matrix(width, columns):
    half = width // 2
    shape = (width, columns)
    return jnp.where(iota(shape, 0) // 2 == iota(shape, 1) % half, 1.0, 0.0).astype(jnp.bfloat16)


def half_sweep(field, mass, source, colour, low, high, most, beside=None, plus=0):
    mine, other = field[colour], field[1 - colour]
    limit, rows, columns = mine.shape
    is_odd = odd((rows, columns), plus=plus)
    beside = beside or (lambda value: both_ways(value, 1))
    together = max(k for k in range(1, most + 1) if (high - low) % k == 0)

    def step(turn, carry):
        start = low + turn * together
        near = [other[jnp.clip(start + k, 0, limit - 1)] for k in range(-1, together + 1)]
        fresh = []
        for k in range(together):
            first, second = (near[k], near[k + 2]) if colour == 0 else (near[k + 2], near[k])
            around = near[k + 1] + jnp.where(is_odd, second, first)
            around = around + both_ways(near[k + 1], 0) + beside(near[k + 1])
            fresh.append(newton(around, mine[start + k], mass[colour][start + k], source[colour][start + k]))
        for k in range(together):
            mine[start + k] = fresh[k]
        return carry

    turns = (high - low) // together
    if turns == 1:
        step(0, 0)
    else:
        lax.fori_loop(0, turns, step, 0)


def two_sweeps(count, field, mass, source, most, plus=0):
    limit = field[0].shape[0]
    half_sweep(field, mass, source, 0, 0, limit, most, plus=plus)
    half_sweep(field, mass, source, 1, 1, limit - 1, most, plus=plus)

    @pl.when(count >= 2)
    def _():
        half_sweep(field, mass, source, 0, 1, limit - 1, most, plus=plus)
        half_sweep(field, mass, source, 1, 2, limit - 2, most, plus=plus)


def source_from_defect(field, mass, source, beside=None, inner=None, plus=0):
    limit, rows, columns = field[0].shape
    is_odd = odd((rows, columns), plus=plus)
    beside = beside or (lambda value: both_ways(value, 1))
    for index in inner or range(limit):
        for colour in range(2):
            other = field[1 - colour]
            first, second = other[max(index - 1, 0)], other[min(index + 1, limit - 1)]
            if colour == 1:
                first, second = second, first
            around = other[index] + jnp.where(is_odd, second, first)
            around = around + both_ways(other[index], 0) + beside(other[index])
            source[colour][index] = source[colour][index] - residual(
                around, field[colour][index], mass[colour][index], 0.0
            )


def shifted(value, axis, by):
    count = lax.axis_size(axis)
    return lax.ppermute(value, axis, [(i, (i + by) % count) for i in range(count)])


def swapped_cores(value):
    count = lax.axis_size("brick")
    return lax.ppermute(value, "brick", [(i, i ^ 1) for i in range(count)])


def swapped_chips(value):
    count = lax.axis_size("brick")
    return lax.ppermute(value, "brick", [(i, (i + 1 if i % 2 else i - 1) % count) for i in range(count)])


def both_swapped(inner, outer):
    far = swapped_chips(outer)
    return far, swapped_cores(inner)


def sides(core, outer, inner):
    on_first = jnp.broadcast_to(core, outer.shape) == 0
    return jnp.where(on_first, outer, inner), jnp.where(on_first, inner, outer)


def my_core():
    return lax.axis_index("brick") & 1


def count_of(counts, level):
    return jnp.max(counts[level])


def kept_pairs(pairs):
    quarter = pairs // 4
    kept = list(range(quarter)) + list(range(pairs - quarter, pairs))
    return kept, list(range(quarter, pairs - quarter))


def ride_right(row, mass, source, rider):
    mass = jnp.where(row < 2, roll(rider, -2, 0), jnp.where(row == 4, roll(rider, -1, 0), mass))
    return mass, jnp.where(row < 2, roll(rider, 2, 0), source)


def ride_left(row, mass, source, rider):
    mass = jnp.where(row > 5, roll(rider, 2, 0), jnp.where(row == 3, roll(rider, 1, 0), mass))
    return mass, jnp.where(row > 5, roll(rider, -2, 0), source)


def rider_from_left(row, mass, source):
    return jnp.where(row < 4, roll(mass, 2, 0), jnp.where(row == 5, roll(mass, 1, 0), roll(source, -2, 0)))


def rider_from_right(row, mass, source):
    return jnp.where(row < 2, roll(source, 2, 0), jnp.where(row == 2, roll(mass, -1, 0), roll(mass, -2, 0)))


def pack_kernel(*refs):
    sweeps, *blocks = refs[:4]
    own, outer, inner, edge_left, edge_right, counts, held, arrived, few, few_arrived = refs[4:]
    count = len(blocks)
    core = my_core()
    pairs = own.shape[2]
    rows, columns = own.shape[3:]
    is_odd = odd((rows, columns))
    row = iota((rows, columns), 0)
    upper = row < rows // 2
    parts = arrived.shape[1]
    some = 2 * pairs // parts

    def part_of(at, part):
        span = pl.ds(some * part, some)
        return pltpu.make_async_copy(blocks[at].at[span], held.at[at, span], arrived.at[at, part])

    def packed(at, pair):
        even, next_one = held[at, 2 * pair], held[at, 2 * pair + 1]
        red = jnp.where(is_odd, next_one, even)
        black = jnp.where(is_odd, even, next_one)
        own[at, 0, pair] = red
        own[at, 1, pair] = black
        if pair < 2:
            edge_left[at, 0, pair] = red
            edge_left[at, 1, pair] = black
        if pair >= pairs - 2:
            edge_right[at, 0, pair - pairs + 2] = red
            edge_right[at, 1, pair - pairs + 2] = black
        turned = roll(black, rows // 2, 0)
        return jnp.where(upper, red, turned), jnp.where(upper, turned, red)

    for at in range(count):
        for part in range(parts):
            part_of(at, part).start()
    copy = pltpu.make_async_copy(sweeps, few, few_arrived)
    copy.start()
    copy.wait()
    for level in range(4):
        counts[level] = jnp.full(counts.shape[1:], few[level])
    for part in range(parts):
        part_of(0, part).wait()
        for pair in range(some // 2 * part, some // 2 * (part + 1)):
            outer[pair], inner[pair] = sides(core, *packed(0, pair))
    for at in (1, 2):
        for part in range(parts):
            part_of(at, part).wait()
    kept, riders = kept_pairs(pairs)
    half = pairs // 2
    for k, (pair, other) in enumerate(zip(kept, riders)):
        mass, source = packed(1, pair), packed(2, pair)
        other_mass, rider = packed(1, other), packed(2, other)
        left = ride_left(row, mass[0], source[0], rider[0])
        right = ride_right(row, mass[1], source[1], rider[1])
        places = (pairs + k, pairs + half + k, 2 * pairs + k)
        for place, one, two in zip(places, (*left, other_mass[0]), (*right, other_mass[1])):
            outer[place], inner[place] = sides(core, one, two)


def corner_kernel(y_outer, y_inner, to_left, to_right):
    core = my_core()
    tiles, rows, columns = y_outer.shape
    pairs = tiles if to_left.shape[0] == 3 else tiles * 2 // 5
    from_right = iota((rows, columns), 0) % (rows // 2) < rows // 4
    for out, near, far, kept in ((to_left, 0, 1, 0), (to_right, pairs - 1, pairs - 2, pairs // 2 - 1)):
        out[0], out[1] = sides(core, y_outer[near], y_inner[near])
        both = [far] if out.shape[0] == 3 else [far, pairs + kept, pairs + pairs // 2 + kept]
        for k, at in enumerate(both):
            left, right = sides(core, y_outer[at], y_inner[at])
            out[2 + k] = jnp.where(from_right, right, left)


def pack_shapes(count, pairs, tile):
    shapes = [(count, 2, pairs, *tile)] + [(pairs if count == 1 else pairs * 5 // 2, *tile)] * 2
    return shapes + [(count, 2, 2, *tile)] * 2


def packed_blocks(sweeps, blocks):
    count = len(blocks)
    rows, *tile = blocks[0].shape
    shapes = pack_shapes(count, rows // 2, tile)
    return pl.pallas_call(
        pack_kernel,
        out_shape=[pltpu.VMEM(shape, jnp.float32) for shape in shapes] + [pltpu.VMEM((4, 8, LANES), jnp.int32)],
        in_specs=[pl.BlockSpec(memory_space=pltpu.HBM)] * (1 + count),
        out_specs=[pl.BlockSpec(memory_space=pltpu.VMEM)] * (len(shapes) + 1),
        scratch_shapes=[
            pltpu.VMEM((count, rows, *tile), jnp.float32),
            pltpu.SemaphoreType.DMA((count, 4)),
            pltpu.SMEM((4,), jnp.int32),
            pltpu.SemaphoreType.DMA,
        ],
        compiler_params=pltpu.CompilerParams(vmem_limit_bytes=12 * MIB),
    )(*[pltpu.with_memory_space_constraint(value, pltpu.HBM) for value in (sweeps, *blocks)])


def first_exchange(own, outer, inner, edge_left, edge_right):
    count, tile = own.shape[0], own.shape[3:]
    y_outer, y_inner = both_swapped(inner, outer)
    x_left = shifted(edge_right, "group", 1)
    x_right = shifted(edge_left, "group", -1)
    corners = call(corner_kernel, [(3 if count == 1 else 5, *tile)] * 2, [y_outer, y_inner])
    c_left = shifted(corners[1], "group", 1)
    c_right = shifted(corners[0], "group", -1)
    return own, x_left, x_right, y_outer, y_inner, c_left, c_right


def assemble_first(window, at, own, x_left, x_right, y_outer, y_inner, c_left, c_right):
    pairs, wide, columns = own.shape[2:]
    row = iota((wide, columns), 0)
    upper = row < wide // 2
    kept, riders = kept_pairs(pairs)
    core = my_core()

    def put(to, red, black, from_left, from_right):
        window[0][to, :wide] = red
        window[0][to, wide:] = jnp.where(upper, from_right, from_left)
        window[1][to, :wide] = black
        window[1][to, wide:] = roll(jnp.where(upper, from_left, from_right), wide // 2, 0)

    def beside(place):
        return sides(core, y_outer[place], y_inner[place])

    for pair in range(pairs):
        if at == 0:
            left, right = beside(pair)
        elif pair in kept:
            left, right = beside(pairs + (at - 1) * (pairs // 2) + kept.index(pair))
        elif at == 1:
            left, right = beside(2 * pairs + riders.index(pair))
        else:
            (left, right), other = beside(pairs + riders.index(pair)), beside(pairs + pairs // 2 + riders.index(pair))
            left, right = rider_from_left(row, left, other[0]), rider_from_right(row, right, other[1])
        put(pair + 2, own[at, 0, pair], own[at, 1, pair], left, right)
    for k in range(2):
        for to, near, x_side, corner in ((k, k == 1, x_left, c_left), (pairs + 2 + k, k == 0, x_right, c_right)):
            if at == 0:
                left, right = (corner[0], corner[1]) if near else (corner[2], corner[2])
            else:
                left = right = corner[2 + at]
            put(to, x_side[at, 0, k], x_side[at, 1, k], left, right)


def first_kernel(counts, *refs):
    halo, refs = refs[:7], refs[7:]
    fine, nxt, edge_left, edge_right, *refs = refs
    again, windows, field, rest = refs[:5], refs[5:9], refs[9:11], refs[11:]
    mass, source = windows[:2], windows[2:]
    for at, window in enumerate((field, mass, source)):
        assemble_first(window, at, *halo)
    first_finish(count_of(counts, 0), field, mass, source, (fine, nxt, edge_left, edge_right), again, *rest)


def first_again_kernel(counts, *refs):
    halo, mass, source, outs, field, rest = refs[:7], refs[7:9], refs[9:11], refs[11:15], refs[15:17], refs[17:]
    assemble_first(field, 0, *halo)
    first_finish(count_of(counts, 0) - 2, field, mass, source, outs, None, *rest)


def first_finish(count, field, mass, source, outs, again, tall, held, sent):
    fine, nxt, edge_left, edge_right = outs
    limit, rows, columns = field[0].shape
    pairs, wide = limit - 4, rows // 2
    two_sweeps(count, field, mass, source, 4)
    is_odd = odd((wide, columns))
    row = iota((wide, columns), 0)
    top, bottom = row == 0, row == wide - 1
    copy = pltpu.make_async_copy(held, fine, sent)

    if again is not None:

        @pl.when(count > 2)
        def _():
            own, outer, inner, *edges = again
            upper = row < wide // 2
            for pair in range(pairs):
                red, black = field[0][pair + 2, :wide], field[1][pair + 2, :wide]
                own[0, 0, pair] = red
                own[0, 1, pair] = black
                turned = roll(black, wide // 2, 0)
                outer[pair], inner[pair] = sides(
                    my_core(), jnp.where(upper, red, turned), jnp.where(upper, turned, red)
                )
                for edge, first in zip(edges, (0, pairs - 2)):
                    if first <= pair < first + 2:
                        edge[0, 0, pair - first] = red
                        edge[0, 1, pair - first] = black

    def keep(index, value):
        for c in range(columns // LANES):
            tall[c, index] = value[:, c * LANES : (c + 1) * LANES]

    @pl.when(count <= 2)
    def _():
        for pair in range(pairs):
            red, black = field[0][pair + 2, :wide], field[1][pair + 2, :wide]
            held[2 * pair] = jnp.where(is_odd, black, red)
            held[2 * pair + 1] = jnp.where(is_odd, red, black)
        copy.start()

        def step(pair, carry):
            total = jnp.zeros((wide, columns), jnp.float32)
            for colour in range(2):
                other = field[1 - colour][pair + 2, :wide]
                first = jnp.where(pair == 0, 0.0, field[1 - colour][pair + 1, :wide])
                second = jnp.where(pair == pairs - 1, 0.0, field[1 - colour][pair + 3, :wide])
                if colour == 1:
                    first, second = second, first
                around = other + jnp.where(is_odd, second, first) + both_ways(other, 1)
                around = around + jnp.where(bottom, 0.0, roll(other, -1, 0))
                around = around + jnp.where(top, 0.0, roll(other, 1, 0))
                at = (pair + 2, slice(0, wide))
                total = total + residual(around, field[colour][at], mass[colour][at], source[colour][at])
            keep(pair, field[0][at] + field[1][at])
            keep(pairs + pair, total)
            keep(2 * pairs + pair, mass[0][at] + mass[1][at])
            return carry

        lax.fori_loop(0, pairs, step, 0, unroll=2)
        low = jnp.where(is_odd, field[1][2, :wide], field[0][2, :wide])
        high = jnp.where(is_odd, field[0][pairs + 1, :wide], field[1][pairs + 1, :wide])
        half, tiles, quarter = columns // 2, pairs // 2, wide // 2
        keep(3 * pairs, high)
        keep(3 * pairs + 1, low)
        lines = (3 * pairs + 2) * wide // 2
        flat = tall.reshape(columns // LANES, 2 * lines, LANES)

        def every_other(start):
            parts = [flat[c, pl.ds(start, lines, stride=2)] for c in range(columns // LANES)]
            return jnp.concatenate(parts, 1)

        firsts, seconds = every_other(0), every_other(1)
        whole = (iota((wide, columns), 0)) % quarter
        y_faces = []
        for t in range(tiles):
            last, head = seconds[t * wide : (t + 1) * wide], firsts[t * wide : (t + 1) * wide]
            y_faces.append(
                jnp.where(
                    whole == 0,
                    roll(last, quarter + 1, 0),
                    jnp.where(whole == quarter - 1, roll(head, quarter - 1, 0), 0.0),
                )
            )
        narrow = pooled(jnp.concatenate([firsts + seconds] + y_faces, 0), pool_matrix(columns, half))
        is_odd_half = odd((wide, half), quarter)
        is_even = same_member((wide, half), quarter)

        def packed(index, factor):
            tile = narrow[index * wide : (index + 1) * wide] * factor
            return jnp.where(is_odd_half, roll(tile, quarter, 0), tile)

        face_x = packed(3 * tiles, 0.5)
        for t in range(tiles):
            values = [
                packed(t, 0.125),
                packed(tiles + t, 0.5),
                packed(2 * tiles + t, 0.5),
                packed(3 * tiles + 1 + t, 0.5),
            ]
            for at, value in enumerate(values):
                nxt[at, t] = value
                if t < 2:
                    if at == 1 and t == 1:
                        value = jnp.where(is_even, value, face_x)
                    edge_left[at, t] = value
                if t >= tiles - 2:
                    if at == 1 and t == tiles - 2:
                        value = jnp.where(is_even, face_x, value)
                    edge_right[at, t - tiles + 2] = value
        nxt[4, 0] = face_x
        for t in range(1, tiles):
            nxt[4, t] = jnp.zeros((wide, half), jnp.float32)
        copy.wait()


def first_level(field, mass, source, sweeps):
    rows, wide, columns = field.shape
    pairs = rows // 2
    half, tiles = columns // 2, pairs // 2
    window = (pairs + 4, 2 * wide, columns)
    outs = [
        (rows, wide, columns),
        (5, tiles, wide, half),
        (4, 2, wide, half),
        (4, 2, wide, half),
    ]

    tall = (columns // LANES, 3 * pairs + 2, wide, LANES)
    *packed, counts = packed_blocks(sweeps, [field, mass, source])
    halo = first_exchange(*packed)
    every = outs + pack_shapes(1, pairs, (wide, columns)) + [window] * 4
    results = call(first_kernel, every, [counts, *halo], [window, window, tall], 1, 24 * MIB)
    once, more, fixed = results[:4], results[4:9], results[9:]

    def again(given):
        args = [counts, *first_exchange(*more), *fixed]
        return list(call(first_again_kernel, outs, args, [window, window, tall], 1, 24 * MIB))

    return counts, lax.cond(sweeps[0] > 2, again, lambda given: given, list(once))


def second_prepare_kernel(own, x_left, x_right, extended, outer, inner, faces):
    tiles, wide, columns = own.shape[1:]
    quarter = wide // 2
    row_of = iota((wide, columns), 0) % quarter
    is_even = same_member((wide, columns), quarter)
    face_x = own[4, 0]
    for t in range(tiles + 4):
        if t < 2:
            source, k = x_left, t
        elif t < tiles + 2:
            source, k = own, t - 2
        else:
            source, k = x_right, t - tiles - 2
        defect = source[1, k]
        if t == 1:
            defect = defect + jnp.where(is_even, 0.0, face_x)
        if t == 2:
            defect = defect + jnp.where(is_even, x_left[1, 0], 0.0)
        if t == tiles + 1:
            defect = defect + jnp.where(is_even, 0.0, x_right[1, 1])
        if t == tiles + 2:
            defect = defect + jnp.where(is_even, face_x, 0.0)
        face_y = source[3, k]
        faces[t] = face_y
        for at in range(3):
            value = defect if at == 1 else source[at, k]
            extended[at, t] = value
            left = jnp.where(row_of == quarter - 1, face_y, value) if at == 1 else value
            right = jnp.where(row_of == 0, face_y, value) if at == 1 else value
            outer[at, t], inner[at, t] = sides(my_core(), left, right)


def assemble_second(window, to, tile, left, right):
    wide = tile.shape[0]
    quarter = wide // 2
    upper = iota(tile.shape, 0) < quarter
    window[0][to, :wide] = jnp.where(upper, tile, roll(right, quarter, 0))
    window[0][to, wide:] = roll(left, quarter, 0)
    window[1][to, :wide] = jnp.where(upper, roll(tile, quarter, 0), right)
    window[1][to, wide:] = left


def second_finish(count, field, mass, source, middle, packed, nxt, tall, held, sent):
    limit, rows, columns = field[0].shape
    pairs = limit - 4
    wide = rows // 2
    quarter = wide // 2
    two_sweeps(count, field, mass, source, 4)
    is_odd = odd((wide, columns), quarter)
    row = iota((wide, columns), 0)
    upper = row < quarter
    top, bottom = row == 0, row == quarter - 1
    for pair in range(pairs):
        red, black = field[0][pair + 2, :wide], field[1][pair + 2, :wide]
        tile = jnp.where(upper, red, roll(black, quarter, 0))
        packed[pair] = tile
        plain = jnp.where(is_odd, roll(tile, quarter, 0), tile)
        held[2 * pair] = plain[:quarter]
        held[2 * pair + 1] = plain[quarter:]
    copy = pltpu.make_async_copy(held, middle, sent)

    @pl.when(count <= 2)
    def _():
        copy.start()
        for pair in range(pairs):
            total = jnp.zeros((wide, columns), jnp.float32)
            for colour in range(2):
                other = field[1 - colour][pair + 2, :wide]
                around = other + both_ways(other, 1)
                around = around + jnp.where(bottom, 0.0, roll(other, -1, 0))
                around = around + jnp.where(top, 0.0, roll(other, 1, 0))
                first = field[1 - colour][pair + 1, :wide] if pair else 0.0
                second = field[1 - colour][pair + 3, :wide] if pair < pairs - 1 else 0.0
                if colour == 1:
                    first, second = second, first
                around = around + jnp.where(is_odd, second, first)
                at = (pair + 2, slice(0, wide))
                total = total + residual(around, field[colour][at], mass[colour][at], source[colour][at])
            values = [field[0][at] + field[1][at], total, mass[0][at] + mass[1][at]]
            for at, value in enumerate(values):
                for r in range(quarter):
                    tall[at, r, pair : pair + 1] = value[r : r + 1]
        low = jnp.where(is_odd, field[1][2, :wide], field[0][2, :wide])
        high = jnp.where(is_odd, field[0][pairs + 1, :wide], field[1][pairs + 1, :wide])
        pieces = []
        for at in range(3):
            for r in range(0, quarter, 2):
                pieces.append((tall[at, r] + tall[at, r + 1]) * (0.125 if at == 0 else 0.5))
        pieces.append(tall[0, 0] * 0.5)
        pieces.append(tall[0, quarter - 1] * 0.5)
        face = jnp.where(upper, high, roll(low, quarter, 0))
        pieces.append((face + roll(face, -1, 0)) * 0.5)
        wide_rows = jnp.concatenate(pieces, 0)
        nxt[...] = pooled(wide_rows, pool_matrix(columns, columns // 2)).reshape(nxt.shape)
        copy.wait()


def second_kernel(counts, extended, outer, inner, faces, middle, packed, nxt, *rest):
    mass, source, field, rest = rest[0:2], rest[2:4], rest[4:6], rest[6:]
    limit, wide, columns = extended.shape[1:]
    quarter = wide // 2
    row_of = iota((wide, columns), 0) % quarter
    top, bottom = row_of == 0, row_of == quarter - 1
    core = my_core()
    for t in range(limit):
        assemble_second(field, t, extended[0, t], *sides(core, outer[0, t], inner[0, t]))
        assemble_second(mass, t, extended[2, t], *sides(core, outer[2, t], inner[2, t]))
        (one, two), face = sides(core, outer[1, t], inner[1, t]), faces[t]
        tile = extended[1, t] + jnp.where(top, one, 0.0) + jnp.where(bottom, two, 0.0)
        one = one + jnp.where(bottom, face, 0.0)
        two = two + jnp.where(top, face, 0.0)
        assemble_second(source, t, tile, one, two)
    source_from_defect(field, mass, source)
    second_finish(count_of(counts, 1), field, mass, source, middle, packed, nxt, *rest)


def second_again_kernel(counts, extended, outer, inner, *rest):
    mass, source = rest[0:2], rest[2:4]
    middle, packed, nxt, *rest = rest[4:]
    field, rest = rest[:2], rest[2:]
    core = my_core()
    for t in range(extended.shape[0]):
        assemble_second(field, t, extended[t], *sides(core, outer[t], inner[t]))
    second_finish(count_of(counts, 1) - 2, field, mass, source, middle, packed, nxt, *rest)


def second_level(parts, edge_left, edge_right, count, counts):
    tiles, wide, columns = parts.shape[1:]
    limit = tiles + 4
    x_left = shifted(edge_right, "group", 1)
    x_right = shifted(edge_left, "group", -1)
    three = (3, limit, wide, columns)
    shapes = [three, three, three, (limit, wide, columns)]
    extended, outer, inner, faces = call(second_prepare_kernel, shapes, [parts, x_left, x_right])
    window = (limit, 2 * wide, columns)
    outs = [(2 * tiles, wide // 2, columns), (tiles, wide, columns), (9, tiles, columns // 2)]
    scratch = [window, window, (3, wide // 2, tiles, columns)]
    args = [counts, extended, *both_swapped(inner, outer), faces]
    middle, packed, nxt, *fixed = call(second_kernel, outs + [window] * 4, args, scratch, 1)

    def again(given):
        packed = given[1]
        x_left = shifted(packed[-2:], "group", 1)
        x_right = shifted(packed[:2], "group", -1)
        extended = jnp.concatenate([x_left, packed, x_right], 0)
        args = [counts, extended, *both_swapped(extended, extended), *fixed]
        return list(call(second_again_kernel, outs, args, scratch, 1))

    done = lax.cond(count > 2, again, lambda given: given, [middle, packed, nxt])
    return done[0], done[2]


def third_prepare_kernel(*refs):
    blocks, out = refs[:-1], refs[-1]
    count = len(blocks)
    rows, columns = blocks[0].shape[1:]
    row = iota((rows, columns), 0)
    for b in range(count):
        span = pl.ds(pl.multiple_of(((lax.axis_index("group") + b) % count) * rows, rows), rows)
        before, after = blocks[b - 1][8], blocks[(b + 1) % count][8]
        for at in range(8):
            value = blocks[b][at]
            if at in (2, 3):
                high = before[2 * (at - 2) : 2 * (at - 2) + 1]
                low = after[rows // 2 + 2 * (at - 2) : rows // 2 + 2 * (at - 2) + 1]
                value = value + jnp.where(row == 0, high, 0.0) + jnp.where(row == rows - 1, low, 0.0)
            out[at, span] = value


def third_chip_kernel(own, other, chip, face):
    edge = my_core()
    for at in range(3):
        values = [own[2 * at + edge], own[2 * at + 1 - edge], other[2 * at + edge], other[2 * at + 1 - edge]]
        if at == 1:
            values[1] = values[1] + other[6 + edge]
            values[2] = values[2] + own[7 - edge]
        for k in range(4):
            chip[4 * at + k] = values[k]
    chip[12] = own[6 + edge]
    face[0] = other[7 - edge]


def third_finish(count, field, mass, source, coarse, packed, message, tall, held, sent):
    rows, columns = field[0].shape[1:]
    core = my_core()
    is_odd = odd((rows, columns), plus=core)
    two_sweeps(count, field, mass, source, 6, core)
    red, black = field[0][2], field[1][2]
    one, two = jnp.where(is_odd, black, red), jnp.where(is_odd, red, black)
    for colour in range(2):
        for k in range(2):
            packed[2 * colour + k] = field[colour][2 + k]
    tall[:rows] = jnp.where(core == 0, one, two)
    tall[rows : 2 * rows] = jnp.where(core == 0, two, one)
    for r in range(rows):
        held[2 * r : 2 * r + 1] = tall[r : r + 1]
        held[2 * r + 1 : 2 * r + 2] = tall[rows + r : rows + r + 1]
    copy = pltpu.make_async_copy(held, coarse, sent)

    @pl.when(count <= 2)
    def _():
        copy.start()
        totals = []
        for q in (2, 3):
            total = jnp.zeros((rows, columns), jnp.float32)
            for colour in range(2):
                other = field[1 - colour]
                beyond = inner_only(is_odd, other[5 - q], q, colour)
                around = other[q] + beyond + both_ways(other[q], 0) + both_ways(other[q], 1)
                total = total + residual(around, field[colour][q], mass[colour][q], source[colour][q])
            totals.append(total * 0.5)
        red, black = field[0][3], field[1][3]
        last = jnp.where(is_odd, red, black)
        pieces = [(field[0][q] + field[1][q]) * 0.125 for q in (2, 3)] + totals
        pieces += [(mass[0][q] + mass[1][q]) * 0.5 for q in (2, 3)] + [one * 0.5, last * 0.5]
        tall[...] = pooled(jnp.concatenate(pieces, 0), pool_matrix(columns, columns))
        half = rows // 2
        narrow = tall[pl.ds(0, 8 * half, stride=2)] + tall[pl.ds(1, 8 * half, stride=2)]
        lane = iota((half, columns), 1) // (columns // 2)
        lower = lane == core
        is_odd_half = odd((half, columns))
        even_row = same_row((half, columns))

        def narrow_of(k):
            return narrow[k * half : (k + 1) * half]

        tiles = []
        for at in range(3):
            tile = jnp.where(lower, narrow_of(2 * at), narrow_of(2 * at + 1))
            tiles.append(jnp.where(is_odd_half, roll(tile, columns // 2, 1), tile))
        low_face = jnp.where(core == 0, narrow_of(6), narrow_of(7))
        high_face = jnp.where(core == 0, narrow_of(7), narrow_of(6))
        tiles.append(jnp.where(even_row, high_face, low_face))
        for at in range(2):
            tile = jnp.where(core == 0, tiles[at], tiles[2 + at])
            tile = jnp.where(lax.axis_index("brick") < message.shape[0], tile, roll(tile, columns // 2, 1))
            for c in range(message.shape[0]):
                message[c, at] = tile
        copy.wait()


def same_row(shape):
    half = shape[1] // 2
    lane = iota(shape, 1)
    return ((iota(shape, 0) + lane + lane // half) & 1) == 0


def inner_only(is_odd, inner, q, colour):
    above = is_odd if colour == 0 else jnp.logical_not(is_odd)
    return jnp.where(above, inner, 0.0) if q == 2 else jnp.where(above, 0.0, inner)


def pack_pair(window, at, even, next_one, is_odd):
    window[0][at] = jnp.where(is_odd, next_one, even)
    window[1][at] = jnp.where(is_odd, even, next_one)


def third_kernel(counts, chip, face, near, far, coarse, packed, message, *rest):
    mass, source, field, rest = rest[0:2], rest[2:4], rest[4:6], rest[6:]
    rows, columns = chip.shape[1:]
    is_odd = odd((rows, columns), plus=my_core())
    for at, window in enumerate((field, source, mass)):
        side = [near[4 * at + k] for k in range(4)]
        own = [chip[4 * at + k] for k in range(4)]
        beyond = [far[4 * at + k] for k in range(4)]
        if at == 1:
            side[0] = side[0] + chip[12]
            own[0] = own[0] + near[12]
            own[3] = own[3] + far[12]
            beyond[0] = beyond[0] + face[0]
        line = side[::-1] + own + beyond
        for q in range(6):
            pack_pair(window, q, line[2 * q], line[2 * q + 1], is_odd)
    source_from_defect(field, mass, source, plus=my_core())
    third_finish(count_of(counts, 2), field, mass, source, coarse, packed, message, *rest)


def third_again_kernel(counts, chip, near, far, *rest):
    mass, source = rest[0:2], rest[2:4]
    coarse, packed, message, *rest = rest[4:]
    field, rest = rest[:2], rest[2:]
    for colour in range(2):
        for k in range(2):
            field[colour][1 - k] = near[2 * colour + k]
            field[colour][2 + k] = chip[2 * colour + k]
            field[colour][4 + k] = far[2 * colour + k]
    third_finish(count_of(counts, 2) - 2, field, mass, source, coarse, packed, message, *rest)


def third_level(part, count, counts):
    groups, chips = lax.axis_size("group"), lax.axis_size("brick") // 2
    tile_rows, columns = part.shape[1:]
    rows = groups * tile_rows
    blocks = [part] + [shifted(part, "group", -d) for d in range(1, groups)]
    (own,) = call(third_prepare_kernel, [(8, rows, columns)], blocks)
    chip, face = call(
        third_chip_kernel, [(13, rows, columns), (1, rows, columns)], [own, swapped_cores(own)]
    )
    near = swapped_chips(chip)
    far = swapped_cores(near)
    window = (6, rows, columns)
    outs = [(2 * rows, columns), (4, rows, columns), (chips, 2, rows // 2, columns)]
    scratch = [window, window, (8 * rows, columns)]
    args = [counts, chip, face, near, far]
    coarse, packed, message, *fixed = call(third_kernel, outs + [window] * 4, args, scratch, 1)

    def again(given):
        packed = given[1]
        near = swapped_chips(packed)
        args = [counts, packed, near, swapped_cores(near), *fixed]
        return list(call(third_again_kernel, outs, args, scratch, 1))

    done = lax.cond(count > 2, again, lambda given: given, [coarse, packed, message])
    return done[0].reshape(rows, 2, columns), done[2]


def fourth_kernel(counts, own, other, out, *windows):
    field, mass, source, (held, sent) = windows[0:2], windows[2:4], windows[4:6], windows[6:]
    chips, _, rows, columns = own.shape
    tiles, half = chips // 2, columns // 2
    lane = iota((rows, columns), 1)
    low = lane < half
    is_odd = odd((rows, columns))
    first, last = lane % half == 0, lane % half == half - 1

    def turned(value):
        return roll(value, half, 1)

    def beside(value):
        after = jnp.where(last, roll(value, half - 1, 1), roll(value, -1, 1))
        return after + jnp.where(first, roll(value, 1 - half, 1), roll(value, 1, 1))

    def put(window, t, one, two):
        window[0][t + 1] = jnp.where(low, one, two)
        window[1][t + 1] = turned(jnp.where(low, two, one))

    def repeat(window, colour):
        window[colour][0] = turned(window[colour][tiles])
        window[colour][tiles + 1] = turned(window[colour][1])

    def load(one, two):
        even_row = same_row((rows, columns))

        def defect(t):
            before, after = two[(t - 1) % chips, 1], two[(t + 1) % chips, 1]
            before = turned(before) if t in (0, tiles) else before
            after = turned(after) if t in (tiles - 1, chips - 1) else after
            if t < tiles:
                return one[t, 1] + jnp.where(even_row, before, after)
            return one[t, 1] + jnp.where(even_row, after, before)

        for t in range(tiles):
            put(field, t, one[t, 0], one[t + tiles, 0])
            put(mass, t, two[t, 0], two[t + tiles, 0])
            put(source, t, defect(t), defect(t + tiles))

    @pl.when(my_core() == 0)
    def _():
        load(own, other)

    @pl.when(my_core() == 1)
    def _():
        load(other, own)

    for colour in range(2):
        repeat(field, colour)
    source_from_defect(field, mass, source, beside, range(1, tiles + 1))

    def one_sweep(step, carry):
        for colour in range(2):
            half_sweep(field, mass, source, colour, 1, tiles + 1, 8, beside)
            repeat(field, colour)
        return carry

    lax.fori_loop(0, count_of(counts, 3), one_sweep, 0)
    for t in range(tiles):
        red, black = field[0][t + 1], field[1][t + 1]
        red_too, black_too = turned(red), turned(black)
        one = jnp.where(low, jnp.where(is_odd, black, red), jnp.where(is_odd, red_too, black_too))
        two = jnp.where(low, jnp.where(is_odd, black_too, red_too), jnp.where(is_odd, red, black))
        for at, value in ((t, one), (t + tiles, two)):
            held[:, at * columns : (at + 1) * columns] = value
    copy = pltpu.make_async_copy(held, out, sent)
    copy.start()
    copy.wait()


def fourth_level(message, counts):
    chips, _, rows, columns = message.shape
    cores = [[2 * chip + c for chip in range(chips)] for c in range(2)]
    own = lax.all_to_all(message, "brick", 0, 0, axis_index_groups=cores)
    other = swapped_cores(own)
    scratch = [(chips // 2 + 2, rows, columns)] * 6
    (out,) = call(fourth_kernel, [(rows, chips * columns)], [counts, own, other], scratch, 1)
    return out


def on_device(initial_field, mass, source, sweeps):
    counts, (fine, parts, edge_left, edge_right) = first_level(initial_field, mass, source, sweeps)
    middle, part = second_level(parts, edge_left, edge_right, sweeps[1], counts)
    coarse, message = third_level(part, sweeps[2], counts)
    coarsest = fourth_level(message, counts)
    return fine, middle, coarse, coarsest


def solution(mesh):
    return jax.shard_map(
        on_device,
        mesh=mesh,
        in_specs=(
            P("group", "brick", None),
            P("group", "brick", None),
            P("group", "brick", None),
            P(),
        ),
        out_specs=(
            P("group", "brick", None),
            P("group", "brick", None),
            P(None, "brick", None),
            P(),
        ),
        check_vma=False,
    )
```

```python
import functools

import jax
import jax.numpy as jnp
from jax import lax
from jax.experimental import pallas as pl
from jax.experimental.pallas import tpu as pltpu
from jax.sharding import PartitionSpec as P


INTERPRET = False
MIB = 1024 * 1024
LANES = 128


def call(kernel, out_shapes, args, scratch=(), results=0, limit=12 * MIB):
    spec = pl.BlockSpec(memory_space=pltpu.VMEM)
    return pl.pallas_call(
        kernel,
        out_shape=[
            (pltpu.HBM if at < results else pltpu.VMEM)(shape, jnp.float32) for at, shape in enumerate(out_shapes)
        ],
        in_specs=[spec] * len(args),
        out_specs=[pl.BlockSpec(memory_space=pltpu.HBM)] * results + [spec] * (len(out_shapes) - results),
        scratch_shapes=[pltpu.VMEM(shape, jnp.float32) for shape in [*scratch, *out_shapes[:results]]]
        + [pltpu.SemaphoreType.DMA] * results,
        compiler_params=pltpu.CompilerParams(vmem_limit_bytes=limit),
        interpret=INTERPRET,
    )(*args)


def iota(shape, axis):
    return lax.broadcasted_iota(jnp.int32, shape, axis)


def odd(shape, period=None, plus=0):
    rows = iota(shape, 0)
    if period is not None:
        rows = rows % period
    return ((rows + iota(shape, 1) + plus) & 1) == 1


def same_member(shape, quarter):
    rows = iota(shape, 0)
    return ((rows % quarter + rows // quarter + iota(shape, 1)) & 1) == 0


def roll(value, shift, axis):
    return pltpu.roll(value, shift % value.shape[axis], axis)


def both_ways(value, axis):
    return roll(value, 1, axis) + roll(value, -1, axis)


def newton(around, value, mass, source):
    curve = mass * (value * value)
    over = (around + source) + 2.0 * (curve * value)
    under = (6.0 + mass) + 3.0 * curve
    guess = pl.reciprocal(under, approx=True)
    guess = guess * (2.0 - under * guess)
    return over * guess


def residual(around, value, mass, source):
    return (around - 6.0 * value) - mass * (value * value * value + value) + source


def pooled(rows, pool):
    high = rows.astype(jnp.bfloat16)
    rest = rows - high.astype(jnp.float32)
    middle = rest.astype(jnp.bfloat16)
    low = (rest - middle.astype(jnp.float32)).astype(jnp.bfloat16)
    dot = functools.partial(jnp.dot, preferred_element_type=jnp.float32)
    return dot(high, pool) + (dot(middle, pool) + dot(low, pool))


def pool_matrix(width, columns):
    half = width // 2
    shape = (width, columns)
    return jnp.where(iota(shape, 0) // 2 == iota(shape, 1) % half, 1.0, 0.0).astype(jnp.bfloat16)


def half_sweep(field, mass, source, colour, low, high, most, beside=None, plus=0):
    mine, other = field[colour], field[1 - colour]
    limit, rows, columns = mine.shape
    is_odd = odd((rows, columns), plus=plus)
    beside = beside or (lambda value: both_ways(value, 1))
    together = max(k for k in range(1, most + 1) if (high - low) % k == 0)

    def step(turn, carry):
        start = low + turn * together
        near = [other[jnp.clip(start + k, 0, limit - 1)] for k in range(-1, together + 1)]
        fresh = []
        for k in range(together):
            first, second = (near[k], near[k + 2]) if colour == 0 else (near[k + 2], near[k])
            around = near[k + 1] + jnp.where(is_odd, second, first)
            around = around + both_ways(near[k + 1], 0) + beside(near[k + 1])
            fresh.append(newton(around, mine[start + k], mass[colour][start + k], source[colour][start + k]))
        for k in range(together):
            mine[start + k] = fresh[k]
        return carry

    turns = (high - low) // together
    if turns == 1:
        step(0, 0)
    else:
        lax.fori_loop(0, turns, step, 0)


def two_sweeps(count, field, mass, source, most, plus=0):
    limit = field[0].shape[0]
    half_sweep(field, mass, source, 0, 0, limit, most, plus=plus)
    half_sweep(field, mass, source, 1, 1, limit - 1, most, plus=plus)

    @pl.when(count >= 2)
    def _():
        half_sweep(field, mass, source, 0, 1, limit - 1, most, plus=plus)
        half_sweep(field, mass, source, 1, 2, limit - 2, most, plus=plus)


def source_from_defect(field, mass, source, beside=None, inner=None, plus=0):
    limit, rows, columns = field[0].shape
    is_odd = odd((rows, columns), plus=plus)
    beside = beside or (lambda value: both_ways(value, 1))
    for index in inner or range(limit):
        for colour in range(2):
            other = field[1 - colour]
            first, second = other[max(index - 1, 0)], other[min(index + 1, limit - 1)]
            if colour == 1:
                first, second = second, first
            around = other[index] + jnp.where(is_odd, second, first)
            around = around + both_ways(other[index], 0) + beside(other[index])
            source[colour][index] = source[colour][index] - residual(
                around, field[colour][index], mass[colour][index], 0.0
            )


def shifted(value, axis, by):
    count = lax.axis_size(axis)
    return lax.ppermute(value, axis, [(i, (i + by) % count) for i in range(count)])


def swapped_cores(value):
    count = lax.axis_size("brick")
    return lax.ppermute(value, "brick", [(i, i ^ 1) for i in range(count)])


def swapped_chips(value):
    count = lax.axis_size("brick")
    return lax.ppermute(value, "brick", [(i, (i + 1 if i % 2 else i - 1) % count) for i in range(count)])


def both_swapped(inner, outer):
    far = swapped_chips(outer)
    return far, swapped_cores(inner)


def sides(core, outer, inner):
    on_first = jnp.broadcast_to(core, outer.shape) == 0
    return jnp.where(on_first, outer, inner), jnp.where(on_first, inner, outer)


def my_core():
    return lax.axis_index("brick") & 1


def count_of(counts, level):
    return jnp.max(counts[level])


def kept_pairs(pairs):
    quarter = pairs // 4
    kept = list(range(quarter)) + list(range(pairs - quarter, pairs))
    return kept, list(range(quarter, pairs - quarter))


def ride_right(row, mass, source, rider):
    mass = jnp.where(row < 2, roll(rider, -2, 0), jnp.where(row == 4, roll(rider, -1, 0), mass))
    return mass, jnp.where(row < 2, roll(rider, 2, 0), source)


def ride_left(row, mass, source, rider):
    mass = jnp.where(row > 5, roll(rider, 2, 0), jnp.where(row == 3, roll(rider, 1, 0), mass))
    return mass, jnp.where(row > 5, roll(rider, -2, 0), source)


def rider_from_left(row, mass, source):
    return jnp.where(row < 4, roll(mass, 2, 0), jnp.where(row == 5, roll(mass, 1, 0), roll(source, -2, 0)))


def rider_from_right(row, mass, source):
    return jnp.where(row < 2, roll(source, 2, 0), jnp.where(row == 2, roll(mass, -1, 0), roll(mass, -2, 0)))


def pack_kernel(*refs):
    sweeps, *blocks = refs[:4]
    own, outer, inner, edge_left, edge_right, counts, held, arrived, few, few_arrived = refs[4:]
    count = len(blocks)
    core = my_core()
    pairs = own.shape[2]
    rows, columns = own.shape[3:]
    is_odd = odd((rows, columns))
    row = iota((rows, columns), 0)
    upper = row < rows // 2
    parts = arrived.shape[1]
    some = 2 * pairs // parts

    def part_of(at, part):
        span = pl.ds(some * part, some)
        return pltpu.make_async_copy(blocks[at].at[span], held.at[at, span], arrived.at[at, part])

    def packed(at, pair):
        even, next_one = held[at, 2 * pair], held[at, 2 * pair + 1]
        red = jnp.where(is_odd, next_one, even)
        black = jnp.where(is_odd, even, next_one)
        own[at, 0, pair] = red
        own[at, 1, pair] = black
        if pair < 2:
            edge_left[at, 0, pair] = red
            edge_left[at, 1, pair] = black
        if pair >= pairs - 2:
            edge_right[at, 0, pair - pairs + 2] = red
            edge_right[at, 1, pair - pairs + 2] = black
        turned = roll(black, rows // 2, 0)
        return jnp.where(upper, red, turned), jnp.where(upper, turned, red)

    for at in range(count):
        for part in range(parts):
            part_of(at, part).start()
    copy = pltpu.make_async_copy(sweeps, few, few_arrived)
    copy.start()
    copy.wait()
    for level in range(4):
        counts[level] = jnp.full(counts.shape[1:], few[level])
    for part in range(parts):
        part_of(0, part).wait()
        for pair in range(some // 2 * part, some // 2 * (part + 1)):
            outer[pair], inner[pair] = sides(core, *packed(0, pair))
    for at in (1, 2):
        for part in range(parts):
            part_of(at, part).wait()
    kept, riders = kept_pairs(pairs)
    half = pairs // 2
    for k, (pair, other) in enumerate(zip(kept, riders)):
        mass, source = packed(1, pair), packed(2, pair)
        other_mass, rider = packed(1, other), packed(2, other)
        left = ride_left(row, mass[0], source[0], rider[0])
        right = ride_right(row, mass[1], source[1], rider[1])
        places = (pairs + k, pairs + half + k, 2 * pairs + k)
        for place, one, two in zip(places, (*left, other_mass[0]), (*right, other_mass[1])):
            outer[place], inner[place] = sides(core, one, two)


def corner_kernel(y_outer, y_inner, to_left, to_right):
    core = my_core()
    tiles, rows, columns = y_outer.shape
    pairs = tiles if to_left.shape[0] == 3 else tiles * 2 // 5
    from_right = iota((rows, columns), 0) % (rows // 2) < rows // 4
    for out, near, far, kept in ((to_left, 0, 1, 0), (to_right, pairs - 1, pairs - 2, pairs // 2 - 1)):
        out[0], out[1] = sides(core, y_outer[near], y_inner[near])
        both = [far] if out.shape[0] == 3 else [far, pairs + kept, pairs + pairs // 2 + kept]
        for k, at in enumerate(both):
            left, right = sides(core, y_outer[at], y_inner[at])
            out[2 + k] = jnp.where(from_right, right, left)


def pack_shapes(count, pairs, tile):
    shapes = [(count, 2, pairs, *tile)] + [(pairs if count == 1 else pairs * 5 // 2, *tile)] * 2
    return shapes + [(count, 2, 2, *tile)] * 2


def packed_blocks(sweeps, blocks):
    count = len(blocks)
    rows, *tile = blocks[0].shape
    shapes = pack_shapes(count, rows // 2, tile)
    return pl.pallas_call(
        pack_kernel,
        out_shape=[pltpu.VMEM(shape, jnp.float32) for shape in shapes] + [pltpu.VMEM((4, 8, LANES), jnp.int32)],
        in_specs=[pl.BlockSpec(memory_space=pltpu.HBM)] * (1 + count),
        out_specs=[pl.BlockSpec(memory_space=pltpu.VMEM)] * (len(shapes) + 1),
        scratch_shapes=[
            pltpu.VMEM((count, rows, *tile), jnp.float32),
            pltpu.SemaphoreType.DMA((count, 4)),
            pltpu.SMEM((4,), jnp.int32),
            pltpu.SemaphoreType.DMA,
        ],
        compiler_params=pltpu.CompilerParams(vmem_limit_bytes=12 * MIB),
    )(*[pltpu.with_memory_space_constraint(value, pltpu.HBM) for value in (sweeps, *blocks)])


def first_exchange(own, outer, inner, edge_left, edge_right):
    count, tile = own.shape[0], own.shape[3:]
    y_outer, y_inner = both_swapped(inner, outer)
    x_left = shifted(edge_right, "group", 1)
    x_right = shifted(edge_left, "group", -1)
    corners = call(corner_kernel, [(3 if count == 1 else 5, *tile)] * 2, [y_outer, y_inner])
    c_left = shifted(corners[1], "group", 1)
    c_right = shifted(corners[0], "group", -1)
    return own, x_left, x_right, y_outer, y_inner, c_left, c_right


def assemble_first(window, at, own, x_left, x_right, y_outer, y_inner, c_left, c_right):
    pairs, wide, columns = own.shape[2:]
    row = iota((wide, columns), 0)
    upper = row < wide // 2
    kept, riders = kept_pairs(pairs)
    core = my_core()

    def put(to, red, black, from_left, from_right):
        window[0][to, :wide] = red
        window[0][to, wide:] = jnp.where(upper, from_right, from_left)
        window[1][to, :wide] = black
        window[1][to, wide:] = roll(jnp.where(upper, from_left, from_right), wide // 2, 0)

    def beside(place):
        return sides(core, y_outer[place], y_inner[place])

    for pair in range(pairs):
        if at == 0:
            left, right = beside(pair)
        elif pair in kept:
            left, right = beside(pairs + (at - 1) * (pairs // 2) + kept.index(pair))
        elif at == 1:
            left, right = beside(2 * pairs + riders.index(pair))
        else:
            (left, right), other = beside(pairs + riders.index(pair)), beside(pairs + pairs // 2 + riders.index(pair))
            left, right = rider_from_left(row, left, other[0]), rider_from_right(row, right, other[1])
        put(pair + 2, own[at, 0, pair], own[at, 1, pair], left, right)
    for k in range(2):
        for to, near, x_side, corner in ((k, k == 1, x_left, c_left), (pairs + 2 + k, k == 0, x_right, c_right)):
            if at == 0:
                left, right = (corner[0], corner[1]) if near else (corner[2], corner[2])
            else:
                left = right = corner[2 + at]
            put(to, x_side[at, 0, k], x_side[at, 1, k], left, right)


def first_kernel(counts, *refs):
    halo, refs = refs[:7], refs[7:]
    fine, nxt, edge_left, edge_right, *refs = refs
    again, windows, field, rest = refs[:5], refs[5:9], refs[9:11], refs[11:]
    mass, source = windows[:2], windows[2:]
    for at, window in enumerate((field, mass, source)):
        assemble_first(window, at, *halo)
    first_finish(count_of(counts, 0), field, mass, source, (fine, nxt, edge_left, edge_right), again, *rest)


def first_again_kernel(counts, *refs):
    halo, mass, source, outs, field, rest = refs[:7], refs[7:9], refs[9:11], refs[11:15], refs[15:17], refs[17:]
    assemble_first(field, 0, *halo)
    first_finish(count_of(counts, 0) - 2, field, mass, source, outs, None, *rest)


def first_finish(count, field, mass, source, outs, again, tall, held, sent):
    fine, nxt, edge_left, edge_right = outs
    limit, rows, columns = field[0].shape
    pairs, wide = limit - 4, rows // 2
    two_sweeps(count, field, mass, source, 4)
    is_odd = odd((wide, columns))
    row = iota((wide, columns), 0)
    top, bottom = row == 0, row == wide - 1
    copy = pltpu.make_async_copy(held, fine, sent)

    if again is not None:

        @pl.when(count > 2)
        def _():
            own, outer, inner, *edges = again
            upper = row < wide // 2
            for pair in range(pairs):
                red, black = field[0][pair + 2, :wide], field[1][pair + 2, :wide]
                own[0, 0, pair] = red
                own[0, 1, pair] = black
                turned = roll(black, wide // 2, 0)
                outer[pair], inner[pair] = sides(
                    my_core(), jnp.where(upper, red, turned), jnp.where(upper, turned, red)
                )
                for edge, first in zip(edges, (0, pairs - 2)):
                    if first <= pair < first + 2:
                        edge[0, 0, pair - first] = red
                        edge[0, 1, pair - first] = black

    def keep(index, value):
        for c in range(columns // LANES):
            tall[c, index] = value[:, c * LANES : (c + 1) * LANES]

    @pl.when(count <= 2)
    def _():
        for pair in range(pairs):
            red, black = field[0][pair + 2, :wide], field[1][pair + 2, :wide]
            held[2 * pair] = jnp.where(is_odd, black, red)
            held[2 * pair + 1] = jnp.where(is_odd, red, black)
        copy.start()

        def step(pair, carry):
            total = jnp.zeros((wide, columns), jnp.float32)
            for colour in range(2):
                other = field[1 - colour][pair + 2, :wide]
                first = jnp.where(pair == 0, 0.0, field[1 - colour][pair + 1, :wide])
                second = jnp.where(pair == pairs - 1, 0.0, field[1 - colour][pair + 3, :wide])
                if colour == 1:
                    first, second = second, first
                around = other + jnp.where(is_odd, second, first) + both_ways(other, 1)
                around = around + jnp.where(bottom, 0.0, roll(other, -1, 0))
                around = around + jnp.where(top, 0.0, roll(other, 1, 0))
                at = (pair + 2, slice(0, wide))
                total = total + residual(around, field[colour][at], mass[colour][at], source[colour][at])
            keep(pair, field[0][at] + field[1][at])
            keep(pairs + pair, total)
            keep(2 * pairs + pair, mass[0][at] + mass[1][at])
            return carry

        lax.fori_loop(0, pairs, step, 0, unroll=2)
        low = jnp.where(is_odd, field[1][2, :wide], field[0][2, :wide])
        high = jnp.where(is_odd, field[0][pairs + 1, :wide], field[1][pairs + 1, :wide])
        half, tiles, quarter = columns // 2, pairs // 2, wide // 2
        keep(3 * pairs, high)
        keep(3 * pairs + 1, low)
        lines = (3 * pairs + 2) * wide // 2
        flat = tall.reshape(columns // LANES, 2 * lines, LANES)

        def every_other(start):
            parts = [flat[c, pl.ds(start, lines, stride=2)] for c in range(columns // LANES)]
            return jnp.concatenate(parts, 1)

        firsts, seconds = every_other(0), every_other(1)
        whole = (iota((wide, columns), 0)) % quarter
        y_faces = []
        for t in range(tiles):
            last, head = seconds[t * wide : (t + 1) * wide], firsts[t * wide : (t + 1) * wide]
            y_faces.append(
                jnp.where(
                    whole == 0,
                    roll(last, quarter + 1, 0),
                    jnp.where(whole == quarter - 1, roll(head, quarter - 1, 0), 0.0),
                )
            )
        narrow = pooled(jnp.concatenate([firsts + seconds] + y_faces, 0), pool_matrix(columns, half))
        is_odd_half = odd((wide, half), quarter)
        is_even = same_member((wide, half), quarter)

        def packed(index, factor):
            tile = narrow[index * wide : (index + 1) * wide] * factor
            return jnp.where(is_odd_half, roll(tile, quarter, 0), tile)

        face_x = packed(3 * tiles, 0.5)
        for t in range(tiles):
            values = [
                packed(t, 0.125),
                packed(tiles + t, 0.5),
                packed(2 * tiles + t, 0.5),
                packed(3 * tiles + 1 + t, 0.5),
            ]
            for at, value in enumerate(values):
                nxt[at, t] = value
                if t < 2:
                    if at == 1 and t == 1:
                        value = jnp.where(is_even, value, face_x)
                    edge_left[at, t] = value
                if t >= tiles - 2:
                    if at == 1 and t == tiles - 2:
                        value = jnp.where(is_even, face_x, value)
                    edge_right[at, t - tiles + 2] = value
        nxt[4, 0] = face_x
        for t in range(1, tiles):
            nxt[4, t] = jnp.zeros((wide, half), jnp.float32)
        copy.wait()


def first_level(field, mass, source, sweeps):
    rows, wide, columns = field.shape
    pairs = rows // 2
    half, tiles = columns // 2, pairs // 2
    window = (pairs + 4, 2 * wide, columns)
    outs = [
        (rows, wide, columns),
        (5, tiles, wide, half),
        (4, 2, wide, half),
        (4, 2, wide, half),
    ]

    tall = (columns // LANES, 3 * pairs + 2, wide, LANES)
    *packed, counts = packed_blocks(sweeps, [field, mass, source])
    halo = first_exchange(*packed)
    every = outs + pack_shapes(1, pairs, (wide, columns)) + [window] * 4
    results = call(first_kernel, every, [counts, *halo], [window, window, tall], 1, 24 * MIB)
    once, more, fixed = results[:4], results[4:9], results[9:]

    def again(given):
        args = [counts, *first_exchange(*more), *fixed]
        return list(call(first_again_kernel, outs, args, [window, window, tall], 1, 24 * MIB))

    return counts, lax.cond(sweeps[0] > 2, again, lambda given: given, list(once))


def sent_place(at, t, limit):
    return at * limit + t if at < 2 else 2 * limit + min(max(t - 1, 0), limit - 3)


def second_prepare_kernel(own, x_left, x_right, extended, outer, inner, faces):
    tiles, wide, columns = own.shape[1:]
    quarter = wide // 2
    row_of = iota((wide, columns), 0) % quarter
    is_even = same_member((wide, columns), quarter)
    face_x = own[4, 0]
    for t in range(tiles + 4):
        if t < 2:
            source, k = x_left, t
        elif t < tiles + 2:
            source, k = own, t - 2
        else:
            source, k = x_right, t - tiles - 2
        defect = source[1, k]
        if t == 1:
            defect = defect + jnp.where(is_even, 0.0, face_x)
        if t == 2:
            defect = defect + jnp.where(is_even, x_left[1, 0], 0.0)
        if t == tiles + 1:
            defect = defect + jnp.where(is_even, 0.0, x_right[1, 1])
        if t == tiles + 2:
            defect = defect + jnp.where(is_even, face_x, 0.0)
        face_y = source[3, k]
        faces[t] = face_y
        for at in range(3):
            value = defect if at == 1 else source[at, k]
            extended[at, t] = value
            left = jnp.where(row_of == quarter - 1, face_y, value) if at == 1 else value
            right = jnp.where(row_of == 0, face_y, value) if at == 1 else value
            if at == 0:
                outer[t] = inner[t] = value
            elif at == 1 or 0 < t < tiles + 3:
                place = sent_place(at, t, tiles + 4)
                outer[place], inner[place] = sides(my_core(), left, right)


def assemble_second(window, to, tile, left, right):
    wide = tile.shape[0]
    quarter = wide // 2
    upper = iota(tile.shape, 0) < quarter
    window[0][to, :wide] = jnp.where(upper, tile, roll(right, quarter, 0))
    window[0][to, wide:] = roll(left, quarter, 0)
    window[1][to, :wide] = jnp.where(upper, roll(tile, quarter, 0), right)
    window[1][to, wide:] = left


def second_finish(count, field, mass, source, middle, packed, nxt, tall, held, sent):
    limit, rows, columns = field[0].shape
    pairs = limit - 4
    wide = rows // 2
    quarter = wide // 2
    two_sweeps(count, field, mass, source, 6)
    is_odd = odd((wide, columns), quarter)
    row = iota((wide, columns), 0)
    upper = row < quarter
    top, bottom = row == 0, row == quarter - 1
    for pair in range(pairs):
        red, black = field[0][pair + 2, :wide], field[1][pair + 2, :wide]
        tile = jnp.where(upper, red, roll(black, quarter, 0))
        packed[pair] = tile
        plain = jnp.where(is_odd, roll(tile, quarter, 0), tile)
        held[2 * pair] = plain[:quarter]
        held[2 * pair + 1] = plain[quarter:]
    copy = pltpu.make_async_copy(held, middle, sent)

    @pl.when(count <= 2)
    def _():
        copy.start()
        for pair in range(pairs):
            total = jnp.zeros((wide, columns), jnp.float32)
            for colour in range(2):
                other = field[1 - colour][pair + 2, :wide]
                around = other + both_ways(other, 1)
                around = around + jnp.where(bottom, 0.0, roll(other, -1, 0))
                around = around + jnp.where(top, 0.0, roll(other, 1, 0))
                first = field[1 - colour][pair + 1, :wide] if pair else 0.0
                second = field[1 - colour][pair + 3, :wide] if pair < pairs - 1 else 0.0
                if colour == 1:
                    first, second = second, first
                around = around + jnp.where(is_odd, second, first)
                at = (pair + 2, slice(0, wide))
                total = total + residual(around, field[colour][at], mass[colour][at], source[colour][at])
            values = [field[0][at] + field[1][at], total, mass[0][at] + mass[1][at]]
            for at, value in enumerate(values):
                for r in range(quarter):
                    tall[at, r, pair : pair + 1] = value[r : r + 1]
        low = jnp.where(is_odd, field[1][2, :wide], field[0][2, :wide])
        high = jnp.where(is_odd, field[0][pairs + 1, :wide], field[1][pairs + 1, :wide])
        pieces = []
        for at in range(3):
            for r in range(0, quarter, 2):
                pieces.append((tall[at, r] + tall[at, r + 1]) * (0.125 if at == 0 else 0.5))
        pieces.append(tall[0, 0] * 0.5)
        pieces.append(tall[0, quarter - 1] * 0.5)
        face = jnp.where(upper, high, roll(low, quarter, 0))
        pieces.append((face + roll(face, -1, 0)) * 0.5)
        wide_rows = jnp.concatenate(pieces, 0)
        nxt[...] = pooled(wide_rows, pool_matrix(columns, columns // 2)).reshape(nxt.shape)
        copy.wait()


def second_kernel(counts, extended, outer, inner, faces, middle, packed, nxt, *rest):
    mass, source, field, rest = rest[0:2], rest[2:4], rest[4:6], rest[6:]
    limit, wide, columns = extended.shape[1:]
    quarter = wide // 2
    row_of = iota((wide, columns), 0) % quarter
    top, bottom = row_of == 0, row_of == quarter - 1
    core = my_core()
    for t in range(limit):
        places = [sent_place(at, t, limit) for at in range(3)]
        beside = [sides(core, outer[place], inner[place]) for place in places]
        assemble_second(field, t, extended[0, t], *beside[0])
        assemble_second(mass, t, extended[2, t], *beside[2])
        (one, two), face = beside[1], faces[t]
        tile = extended[1, t] + jnp.where(top, one, 0.0) + jnp.where(bottom, two, 0.0)
        one = one + jnp.where(bottom, face, 0.0)
        two = two + jnp.where(top, face, 0.0)
        assemble_second(source, t, tile, one, two)
    source_from_defect(field, mass, source)
    second_finish(count_of(counts, 1), field, mass, source, middle, packed, nxt, *rest)


def second_again_kernel(counts, extended, outer, inner, *rest):
    mass, source = rest[0:2], rest[2:4]
    middle, packed, nxt, *rest = rest[4:]
    field, rest = rest[:2], rest[2:]
    core = my_core()
    for t in range(extended.shape[0]):
        assemble_second(field, t, extended[t], *sides(core, outer[t], inner[t]))
    second_finish(count_of(counts, 1) - 2, field, mass, source, middle, packed, nxt, *rest)


def second_level(parts, edge_left, edge_right, count, counts):
    tiles, wide, columns = parts.shape[1:]
    limit = tiles + 4
    x_left = shifted(edge_right, "group", 1)
    x_right = shifted(edge_left, "group", -1)
    three = (3, limit, wide, columns)
    message = (3 * limit - 2, wide, columns)
    shapes = [three, message, message, (limit, wide, columns)]
    extended, outer, inner, faces = call(second_prepare_kernel, shapes, [parts, x_left, x_right])
    window = (limit, 2 * wide, columns)
    outs = [(2 * tiles, wide // 2, columns), (tiles, wide, columns), (9, tiles, columns // 2)]
    scratch = [window, window, (3, wide // 2, tiles, columns)]
    args = [counts, extended, *both_swapped(inner, outer), faces]
    middle, packed, nxt, *fixed = call(second_kernel, outs + [window] * 4, args, scratch, 1)

    def again(given):
        packed = given[1]
        x_left = shifted(packed[-2:], "group", 1)
        x_right = shifted(packed[:2], "group", -1)
        extended = jnp.concatenate([x_left, packed, x_right], 0)
        args = [counts, extended, *both_swapped(extended, extended), *fixed]
        return list(call(second_again_kernel, outs, args, scratch, 1))

    done = lax.cond(count > 2, again, lambda given: given, [middle, packed, nxt])
    return done[0], done[2]


def third_prepare_kernel(*refs):
    blocks, out = refs[:-1], refs[-1]
    count = len(blocks)
    rows, columns = blocks[0].shape[1:]
    row = iota((rows, columns), 0)
    for b in range(count):
        span = pl.ds(pl.multiple_of(((lax.axis_index("group") + b) % count) * rows, rows), rows)
        before, after = blocks[b - 1][8], blocks[(b + 1) % count][8]
        for at in range(8):
            value = blocks[b][at]
            if at in (2, 3):
                high = before[2 * (at - 2) : 2 * (at - 2) + 1]
                low = after[rows // 2 + 2 * (at - 2) : rows // 2 + 2 * (at - 2) + 1]
                value = value + jnp.where(row == 0, high, 0.0) + jnp.where(row == rows - 1, low, 0.0)
            out[at, span] = value


FIELD, DEFECT, MASS, FACE = 0, 4, 7, 10


def third_chip_kernel(own, other, chip, rest):
    edge = my_core()
    for at, start in enumerate((FIELD, DEFECT, MASS)):
        values = [own[2 * at + edge], own[2 * at + 1 - edge], other[2 * at + edge], other[2 * at + 1 - edge]]
        if at == 1:
            values[1] = values[1] + other[6 + edge]
            values[2] = values[2] + own[7 - edge]
        for k in range(4 if at == 0 else 3):
            chip[start + k] = values[k]
        if at > 0:
            rest[at - 1] = values[3]
    chip[FACE] = own[6 + edge]
    rest[2] = other[7 - edge]


def third_finish(count, field, mass, source, coarse, packed, message, tall, held, sent):
    rows, columns = field[0].shape[1:]
    core = my_core()
    is_odd = odd((rows, columns), plus=core)
    two_sweeps(count, field, mass, source, 6, core)
    red, black = field[0][2], field[1][2]
    one, two = jnp.where(is_odd, black, red), jnp.where(is_odd, red, black)
    for colour in range(2):
        for k in range(2):
            packed[2 * colour + k] = field[colour][2 + k]
    tall[:rows] = jnp.where(core == 0, one, two)
    tall[rows : 2 * rows] = jnp.where(core == 0, two, one)
    for r in range(rows):
        held[2 * r : 2 * r + 1] = tall[r : r + 1]
        held[2 * r + 1 : 2 * r + 2] = tall[rows + r : rows + r + 1]
    copy = pltpu.make_async_copy(held, coarse, sent)

    @pl.when(count <= 2)
    def _():
        copy.start()
        totals = []
        for q in (2, 3):
            total = jnp.zeros((rows, columns), jnp.float32)
            for colour in range(2):
                other = field[1 - colour]
                beyond = inner_only(is_odd, other[5 - q], q, colour)
                around = other[q] + beyond + both_ways(other[q], 0) + both_ways(other[q], 1)
                total = total + residual(around, field[colour][q], mass[colour][q], source[colour][q])
            totals.append(total * 0.5)
        red, black = field[0][3], field[1][3]
        last = jnp.where(is_odd, red, black)
        pieces = [(field[0][q] + field[1][q]) * 0.125 for q in (2, 3)] + totals
        pieces += [(mass[0][q] + mass[1][q]) * 0.5 for q in (2, 3)] + [one * 0.5, last * 0.5]
        tall[...] = pooled(jnp.concatenate(pieces, 0), pool_matrix(columns, columns))
        half = rows // 2
        narrow = tall[pl.ds(0, 8 * half, stride=2)] + tall[pl.ds(1, 8 * half, stride=2)]
        lane = iota((half, columns), 1) // (columns // 2)
        lower = lane == core
        is_odd_half = odd((half, columns))
        even_row = same_row((half, columns))

        def narrow_of(k):
            return narrow[k * half : (k + 1) * half]

        tiles = []
        for at in range(3):
            tile = jnp.where(lower, narrow_of(2 * at), narrow_of(2 * at + 1))
            tiles.append(jnp.where(is_odd_half, roll(tile, columns // 2, 1), tile))
        low_face = jnp.where(core == 0, narrow_of(6), narrow_of(7))
        high_face = jnp.where(core == 0, narrow_of(7), narrow_of(6))
        tiles.append(jnp.where(even_row, high_face, low_face))
        for at in range(2):
            tile = jnp.where(core == 0, tiles[at], tiles[2 + at])
            tile = jnp.where(lax.axis_index("brick") < message.shape[0], tile, roll(tile, columns // 2, 1))
            for c in range(message.shape[0]):
                message[c, at] = tile
        copy.wait()


def same_row(shape):
    half = shape[1] // 2
    lane = iota(shape, 1)
    return ((iota(shape, 0) + lane + lane // half) & 1) == 0


def inner_only(is_odd, inner, q, colour):
    above = is_odd if colour == 0 else jnp.logical_not(is_odd)
    return jnp.where(above, inner, 0.0) if q == 2 else jnp.where(above, 0.0, inner)


def pack_pair(window, at, even, next_one, is_odd):
    window[0][at] = jnp.where(is_odd, next_one, even)
    window[1][at] = jnp.where(is_odd, even, next_one)


def third_kernel(counts, chip, inner, near, far, coarse, packed, message, *rest):
    mass, source, field, rest = rest[0:2], rest[2:4], rest[4:6], rest[6:]
    rows, columns = chip.shape[1:]
    is_odd = odd((rows, columns), plus=my_core())
    for at, (window, start) in enumerate(((field, FIELD), (source, DEFECT), (mass, MASS))):
        side, own, beyond = ([part[start + min(k, 3 if at == 0 else 2)] for k in range(4)] for part in (near, chip, far))
        if at > 0:
            own[3] = inner[at - 1]
        if at == 1:
            side[0] = side[0] + chip[FACE]
            own[0] = own[0] + near[FACE]
            own[3] = own[3] + far[FACE]
            beyond[0] = beyond[0] + inner[2]
        line = side[::-1] + own + beyond
        for q in range(6):
            pack_pair(window, q, line[2 * q], line[2 * q + 1], is_odd)
    source_from_defect(field, mass, source, plus=my_core())
    third_finish(count_of(counts, 2), field, mass, source, coarse, packed, message, *rest)


def third_again_kernel(counts, chip, near, far, *rest):
    mass, source = rest[0:2], rest[2:4]
    coarse, packed, message, *rest = rest[4:]
    field, rest = rest[:2], rest[2:]
    for colour in range(2):
        for k in range(2):
            field[colour][1 - k] = near[2 * colour + k]
            field[colour][2 + k] = chip[2 * colour + k]
            field[colour][4 + k] = far[2 * colour + k]
    third_finish(count_of(counts, 2) - 2, field, mass, source, coarse, packed, message, *rest)


def third_level(part, count, counts):
    groups, chips = lax.axis_size("group"), lax.axis_size("brick") // 2
    tile_rows, columns = part.shape[1:]
    rows = groups * tile_rows
    blocks = [part] + [shifted(part, "group", -d) for d in range(1, groups)]
    (own,) = call(third_prepare_kernel, [(8, rows, columns)], blocks)
    shapes = [(11, rows, columns), (3, rows, columns)]
    chip, inner = call(third_chip_kernel, shapes, [own, swapped_cores(own)])
    near = swapped_chips(chip)
    far = swapped_cores(near)
    window = (6, rows, columns)
    outs = [(2 * rows, columns), (4, rows, columns), (chips, 2, rows // 2, columns)]
    scratch = [window, window, (8 * rows, columns)]
    args = [counts, chip, inner, near, far]
    coarse, packed, message, *fixed = call(third_kernel, outs + [window] * 4, args, scratch, 1)

    def again(given):
        packed = given[1]
        near = swapped_chips(packed)
        args = [counts, packed, near, swapped_cores(near), *fixed]
        return list(call(third_again_kernel, outs, args, scratch, 1))

    done = lax.cond(count > 2, again, lambda given: given, [coarse, packed, message])
    return done[0].reshape(rows, 2, columns), done[2]


def fourth_kernel(counts, own, other, out, *windows):
    field, mass, source, (held, sent) = windows[0:2], windows[2:4], windows[4:6], windows[6:]
    chips, _, rows, columns = own.shape
    tiles, half = chips // 2, columns // 2
    lane = iota((rows, columns), 1)
    low = lane < half
    is_odd = odd((rows, columns))
    first, last = lane % half == 0, lane % half == half - 1

    def turned(value):
        return roll(value, half, 1)

    def beside(value):
        after = jnp.where(last, roll(value, half - 1, 1), roll(value, -1, 1))
        return after + jnp.where(first, roll(value, 1 - half, 1), roll(value, 1, 1))

    def put(window, t, one, two):
        window[0][t + 1] = jnp.where(low, one, two)
        window[1][t + 1] = turned(jnp.where(low, two, one))

    def repeat(window, colour):
        window[colour][0] = turned(window[colour][tiles])
        window[colour][tiles + 1] = turned(window[colour][1])

    def load(one, two):
        even_row = same_row((rows, columns))

        def defect(t):
            before, after = two[(t - 1) % chips, 1], two[(t + 1) % chips, 1]
            before = turned(before) if t in (0, tiles) else before
            after = turned(after) if t in (tiles - 1, chips - 1) else after
            if t < tiles:
                return one[t, 1] + jnp.where(even_row, before, after)
            return one[t, 1] + jnp.where(even_row, after, before)

        for t in range(tiles):
            put(field, t, one[t, 0], one[t + tiles, 0])
            put(mass, t, two[t, 0], two[t + tiles, 0])
            put(source, t, defect(t), defect(t + tiles))

    @pl.when(my_core() == 0)
    def _():
        load(own, other)

    @pl.when(my_core() == 1)
    def _():
        load(other, own)

    for colour in range(2):
        repeat(field, colour)
    source_from_defect(field, mass, source, beside, range(1, tiles + 1))

    def one_sweep(step, carry):
        for colour in range(2):
            half_sweep(field, mass, source, colour, 1, tiles + 1, 16, beside)
            repeat(field, colour)
        return carry

    lax.fori_loop(0, count_of(counts, 3), one_sweep, 0)
    for t in range(tiles):
        red, black = field[0][t + 1], field[1][t + 1]
        red_too, black_too = turned(red), turned(black)
        one = jnp.where(low, jnp.where(is_odd, black, red), jnp.where(is_odd, red_too, black_too))
        two = jnp.where(low, jnp.where(is_odd, black_too, red_too), jnp.where(is_odd, red, black))
        for at, value in ((t, one), (t + tiles, two)):
            held[:, at * columns : (at + 1) * columns] = value
    copy = pltpu.make_async_copy(held, out, sent)
    copy.start()
    copy.wait()


def fourth_level(message, counts):
    chips, _, rows, columns = message.shape
    cores = [[2 * chip + c for chip in range(chips)] for c in range(2)]
    own = lax.all_to_all(message, "brick", 0, 0, axis_index_groups=cores)
    other = swapped_cores(own)
    scratch = [(chips // 2 + 2, rows, columns)] * 6
    (out,) = call(fourth_kernel, [(rows, chips * columns)], [counts, own, other], scratch, 1)
    return out


def on_device(initial_field, mass, source, sweeps):
    counts, (fine, parts, edge_left, edge_right) = first_level(initial_field, mass, source, sweeps)
    middle, part = second_level(parts, edge_left, edge_right, sweeps[1], counts)
    coarse, message = third_level(part, sweeps[2], counts)
    coarsest = fourth_level(message, counts)
    return fine, middle, coarse, coarsest


def solution(mesh):
    return jax.shard_map(
        on_device,
        mesh=mesh,
        in_specs=(
            P("group", "brick", None),
            P("group", "brick", None),
            P("group", "brick", None),
            P(),
        ),
        out_specs=(
            P("group", "brick", None),
            P("group", "brick", None),
            P(None, "brick", None),
            P(),
        ),
        check_vma=False,
    )
```

```python
import functools

import jax
import jax.numpy as jnp
from jax import lax
from jax.experimental import pallas as pl
from jax.experimental.pallas import tpu as pltpu
from jax.sharding import PartitionSpec as P


INTERPRET = False
MIB = 1024 * 1024
LANES = 128


def call(kernel, out_shapes, args, scratch=(), results=0, limit=12 * MIB):
    spec = pl.BlockSpec(memory_space=pltpu.VMEM)
    return pl.pallas_call(
        kernel,
        out_shape=[
            (pltpu.HBM if at < results else pltpu.VMEM)(shape, jnp.float32) for at, shape in enumerate(out_shapes)
        ],
        in_specs=[spec] * len(args),
        out_specs=[pl.BlockSpec(memory_space=pltpu.HBM)] * results + [spec] * (len(out_shapes) - results),
        scratch_shapes=[pltpu.VMEM(shape, jnp.float32) for shape in [*scratch, *out_shapes[:results]]]
        + [pltpu.SemaphoreType.DMA] * results,
        compiler_params=pltpu.CompilerParams(vmem_limit_bytes=limit),
        interpret=INTERPRET,
    )(*args)


def iota(shape, axis):
    return lax.broadcasted_iota(jnp.int32, shape, axis)


def odd(shape, period=None, plus=0):
    rows = iota(shape, 0)
    if period is not None:
        rows = rows % period
    return ((rows + iota(shape, 1) + plus) & 1) == 1


def same_member(shape, quarter):
    rows = iota(shape, 0)
    return ((rows % quarter + rows // quarter + iota(shape, 1)) & 1) == 0


def roll(value, shift, axis):
    return pltpu.roll(value, shift % value.shape[axis], axis)


def both_ways(value, axis):
    return roll(value, 1, axis) + roll(value, -1, axis)


def newton(around, value, mass, source):
    curve = mass * (value * value)
    over = (around + source) + 2.0 * (curve * value)
    under = (6.0 + mass) + 3.0 * curve
    guess = pl.reciprocal(under, approx=True)
    guess = guess * (2.0 - under * guess)
    return over * guess


def residual(around, value, mass, source):
    return (around - 6.0 * value) - mass * (value * value * value + value) + source


def pooled(rows, pool):
    high = rows.astype(jnp.bfloat16)
    rest = rows - high.astype(jnp.float32)
    middle = rest.astype(jnp.bfloat16)
    low = (rest - middle.astype(jnp.float32)).astype(jnp.bfloat16)
    dot = functools.partial(jnp.dot, preferred_element_type=jnp.float32)
    return dot(high, pool) + (dot(middle, pool) + dot(low, pool))


def pool_matrix(width, columns):
    half = width // 2
    shape = (width, columns)
    return jnp.where(iota(shape, 0) // 2 == iota(shape, 1) % half, 1.0, 0.0).astype(jnp.bfloat16)


def half_sweep(field, mass, source, colour, low, high, most, beside=None, plus=0):
    mine, other = field[colour], field[1 - colour]
    limit, rows, columns = mine.shape
    is_odd = odd((rows, columns), plus=plus)
    beside = beside or (lambda value: both_ways(value, 1))
    together = max(k for k in range(1, most + 1) if (high - low) % k == 0)

    def step(turn, carry):
        start = low + turn * together
        near = [other[jnp.clip(start + k, 0, limit - 1)] for k in range(-1, together + 1)]
        fresh = []
        for k in range(together):
            first, second = (near[k], near[k + 2]) if colour == 0 else (near[k + 2], near[k])
            around = near[k + 1] + jnp.where(is_odd, second, first)
            around = around + both_ways(near[k + 1], 0) + beside(near[k + 1])
            fresh.append(newton(around, mine[start + k], mass[colour][start + k], source[colour][start + k]))
        for k in range(together):
            mine[start + k] = fresh[k]
        return carry

    turns = (high - low) // together
    if turns == 1:
        step(0, 0)
    else:
        lax.fori_loop(0, turns, step, 0)


def two_sweeps(count, field, mass, source, most, plus=0):
    limit = field[0].shape[0]
    half_sweep(field, mass, source, 0, 0, limit, most, plus=plus)
    half_sweep(field, mass, source, 1, 1, limit - 1, most, plus=plus)

    @pl.when(count >= 2)
    def _():
        half_sweep(field, mass, source, 0, 1, limit - 1, most, plus=plus)
        half_sweep(field, mass, source, 1, 2, limit - 2, most, plus=plus)


def source_from_defect(field, mass, source, beside=None, inner=None, plus=0):
    limit, rows, columns = field[0].shape
    is_odd = odd((rows, columns), plus=plus)
    beside = beside or (lambda value: both_ways(value, 1))
    for index in inner or range(limit):
        for colour in range(2):
            other = field[1 - colour]
            first, second = other[max(index - 1, 0)], other[min(index + 1, limit - 1)]
            if colour == 1:
                first, second = second, first
            around = other[index] + jnp.where(is_odd, second, first)
            around = around + both_ways(other[index], 0) + beside(other[index])
            source[colour][index] = source[colour][index] - residual(
                around, field[colour][index], mass[colour][index], 0.0
            )


def shifted(value, axis, by):
    count = lax.axis_size(axis)
    return lax.ppermute(value, axis, [(i, (i + by) % count) for i in range(count)])


def swapped_cores(value):
    count = lax.axis_size("brick")
    return lax.ppermute(value, "brick", [(i, i ^ 1) for i in range(count)])


def swapped_chips(value):
    count = lax.axis_size("brick")
    return lax.ppermute(value, "brick", [(i, (i + 1 if i % 2 else i - 1) % count) for i in range(count)])


def both_swapped(inner, outer):
    far = swapped_chips(outer)
    return far, swapped_cores(inner)


def sides(core, outer, inner):
    on_first = jnp.broadcast_to(core, outer.shape) == 0
    return jnp.where(on_first, outer, inner), jnp.where(on_first, inner, outer)


def my_core():
    return lax.axis_index("brick") & 1


def count_of(counts, level):
    return jnp.max(counts[level])


def kept_pairs(pairs):
    quarter = pairs // 4
    kept = list(range(quarter)) + list(range(pairs - quarter, pairs))
    return kept, list(range(quarter, pairs - quarter))


def ride_right(row, mass, source, rider):
    mass = jnp.where(row < 2, roll(rider, -2, 0), jnp.where(row == 4, roll(rider, -1, 0), mass))
    return mass, jnp.where(row < 2, roll(rider, 2, 0), source)


def ride_left(row, mass, source, rider):
    mass = jnp.where(row > 5, roll(rider, 2, 0), jnp.where(row == 3, roll(rider, 1, 0), mass))
    return mass, jnp.where(row > 5, roll(rider, -2, 0), source)


def rider_from_left(row, mass, source):
    return jnp.where(row < 4, roll(mass, 2, 0), jnp.where(row == 5, roll(mass, 1, 0), roll(source, -2, 0)))


def rider_from_right(row, mass, source):
    return jnp.where(row < 2, roll(source, 2, 0), jnp.where(row == 2, roll(mass, -1, 0), roll(mass, -2, 0)))


def pack_kernel(*refs):
    sweeps, *blocks = refs[:4]
    own, outer, inner, edge_left, edge_right, counts, held, arrived, few, few_arrived = refs[4:]
    count = len(blocks)
    core = my_core()
    pairs = own.shape[2]
    rows, columns = own.shape[3:]
    is_odd = odd((rows, columns))
    row = iota((rows, columns), 0)
    upper = row < rows // 2
    parts = arrived.shape[1]
    some = 2 * pairs // parts

    def part_of(at, part):
        span = pl.ds(some * part, some)
        return pltpu.make_async_copy(blocks[at].at[span], held.at[at, span], arrived.at[at, part])

    def packed(at, pair):
        even, next_one = held[at, 2 * pair], held[at, 2 * pair + 1]
        red = jnp.where(is_odd, next_one, even)
        black = jnp.where(is_odd, even, next_one)
        own[at, 0, pair] = red
        own[at, 1, pair] = black
        if pair < 2:
            edge_left[at, 0, pair] = red
            edge_left[at, 1, pair] = black
        if pair >= pairs - 2:
            edge_right[at, 0, pair - pairs + 2] = red
            edge_right[at, 1, pair - pairs + 2] = black
        turned = roll(black, rows // 2, 0)
        return jnp.where(upper, red, turned), jnp.where(upper, turned, red)

    for at in range(count):
        for part in range(parts):
            part_of(at, part).start()
    copy = pltpu.make_async_copy(sweeps, few, few_arrived)
    copy.start()
    copy.wait()
    for level in range(4):
        counts[level] = jnp.full(counts.shape[1:], few[level])
    for part in range(parts):
        part_of(0, part).wait()
        for pair in range(some // 2 * part, some // 2 * (part + 1)):
            outer[pair], inner[pair] = sides(core, *packed(0, pair))
    for at in (1, 2):
        for part in range(parts):
            part_of(at, part).wait()
    kept, riders = kept_pairs(pairs)
    half = pairs // 2
    for k, (pair, other) in enumerate(zip(kept, riders)):
        mass, source = packed(1, pair), packed(2, pair)
        other_mass, rider = packed(1, other), packed(2, other)
        left = ride_left(row, mass[0], source[0], rider[0])
        right = ride_right(row, mass[1], source[1], rider[1])
        places = (pairs + k, pairs + half + k, 2 * pairs + k)
        for place, one, two in zip(places, (*left, other_mass[0]), (*right, other_mass[1])):
            outer[place], inner[place] = sides(core, one, two)


def corner_kernel(y_outer, y_inner, to_left, to_right):
    core = my_core()
    tiles, rows, columns = y_outer.shape
    pairs = tiles if to_left.shape[0] == 3 else tiles * 2 // 5
    from_right = iota((rows, columns), 0) % (rows // 2) < rows // 4
    for out, near, far, kept in ((to_left, 0, 1, 0), (to_right, pairs - 1, pairs - 2, pairs // 2 - 1)):
        out[0], out[1] = sides(core, y_outer[near], y_inner[near])
        both = [far] if out.shape[0] == 3 else [far, pairs + kept, pairs + pairs // 2 + kept]
        for k, at in enumerate(both):
            left, right = sides(core, y_outer[at], y_inner[at])
            out[2 + k] = jnp.where(from_right, right, left)


def pack_shapes(count, pairs, tile):
    shapes = [(count, 2, pairs, *tile)] + [(pairs if count == 1 else pairs * 5 // 2, *tile)] * 2
    return shapes + [(count, 2, 2, *tile)] * 2


def packed_blocks(sweeps, blocks):
    count = len(blocks)
    rows, *tile = blocks[0].shape
    shapes = pack_shapes(count, rows // 2, tile)
    return pl.pallas_call(
        pack_kernel,
        out_shape=[pltpu.VMEM(shape, jnp.float32) for shape in shapes] + [pltpu.VMEM((4, 8, LANES), jnp.int32)],
        in_specs=[pl.BlockSpec(memory_space=pltpu.HBM)] * (1 + count),
        out_specs=[pl.BlockSpec(memory_space=pltpu.VMEM)] * (len(shapes) + 1),
        scratch_shapes=[
            pltpu.VMEM((count, rows, *tile), jnp.float32),
            pltpu.SemaphoreType.DMA((count, 4)),
            pltpu.SMEM((4,), jnp.int32),
            pltpu.SemaphoreType.DMA,
        ],
        compiler_params=pltpu.CompilerParams(vmem_limit_bytes=12 * MIB),
    )(*[pltpu.with_memory_space_constraint(value, pltpu.HBM) for value in (sweeps, *blocks)])


def first_exchange(own, outer, inner, edge_left, edge_right):
    count, tile = own.shape[0], own.shape[3:]
    y_outer, y_inner = both_swapped(inner, outer)
    x_left = shifted(edge_right, "group", 1)
    x_right = shifted(edge_left, "group", -1)
    corners = call(corner_kernel, [(3 if count == 1 else 5, *tile)] * 2, [y_outer, y_inner])
    c_left = shifted(corners[1], "group", 1)
    c_right = shifted(corners[0], "group", -1)
    return own, x_left, x_right, y_outer, y_inner, c_left, c_right


def put_first(window, to, red, black, from_left, from_right):
    wide = red.shape[0]
    upper = iota(red.shape, 0) < wide // 2
    window[0][to, :wide] = red
    window[0][to, wide:] = jnp.where(upper, from_right, from_left)
    window[1][to, :wide] = black
    window[1][to, wide:] = roll(jnp.where(upper, from_left, from_right), wide // 2, 0)


def assemble_own(window, at, own, y_outer, y_inner):
    pairs, wide, columns = own.shape[2:]
    row = iota((wide, columns), 0)
    kept, riders = kept_pairs(pairs)
    core = my_core()

    def beside(place):
        return sides(core, y_outer[place], y_inner[place])

    for pair in range(pairs):
        if at == 0:
            left, right = beside(pair)
        elif pair in kept:
            left, right = beside(pairs + (at - 1) * (pairs // 2) + kept.index(pair))
        elif at == 1:
            left, right = beside(2 * pairs + riders.index(pair))
        else:
            (left, right), other = beside(pairs + riders.index(pair)), beside(pairs + pairs // 2 + riders.index(pair))
            left, right = rider_from_left(row, left, other[0]), rider_from_right(row, right, other[1])
        put_first(window, pair, own[at, 0, pair], own[at, 1, pair], left, right)


def assemble_edges(window, at, places, x_left, x_right, c_left, c_right):
    for side, x_side, corner in ((0, x_left, c_left), (1, x_right, c_right)):
        for k in range(2):
            if at == 0:
                near = k != side
                left, right = (corner[0], corner[1]) if near else (corner[2], corner[2])
            else:
                left = right = corner[2 + at]
            put_first(window, places[2 * side + k], x_side[at, 0, k], x_side[at, 1, k], left, right)


def inner_sweeps(count, field, mass, source):
    pairs = field[0].shape[0]

    def half(colour, less):
        whole = (pairs - 2 * less) // 4 * 4
        half_sweep(field, mass, source, colour, less, less + whole, 4)
        if whole < pairs - 2 * less:
            half_sweep(field, mass, source, colour, less + whole, pairs - less, 4)

    half(0, 1)
    half(1, 2)

    @pl.when(count >= 2)
    def _():
        half(0, 3)
        half(1, 4)


def edge_sweeps(count, field, mass_of, source_of):
    limit, rows, columns = field[0].shape
    is_odd = odd((rows, columns))

    def some(colour, positions):
        mine, other = field[colour], field[1 - colour]
        fresh = []
        for w in positions:
            first, second = other[max(w - 1, 0)], other[min(w + 1, limit - 1)]
            if colour == 1:
                first, second = second, first
            value = other[w]
            around = value + jnp.where(is_odd, second, first) + both_ways(value, 0) + both_ways(value, 1)
            fresh.append(newton(around, mine[w], mass_of(colour, w), source_of(colour, w)))
        for w, value in zip(positions, fresh):
            mine[w] = value

    def half(colour, low, high):
        some(colour, range(low, high))
        some(colour, range(limit - high, limit - low))

    half(0, 0, 3)
    half(1, 1, 4)

    @pl.when(count >= 2)
    def _():
        half(0, 1, 5)
        half(1, 2, 6)


def first_inner_kernel(counts, own, y_outer, y_inner, *windows):
    field, mass, source = windows[:2], windows[2:4], windows[4:]
    for at, window in enumerate((field, mass, source)):
        assemble_own(window, at, own, y_outer, y_inner)
    inner_sweeps(count_of(counts, 0), field, mass, source)


def first_inner_again_kernel(counts, own, y_outer, y_inner, *windows):
    mass, source, field = windows[:2], windows[2:4], windows[4:]
    assemble_own(field, 0, own, y_outer, y_inner)
    inner_sweeps(count_of(counts, 0) - 2, field, mass, source)


def first_outer(count, halo, inner, mass, source, edges, field):
    pairs = inner[0].shape[0]
    for colour in range(2):
        for pair in range(pairs):
            field[colour][pair + 2] = inner[colour][pair]
    assemble_edges(field, 0, (0, 1, pairs + 2, pairs + 3), *halo)

    def of(whole, beyond):
        def at(colour, w):
            if 2 <= w < pairs + 2:
                return whole[colour][w - 2]
            return beyond[colour][w if w < 2 else w - pairs]

        return at

    edge_sweeps(count, field, of(mass, edges[:2]), of(source, edges[2:]))


def first_kernel(counts, *refs):
    halo, inner, mass, source, refs = refs[:4], refs[4:6], refs[6:8], refs[8:10], refs[10:]
    outs, again, edges, field, rest = refs[:4], refs[4:9], refs[9:13], refs[13:15], refs[15:]
    for at, window in ((1, edges[:2]), (2, edges[2:])):
        assemble_edges(window, at, range(4), *halo)
    count = count_of(counts, 0)
    first_outer(count, halo, inner, mass, source, edges, field)
    first_finish(count, field, mass, source, outs, again, *rest)


def first_again_kernel(counts, *refs):
    halo, inner, mass, source, edges, refs = refs[:4], refs[4:6], refs[6:8], refs[8:10], refs[10:14], refs[14:]
    outs, field, rest = refs[:4], refs[4:6], refs[6:]
    count = count_of(counts, 0) - 2
    first_outer(count, halo, inner, mass, source, edges, field)
    first_finish(count, field, mass, source, outs, None, *rest)


def first_finish(count, field, mass, source, outs, again, tall, held, sent):
    fine, nxt, edge_left, edge_right = outs
    limit, rows, columns = field[0].shape
    pairs, wide = limit - 4, rows // 2
    is_odd = odd((wide, columns))
    row = iota((wide, columns), 0)
    top, bottom = row == 0, row == wide - 1
    copy = pltpu.make_async_copy(held, fine, sent)

    if again is not None:

        @pl.when(count > 2)
        def _():
            own, outer, inner, *edges = again
            upper = row < wide // 2
            for pair in range(pairs):
                red, black = field[0][pair + 2, :wide], field[1][pair + 2, :wide]
                own[0, 0, pair] = red
                own[0, 1, pair] = black
                turned = roll(black, wide // 2, 0)
                outer[pair], inner[pair] = sides(
                    my_core(), jnp.where(upper, red, turned), jnp.where(upper, turned, red)
                )
                for edge, first in zip(edges, (0, pairs - 2)):
                    if first <= pair < first + 2:
                        edge[0, 0, pair - first] = red
                        edge[0, 1, pair - first] = black

    def keep(index, value):
        for c in range(columns // LANES):
            tall[c, index] = value[:, c * LANES : (c + 1) * LANES]

    @pl.when(count <= 2)
    def _():
        for pair in range(pairs):
            red, black = field[0][pair + 2, :wide], field[1][pair + 2, :wide]
            held[2 * pair] = jnp.where(is_odd, black, red)
            held[2 * pair + 1] = jnp.where(is_odd, red, black)
        copy.start()

        def step(pair, carry):
            total = jnp.zeros((wide, columns), jnp.float32)
            for colour in range(2):
                other = field[1 - colour][pair + 2, :wide]
                first = jnp.where(pair == 0, 0.0, field[1 - colour][pair + 1, :wide])
                second = jnp.where(pair == pairs - 1, 0.0, field[1 - colour][pair + 3, :wide])
                if colour == 1:
                    first, second = second, first
                around = other + jnp.where(is_odd, second, first) + both_ways(other, 1)
                around = around + jnp.where(bottom, 0.0, roll(other, -1, 0))
                around = around + jnp.where(top, 0.0, roll(other, 1, 0))
                at, own = (pair + 2, slice(0, wide)), (pair, slice(0, wide))
                total = total + residual(around, field[colour][at], mass[colour][own], source[colour][own])
            keep(pair, field[0][at] + field[1][at])
            keep(pairs + pair, total)
            keep(2 * pairs + pair, mass[0][own] + mass[1][own])
            return carry

        lax.fori_loop(0, pairs, step, 0, unroll=2)
        low = jnp.where(is_odd, field[1][2, :wide], field[0][2, :wide])
        high = jnp.where(is_odd, field[0][pairs + 1, :wide], field[1][pairs + 1, :wide])
        half, tiles, quarter = columns // 2, pairs // 2, wide // 2
        keep(3 * pairs, high)
        keep(3 * pairs + 1, low)
        lines = (3 * pairs + 2) * wide // 2
        flat = tall.reshape(columns // LANES, 2 * lines, LANES)

        def every_other(start):
            parts = [flat[c, pl.ds(start, lines, stride=2)] for c in range(columns // LANES)]
            return jnp.concatenate(parts, 1)

        firsts, seconds = every_other(0), every_other(1)
        whole = (iota((wide, columns), 0)) % quarter
        y_faces = []
        for t in range(tiles):
            last, head = seconds[t * wide : (t + 1) * wide], firsts[t * wide : (t + 1) * wide]
            y_faces.append(
                jnp.where(
                    whole == 0,
                    roll(last, quarter + 1, 0),
                    jnp.where(whole == quarter - 1, roll(head, quarter - 1, 0), 0.0),
                )
            )
        narrow = pooled(jnp.concatenate([firsts + seconds] + y_faces, 0), pool_matrix(columns, half))
        is_odd_half = odd((wide, half), quarter)
        is_even = same_member((wide, half), quarter)

        def packed(index, factor):
            tile = narrow[index * wide : (index + 1) * wide] * factor
            return jnp.where(is_odd_half, roll(tile, quarter, 0), tile)

        face_x = packed(3 * tiles, 0.5)
        for t in range(tiles):
            values = [
                packed(t, 0.125),
                packed(tiles + t, 0.5),
                packed(2 * tiles + t, 0.5),
                packed(3 * tiles + 1 + t, 0.5),
            ]
            for at, value in enumerate(values):
                nxt[at, t] = value
                if t < 2:
                    if at == 1 and t == 1:
                        value = jnp.where(is_even, value, face_x)
                    edge_left[at, t] = value
                if t >= tiles - 2:
                    if at == 1 and t == tiles - 2:
                        value = jnp.where(is_even, face_x, value)
                    edge_right[at, t - tiles + 2] = value
        nxt[4, 0] = face_x
        for t in range(1, tiles):
            nxt[4, t] = jnp.zeros((wide, half), jnp.float32)
        copy.wait()


def first_level(field, mass, source, sweeps):
    rows, wide, columns = field.shape
    pairs = rows // 2
    half, tiles = columns // 2, pairs // 2
    window = (pairs + 4, 2 * wide, columns)
    outs = [
        (rows, wide, columns),
        (5, tiles, wide, half),
        (4, 2, wide, half),
        (4, 2, wide, half),
    ]

    inner, edge = (pairs, 2 * wide, columns), (4, 2 * wide, columns)
    scratch = [window, window, (columns // LANES, 3 * pairs + 2, wide, LANES)]
    *packed, counts = packed_blocks(sweeps, [field, mass, source])
    own, x_left, x_right, y_outer, y_inner, c_left, c_right = first_exchange(*packed)
    windows = call(first_inner_kernel, [inner] * 6, [counts, own, y_outer, y_inner])
    every = outs + pack_shapes(1, pairs, (wide, columns)) + [edge] * 4
    args = [counts, x_left, x_right, c_left, c_right, *windows]
    results = call(first_kernel, every, args, scratch, 1, 20 * MIB)
    once, more, edges = results[:4], results[4:9], results[9:]

    def again(given):
        own, x_left, x_right, y_outer, y_inner, c_left, c_right = first_exchange(*more)
        fixed = windows[2:]
        field = call(first_inner_again_kernel, [inner] * 2, [counts, own, y_outer, y_inner, *fixed])
        args = [counts, x_left, x_right, c_left, c_right, *field, *fixed, *edges]
        return list(call(first_again_kernel, outs, args, scratch, 1, 20 * MIB))

    return counts, lax.cond(sweeps[0] > 2, again, lambda given: given, list(once))


def sent_place(at, t, limit):
    return at * limit + t if at < 2 else 2 * limit + min(max(t - 1, 0), limit - 3)


def second_prepare_kernel(own, x_left, x_right, extended, outer, inner, faces):
    tiles, wide, columns = own.shape[1:]
    quarter = wide // 2
    row_of = iota((wide, columns), 0) % quarter
    is_even = same_member((wide, columns), quarter)
    face_x = own[4, 0]
    for t in range(tiles + 4):
        if t < 2:
            source, k = x_left, t
        elif t < tiles + 2:
            source, k = own, t - 2
        else:
            source, k = x_right, t - tiles - 2
        defect = source[1, k]
        if t == 1:
            defect = defect + jnp.where(is_even, 0.0, face_x)
        if t == 2:
            defect = defect + jnp.where(is_even, x_left[1, 0], 0.0)
        if t == tiles + 1:
            defect = defect + jnp.where(is_even, 0.0, x_right[1, 1])
        if t == tiles + 2:
            defect = defect + jnp.where(is_even, face_x, 0.0)
        face_y = source[3, k]
        faces[t] = face_y
        for at in range(3):
            value = defect if at == 1 else source[at, k]
            extended[at, t] = value
            left = jnp.where(row_of == quarter - 1, face_y, value) if at == 1 else value
            right = jnp.where(row_of == 0, face_y, value) if at == 1 else value
            if at == 0:
                outer[t] = inner[t] = value
            elif at == 1 or 0 < t < tiles + 3:
                place = sent_place(at, t, tiles + 4)
                outer[place], inner[place] = sides(my_core(), left, right)


def assemble_second(window, to, tile, left, right):
    wide = tile.shape[0]
    quarter = wide // 2
    upper = iota(tile.shape, 0) < quarter
    window[0][to, :wide] = jnp.where(upper, tile, roll(right, quarter, 0))
    window[0][to, wide:] = roll(left, quarter, 0)
    window[1][to, :wide] = jnp.where(upper, roll(tile, quarter, 0), right)
    window[1][to, wide:] = left


def second_finish(count, field, mass, source, middle, packed, nxt, tall, held, sent):
    limit, rows, columns = field[0].shape
    pairs = limit - 4
    wide = rows // 2
    quarter = wide // 2
    two_sweeps(count, field, mass, source, 6)
    is_odd = odd((wide, columns), quarter)
    row = iota((wide, columns), 0)
    upper = row < quarter
    top, bottom = row == 0, row == quarter - 1
    for pair in range(pairs):
        red, black = field[0][pair + 2, :wide], field[1][pair + 2, :wide]
        tile = jnp.where(upper, red, roll(black, quarter, 0))
        packed[pair] = tile
        plain = jnp.where(is_odd, roll(tile, quarter, 0), tile)
        held[2 * pair] = plain[:quarter]
        held[2 * pair + 1] = plain[quarter:]
    copy = pltpu.make_async_copy(held, middle, sent)

    @pl.when(count <= 2)
    def _():
        copy.start()
        for pair in range(pairs):
            total = jnp.zeros((wide, columns), jnp.float32)
            for colour in range(2):
                other = field[1 - colour][pair + 2, :wide]
                around = other + both_ways(other, 1)
                around = around + jnp.where(bottom, 0.0, roll(other, -1, 0))
                around = around + jnp.where(top, 0.0, roll(other, 1, 0))
                first = field[1 - colour][pair + 1, :wide] if pair else 0.0
                second = field[1 - colour][pair + 3, :wide] if pair < pairs - 1 else 0.0
                if colour == 1:
                    first, second = second, first
                around = around + jnp.where(is_odd, second, first)
                at = (pair + 2, slice(0, wide))
                total = total + residual(around, field[colour][at], mass[colour][at], source[colour][at])
            values = [field[0][at] + field[1][at], total, mass[0][at] + mass[1][at]]
            for at, value in enumerate(values):
                for r in range(quarter):
                    tall[at, r, pair : pair + 1] = value[r : r + 1]
        low = jnp.where(is_odd, field[1][2, :wide], field[0][2, :wide])
        high = jnp.where(is_odd, field[0][pairs + 1, :wide], field[1][pairs + 1, :wide])
        pieces = []
        for at in range(3):
            for r in range(0, quarter, 2):
                pieces.append((tall[at, r] + tall[at, r + 1]) * (0.125 if at == 0 else 0.5))
        pieces.append(tall[0, 0] * 0.5)
        pieces.append(tall[0, quarter - 1] * 0.5)
        face = jnp.where(upper, high, roll(low, quarter, 0))
        pieces.append((face + roll(face, -1, 0)) * 0.5)
        wide_rows = jnp.concatenate(pieces, 0)
        nxt[...] = pooled(wide_rows, pool_matrix(columns, columns // 2)).reshape(nxt.shape)
        copy.wait()


def second_kernel(counts, extended, outer, inner, faces, middle, packed, nxt, *rest):
    mass, source, field, rest = rest[0:2], rest[2:4], rest[4:6], rest[6:]
    limit, wide, columns = extended.shape[1:]
    quarter = wide // 2
    row_of = iota((wide, columns), 0) % quarter
    top, bottom = row_of == 0, row_of == quarter - 1
    core = my_core()
    for t in range(limit):
        places = [sent_place(at, t, limit) for at in range(3)]
        beside = [sides(core, outer[place], inner[place]) for place in places]
        assemble_second(field, t, extended[0, t], *beside[0])
        assemble_second(mass, t, extended[2, t], *beside[2])
        (one, two), face = beside[1], faces[t]
        tile = extended[1, t] + jnp.where(top, one, 0.0) + jnp.where(bottom, two, 0.0)
        one = one + jnp.where(bottom, face, 0.0)
        two = two + jnp.where(top, face, 0.0)
        assemble_second(source, t, tile, one, two)
    source_from_defect(field, mass, source)
    second_finish(count_of(counts, 1), field, mass, source, middle, packed, nxt, *rest)


def second_again_kernel(counts, extended, outer, inner, *rest):
    mass, source = rest[0:2], rest[2:4]
    middle, packed, nxt, *rest = rest[4:]
    field, rest = rest[:2], rest[2:]
    core = my_core()
    for t in range(extended.shape[0]):
        assemble_second(field, t, extended[t], *sides(core, outer[t], inner[t]))
    second_finish(count_of(counts, 1) - 2, field, mass, source, middle, packed, nxt, *rest)


def second_level(parts, edge_left, edge_right, count, counts):
    tiles, wide, columns = parts.shape[1:]
    limit = tiles + 4
    x_left = shifted(edge_right, "group", 1)
    x_right = shifted(edge_left, "group", -1)
    three = (3, limit, wide, columns)
    message = (3 * limit - 2, wide, columns)
    shapes = [three, message, message, (limit, wide, columns)]
    extended, outer, inner, faces = call(second_prepare_kernel, shapes, [parts, x_left, x_right])
    window = (limit, 2 * wide, columns)
    outs = [(2 * tiles, wide // 2, columns), (tiles, wide, columns), (9, tiles, columns // 2)]
    scratch = [window, window, (3, wide // 2, tiles, columns)]
    args = [counts, extended, *both_swapped(inner, outer), faces]
    middle, packed, nxt, *fixed = call(second_kernel, outs + [window] * 4, args, scratch, 1)

    def again(given):
        packed = given[1]
        x_left = shifted(packed[-2:], "group", 1)
        x_right = shifted(packed[:2], "group", -1)
        extended = jnp.concatenate([x_left, packed, x_right], 0)
        args = [counts, extended, *both_swapped(extended, extended), *fixed]
        return list(call(second_again_kernel, outs, args, scratch, 1))

    done = lax.cond(count > 2, again, lambda given: given, [middle, packed, nxt])
    return done[0], done[2]


def third_prepare_kernel(*refs):
    blocks, out = refs[:-1], refs[-1]
    count = len(blocks)
    rows, columns = blocks[0].shape[1:]
    row = iota((rows, columns), 0)
    for b in range(count):
        span = pl.ds(pl.multiple_of(((lax.axis_index("group") + b) % count) * rows, rows), rows)
        before, after = blocks[b - 1][8], blocks[(b + 1) % count][8]
        for at in range(8):
            value = blocks[b][at]
            if at in (2, 3):
                high = before[2 * (at - 2) : 2 * (at - 2) + 1]
                low = after[rows // 2 + 2 * (at - 2) : rows // 2 + 2 * (at - 2) + 1]
                value = value + jnp.where(row == 0, high, 0.0) + jnp.where(row == rows - 1, low, 0.0)
            out[at, span] = value


FIELD, DEFECT, MASS, FACE = 0, 4, 7, 10


def third_chip_kernel(own, other, chip, rest):
    edge = my_core()
    for at, start in enumerate((FIELD, DEFECT, MASS)):
        values = [own[2 * at + edge], own[2 * at + 1 - edge], other[2 * at + edge], other[2 * at + 1 - edge]]
        if at == 1:
            values[1] = values[1] + other[6 + edge]
            values[2] = values[2] + own[7 - edge]
        for k in range(4 if at == 0 else 3):
            chip[start + k] = values[k]
        if at > 0:
            rest[at - 1] = values[3]
    chip[FACE] = own[6 + edge]
    rest[2] = other[7 - edge]


def third_finish(count, field, mass, source, coarse, packed, message, tall, held, sent):
    rows, columns = field[0].shape[1:]
    core = my_core()
    is_odd = odd((rows, columns), plus=core)
    two_sweeps(count, field, mass, source, 6, core)
    red, black = field[0][2], field[1][2]
    one, two = jnp.where(is_odd, black, red), jnp.where(is_odd, red, black)
    for colour in range(2):
        for k in range(2):
            packed[2 * colour + k] = field[colour][2 + k]
    tall[:rows] = jnp.where(core == 0, one, two)
    tall[rows : 2 * rows] = jnp.where(core == 0, two, one)
    for r in range(rows):
        held[2 * r : 2 * r + 1] = tall[r : r + 1]
        held[2 * r + 1 : 2 * r + 2] = tall[rows + r : rows + r + 1]
    copy = pltpu.make_async_copy(held, coarse, sent)

    @pl.when(count <= 2)
    def _():
        copy.start()
        totals = []
        for q in (2, 3):
            total = jnp.zeros((rows, columns), jnp.float32)
            for colour in range(2):
                other = field[1 - colour]
                beyond = inner_only(is_odd, other[5 - q], q, colour)
                around = other[q] + beyond + both_ways(other[q], 0) + both_ways(other[q], 1)
                total = total + residual(around, field[colour][q], mass[colour][q], source[colour][q])
            totals.append(total * 0.5)
        red, black = field[0][3], field[1][3]
        last = jnp.where(is_odd, red, black)
        pieces = [(field[0][q] + field[1][q]) * 0.125 for q in (2, 3)] + totals
        pieces += [(mass[0][q] + mass[1][q]) * 0.5 for q in (2, 3)] + [one * 0.5, last * 0.5]
        tall[...] = pooled(jnp.concatenate(pieces, 0), pool_matrix(columns, columns))
        half = rows // 2
        narrow = tall[pl.ds(0, 8 * half, stride=2)] + tall[pl.ds(1, 8 * half, stride=2)]
        lane = iota((half, columns), 1) // (columns // 2)
        lower = lane == core
        is_odd_half = odd((half, columns))
        even_row = same_row((half, columns))

        def narrow_of(k):
            return narrow[k * half : (k + 1) * half]

        tiles = []
        for at in range(3):
            tile = jnp.where(lower, narrow_of(2 * at), narrow_of(2 * at + 1))
            tiles.append(jnp.where(is_odd_half, roll(tile, columns // 2, 1), tile))
        low_face = jnp.where(core == 0, narrow_of(6), narrow_of(7))
        high_face = jnp.where(core == 0, narrow_of(7), narrow_of(6))
        tiles.append(jnp.where(even_row, high_face, low_face))
        for at in range(2):
            tile = jnp.where(core == 0, tiles[at], tiles[2 + at])
            tile = jnp.where(lax.axis_index("brick") < message.shape[0], tile, roll(tile, columns // 2, 1))
            for c in range(message.shape[0]):
                message[c, at] = tile
        copy.wait()


def same_row(shape):
    half = shape[1] // 2
    lane = iota(shape, 1)
    return ((iota(shape, 0) + lane + lane // half) & 1) == 0


def inner_only(is_odd, inner, q, colour):
    above = is_odd if colour == 0 else jnp.logical_not(is_odd)
    return jnp.where(above, inner, 0.0) if q == 2 else jnp.where(above, 0.0, inner)


def pack_pair(window, at, even, next_one, is_odd):
    window[0][at] = jnp.where(is_odd, next_one, even)
    window[1][at] = jnp.where(is_odd, even, next_one)


def third_kernel(counts, chip, inner, near, far, coarse, packed, message, *rest):
    mass, source, field, rest = rest[0:2], rest[2:4], rest[4:6], rest[6:]
    rows, columns = chip.shape[1:]
    is_odd = odd((rows, columns), plus=my_core())
    for at, (window, start) in enumerate(((field, FIELD), (source, DEFECT), (mass, MASS))):
        side, own, beyond = ([part[start + min(k, 3 if at == 0 else 2)] for k in range(4)] for part in (near, chip, far))
        if at > 0:
            own[3] = inner[at - 1]
        if at == 1:
            side[0] = side[0] + chip[FACE]
            own[0] = own[0] + near[FACE]
            own[3] = own[3] + far[FACE]
            beyond[0] = beyond[0] + inner[2]
        line = side[::-1] + own + beyond
        for q in range(6):
            pack_pair(window, q, line[2 * q], line[2 * q + 1], is_odd)
    source_from_defect(field, mass, source, plus=my_core())
    third_finish(count_of(counts, 2), field, mass, source, coarse, packed, message, *rest)


def third_again_kernel(counts, chip, near, far, *rest):
    mass, source = rest[0:2], rest[2:4]
    coarse, packed, message, *rest = rest[4:]
    field, rest = rest[:2], rest[2:]
    for colour in range(2):
        for k in range(2):
            field[colour][1 - k] = near[2 * colour + k]
            field[colour][2 + k] = chip[2 * colour + k]
            field[colour][4 + k] = far[2 * colour + k]
    third_finish(count_of(counts, 2) - 2, field, mass, source, coarse, packed, message, *rest)


def third_level(part, count, counts):
    groups, chips = lax.axis_size("group"), lax.axis_size("brick") // 2
    tile_rows, columns = part.shape[1:]
    rows = groups * tile_rows
    blocks = [part] + [shifted(part, "group", -d) for d in range(1, groups)]
    (own,) = call(third_prepare_kernel, [(8, rows, columns)], blocks)
    shapes = [(11, rows, columns), (3, rows, columns)]
    chip, inner = call(third_chip_kernel, shapes, [own, swapped_cores(own)])
    near = swapped_chips(chip)
    far = swapped_cores(near)
    window = (6, rows, columns)
    outs = [(2 * rows, columns), (4, rows, columns), (chips, 2, rows // 2, columns)]
    scratch = [window, window, (8 * rows, columns)]
    args = [counts, chip, inner, near, far]
    coarse, packed, message, *fixed = call(third_kernel, outs + [window] * 4, args, scratch, 1)

    def again(given):
        packed = given[1]
        near = swapped_chips(packed)
        args = [counts, packed, near, swapped_cores(near), *fixed]
        return list(call(third_again_kernel, outs, args, scratch, 1))

    done = lax.cond(count > 2, again, lambda given: given, [coarse, packed, message])
    return done[0].reshape(rows, 2, columns), done[2]


def fourth_kernel(counts, own, other, out, *windows):
    field, mass, source, (held, sent) = windows[0:2], windows[2:4], windows[4:6], windows[6:]
    chips, _, rows, columns = own.shape
    tiles, half = chips // 2, columns // 2
    lane = iota((rows, columns), 1)
    low = lane < half
    is_odd = odd((rows, columns))
    first, last = lane % half == 0, lane % half == half - 1

    def turned(value):
        return roll(value, half, 1)

    def beside(value):
        after = jnp.where(last, roll(value, half - 1, 1), roll(value, -1, 1))
        return after + jnp.where(first, roll(value, 1 - half, 1), roll(value, 1, 1))

    def put(window, t, one, two):
        window[0][t + 1] = jnp.where(low, one, two)
        window[1][t + 1] = turned(jnp.where(low, two, one))

    def repeat(window, colour):
        window[colour][0] = turned(window[colour][tiles])
        window[colour][tiles + 1] = turned(window[colour][1])

    def load(one, two):
        even_row = same_row((rows, columns))

        def defect(t):
            before, after = two[(t - 1) % chips, 1], two[(t + 1) % chips, 1]
            before = turned(before) if t in (0, tiles) else before
            after = turned(after) if t in (tiles - 1, chips - 1) else after
            if t < tiles:
                return one[t, 1] + jnp.where(even_row, before, after)
            return one[t, 1] + jnp.where(even_row, after, before)

        for t in range(tiles):
            put(field, t, one[t, 0], one[t + tiles, 0])
            put(mass, t, two[t, 0], two[t + tiles, 0])
            put(source, t, defect(t), defect(t + tiles))

    @pl.when(my_core() == 0)
    def _():
        load(own, other)

    @pl.when(my_core() == 1)
    def _():
        load(other, own)

    for colour in range(2):
        repeat(field, colour)
    source_from_defect(field, mass, source, beside, range(1, tiles + 1))

    def one_sweep(step, carry):
        for colour in range(2):
            half_sweep(field, mass, source, colour, 1, tiles + 1, 16, beside)
            repeat(field, colour)
        return carry

    lax.fori_loop(0, count_of(counts, 3), one_sweep, 0)
    for t in range(tiles):
        red, black = field[0][t + 1], field[1][t + 1]
        red_too, black_too = turned(red), turned(black)
        one = jnp.where(low, jnp.where(is_odd, black, red), jnp.where(is_odd, red_too, black_too))
        two = jnp.where(low, jnp.where(is_odd, black_too, red_too), jnp.where(is_odd, red, black))
        for at, value in ((t, one), (t + tiles, two)):
            held[:, at * columns : (at + 1) * columns] = value
    copy = pltpu.make_async_copy(held, out, sent)
    copy.start()
    copy.wait()


def fourth_level(message, counts):
    chips, _, rows, columns = message.shape
    cores = [[2 * chip + c for chip in range(chips)] for c in range(2)]
    own = lax.all_to_all(message, "brick", 0, 0, axis_index_groups=cores)
    other = swapped_cores(own)
    scratch = [(chips // 2 + 2, rows, columns)] * 6
    (out,) = call(fourth_kernel, [(rows, chips * columns)], [counts, own, other], scratch, 1)
    return out


def on_device(initial_field, mass, source, sweeps):
    counts, (fine, parts, edge_left, edge_right) = first_level(initial_field, mass, source, sweeps)
    middle, part = second_level(parts, edge_left, edge_right, sweeps[1], counts)
    coarse, message = third_level(part, sweeps[2], counts)
    coarsest = fourth_level(message, counts)
    return fine, middle, coarse, coarsest


def solution(mesh):
    return jax.shard_map(
        on_device,
        mesh=mesh,
        in_specs=(
            P("group", "brick", None),
            P("group", "brick", None),
            P("group", "brick", None),
            P(),
        ),
        out_specs=(
            P("group", "brick", None),
            P("group", "brick", None),
            P(None, "brick", None),
            P(),
        ),
        check_vma=False,
    )
```

```python
import functools

import jax
import jax.numpy as jnp
from jax import lax
from jax.experimental import pallas as pl
from jax.experimental.pallas import tpu as pltpu
from jax.sharding import PartitionSpec as P


INTERPRET = False
MIB = 1024 * 1024
LANES = 128


def call(kernel, out_shapes, args, scratch=(), results=0, limit=12 * MIB):
    spec = pl.BlockSpec(memory_space=pltpu.VMEM)
    return pl.pallas_call(
        kernel,
        out_shape=[
            (pltpu.HBM if at < results else pltpu.VMEM)(shape, jnp.float32) for at, shape in enumerate(out_shapes)
        ],
        in_specs=[spec] * len(args),
        out_specs=[pl.BlockSpec(memory_space=pltpu.HBM)] * results + [spec] * (len(out_shapes) - results),
        scratch_shapes=[pltpu.VMEM(shape, jnp.float32) for shape in [*scratch, *out_shapes[:results]]]
        + [pltpu.SemaphoreType.DMA] * results,
        compiler_params=pltpu.CompilerParams(vmem_limit_bytes=limit),
        interpret=INTERPRET,
    )(*args)


def iota(shape, axis):
    return lax.broadcasted_iota(jnp.int32, shape, axis)


def odd(shape, period=None, plus=0):
    rows = iota(shape, 0)
    if period is not None:
        rows = rows % period
    return ((rows + iota(shape, 1) + plus) & 1) == 1


def same_member(shape, quarter):
    rows = iota(shape, 0)
    return ((rows % quarter + rows // quarter + iota(shape, 1)) & 1) == 0


def roll(value, shift, axis):
    return pltpu.roll(value, shift % value.shape[axis], axis)


def both_ways(value, axis):
    return roll(value, 1, axis) + roll(value, -1, axis)


def newton(around, value, mass, source):
    curve = mass * (value * value)
    over = (around + source) + 2.0 * (curve * value)
    under = (6.0 + mass) + 3.0 * curve
    guess = pl.reciprocal(under, approx=True)
    guess = guess * (2.0 - under * guess)
    return over * guess


def residual(around, value, mass, source):
    return (around - 6.0 * value) - mass * (value * value * value + value) + source


def pooled(rows, pool):
    high = rows.astype(jnp.bfloat16)
    rest = rows - high.astype(jnp.float32)
    middle = rest.astype(jnp.bfloat16)
    low = (rest - middle.astype(jnp.float32)).astype(jnp.bfloat16)
    dot = functools.partial(jnp.dot, preferred_element_type=jnp.float32)
    return dot(high, pool) + (dot(middle, pool) + dot(low, pool))


def pool_matrix(width, columns):
    half = width // 2
    shape = (width, columns)
    return jnp.where(iota(shape, 0) // 2 == iota(shape, 1) % half, 1.0, 0.0).astype(jnp.bfloat16)


def half_sweep(field, mass, source, colour, low, high, most, beside=None, plus=0):
    mine, other = field[colour], field[1 - colour]
    limit, rows, columns = mine.shape
    is_odd = odd((rows, columns), plus=plus)
    beside = beside or (lambda value: both_ways(value, 1))
    together = max(k for k in range(1, most + 1) if (high - low) % k == 0)

    def step(turn, carry):
        start = low + turn * together
        near = [other[jnp.clip(start + k, 0, limit - 1)] for k in range(-1, together + 1)]
        fresh = []
        for k in range(together):
            first, second = (near[k], near[k + 2]) if colour == 0 else (near[k + 2], near[k])
            around = near[k + 1] + jnp.where(is_odd, second, first)
            around = around + both_ways(near[k + 1], 0) + beside(near[k + 1])
            fresh.append(newton(around, mine[start + k], mass[colour][start + k], source[colour][start + k]))
        for k in range(together):
            mine[start + k] = fresh[k]
        return carry

    turns = (high - low) // together
    if turns == 1:
        step(0, 0)
    else:
        lax.fori_loop(0, turns, step, 0)


def two_sweeps(count, field, mass, source, most, plus=0):
    limit = field[0].shape[0]
    half_sweep(field, mass, source, 0, 0, limit, most, plus=plus)
    half_sweep(field, mass, source, 1, 1, limit - 1, most, plus=plus)

    @pl.when(count >= 2)
    def _():
        half_sweep(field, mass, source, 0, 1, limit - 1, most, plus=plus)
        half_sweep(field, mass, source, 1, 2, limit - 2, most, plus=plus)


def source_from_defect(field, mass, source, beside=None, inner=None, plus=0):
    limit, rows, columns = field[0].shape
    is_odd = odd((rows, columns), plus=plus)
    beside = beside or (lambda value: both_ways(value, 1))
    for index in inner or range(limit):
        for colour in range(2):
            other = field[1 - colour]
            first, second = other[max(index - 1, 0)], other[min(index + 1, limit - 1)]
            if colour == 1:
                first, second = second, first
            around = other[index] + jnp.where(is_odd, second, first)
            around = around + both_ways(other[index], 0) + beside(other[index])
            source[colour][index] = source[colour][index] - residual(
                around, field[colour][index], mass[colour][index], 0.0
            )


def shifted(value, axis, by):
    count = lax.axis_size(axis)
    return lax.ppermute(value, axis, [(i, (i + by) % count) for i in range(count)])


def swapped_cores(value):
    count = lax.axis_size("brick")
    return lax.ppermute(value, "brick", [(i, i ^ 1) for i in range(count)])


def swapped_chips(value):
    count = lax.axis_size("brick")
    return lax.ppermute(value, "brick", [(i, (i + 1 if i % 2 else i - 1) % count) for i in range(count)])


def both_swapped(inner, outer):
    far = swapped_chips(outer)
    return far, swapped_cores(inner)


def sides(core, outer, inner):
    on_first = jnp.broadcast_to(core, outer.shape) == 0
    return jnp.where(on_first, outer, inner), jnp.where(on_first, inner, outer)


def my_core():
    return lax.axis_index("brick") & 1


def count_of(counts, level):
    return jnp.max(counts[level])


def kept_pairs(pairs):
    quarter = pairs // 4
    kept = list(range(quarter)) + list(range(pairs - quarter, pairs))
    return kept, list(range(quarter, pairs - quarter))


def ride_right(row, mass, source, rider):
    mass = jnp.where(row < 2, roll(rider, -2, 0), jnp.where(row == 4, roll(rider, -1, 0), mass))
    return mass, jnp.where(row < 2, roll(rider, 2, 0), source)


def ride_left(row, mass, source, rider):
    mass = jnp.where(row > 5, roll(rider, 2, 0), jnp.where(row == 3, roll(rider, 1, 0), mass))
    return mass, jnp.where(row > 5, roll(rider, -2, 0), source)


def rider_from_left(row, mass, source):
    return jnp.where(row < 4, roll(mass, 2, 0), jnp.where(row == 5, roll(mass, 1, 0), roll(source, -2, 0)))


def rider_from_right(row, mass, source):
    return jnp.where(row < 2, roll(source, 2, 0), jnp.where(row == 2, roll(mass, -1, 0), roll(mass, -2, 0)))


def pack_kernel(*refs):
    sweeps, *blocks = refs[:4]
    own, outer, inner, edge_left, edge_right, counts, *ahead = refs[4:13]
    held, arrived, few, few_arrived, sent, *singles = refs[13:]
    count = len(blocks)
    core = my_core()
    pairs = own.shape[2]
    rows, columns = own.shape[3:]
    is_odd = odd((rows, columns))
    row = iota((rows, columns), 0)
    upper = row < rows // 2
    parts = arrived.shape[1]
    some = 2 * pairs // parts

    def part_of(at, part):
        span = pl.ds(some * part, some)
        return pltpu.make_async_copy(blocks[at].at[span], held.at[at, span], arrived.at[at, part])

    def packed(at, pair):
        even, next_one = held[at, 2 * pair], held[at, 2 * pair + 1]
        red = jnp.where(is_odd, next_one, even)
        black = jnp.where(is_odd, even, next_one)
        own[at, 0, pair] = red
        own[at, 1, pair] = black
        if pair < 2:
            edge_left[at, 0, pair] = red
            edge_left[at, 1, pair] = black
        if pair >= pairs - 2:
            edge_right[at, 0, pair - pairs + 2] = red
            edge_right[at, 1, pair - pairs + 2] = black
        turned = roll(black, rows // 2, 0)
        return jnp.where(upper, red, turned), jnp.where(upper, turned, red)

    for at in range(count):
        for part in range(parts):
            part_of(at, part).start()
    copy = pltpu.make_async_copy(sweeps, few, few_arrived)
    copy.start()
    copy.wait()
    alone = []
    for level, (single, out) in enumerate(zip(singles, ahead)):
        single[0] = few[level]
        alone.append(pltpu.make_async_copy(single, out, sent.at[level]))
        alone[-1].start()
    for level in range(4):
        counts[level] = jnp.full(counts.shape[1:], few[level])
    for part in range(parts):
        part_of(0, part).wait()
        for pair in range(some // 2 * part, some // 2 * (part + 1)):
            outer[pair], inner[pair] = sides(core, *packed(0, pair))
    for at in (1, 2):
        for part in range(parts):
            part_of(at, part).wait()
    kept, riders = kept_pairs(pairs)
    half = pairs // 2
    for k, (pair, other) in enumerate(zip(kept, riders)):
        mass, source = packed(1, pair), packed(2, pair)
        other_mass, rider = packed(1, other), packed(2, other)
        left = ride_left(row, mass[0], source[0], rider[0])
        right = ride_right(row, mass[1], source[1], rider[1])
        places = (pairs + k, pairs + half + k, 2 * pairs + k)
        for place, one, two in zip(places, (*left, other_mass[0]), (*right, other_mass[1])):
            outer[place], inner[place] = sides(core, one, two)
    for copy in alone:
        copy.wait()


def corner_kernel(y_outer, y_inner, to_left, to_right):
    core = my_core()
    tiles, rows, columns = y_outer.shape
    pairs = tiles if to_left.shape[0] == 3 else tiles * 2 // 5
    from_right = iota((rows, columns), 0) % (rows // 2) < rows // 4
    for out, near, far, kept in ((to_left, 0, 1, 0), (to_right, pairs - 1, pairs - 2, pairs // 2 - 1)):
        out[0], out[1] = sides(core, y_outer[near], y_inner[near])
        both = [far] if out.shape[0] == 3 else [far, pairs + kept, pairs + pairs // 2 + kept]
        for k, at in enumerate(both):
            left, right = sides(core, y_outer[at], y_inner[at])
            out[2 + k] = jnp.where(from_right, right, left)


def pack_shapes(count, pairs, tile):
    shapes = [(count, 2, pairs, *tile)] + [(pairs if count == 1 else pairs * 5 // 2, *tile)] * 2
    return shapes + [(count, 2, 2, *tile)] * 2


def packed_blocks(sweeps, blocks):
    count = len(blocks)
    rows, *tile = blocks[0].shape
    shapes = pack_shapes(count, rows // 2, tile)
    return pl.pallas_call(
        pack_kernel,
        out_shape=[pltpu.VMEM(shape, jnp.float32) for shape in shapes] + [pltpu.VMEM((4, 8, LANES), jnp.int32)]
        + [pltpu.HBM((1,), jnp.int32)] * 3,
        in_specs=[pl.BlockSpec(memory_space=pltpu.HBM)] * (1 + count),
        out_specs=[pl.BlockSpec(memory_space=pltpu.VMEM)] * (len(shapes) + 1)
        + [pl.BlockSpec(memory_space=pltpu.HBM)] * 3,
        scratch_shapes=[
            pltpu.VMEM((count, rows, *tile), jnp.float32),
            pltpu.SemaphoreType.DMA((count, 4)),
            pltpu.SMEM((4,), jnp.int32),
            pltpu.SemaphoreType.DMA,
            pltpu.SemaphoreType.DMA((3,)),
            *[pltpu.SMEM((1,), jnp.int32)] * 3,
        ],
        compiler_params=pltpu.CompilerParams(vmem_limit_bytes=12 * MIB),
    )(*[pltpu.with_memory_space_constraint(value, pltpu.HBM) for value in (sweeps, *blocks)])


def first_exchange(own, outer, inner, edge_left, edge_right):
    count, tile = own.shape[0], own.shape[3:]
    y_outer, y_inner = both_swapped(inner, outer)
    x_left = shifted(edge_right, "group", 1)
    x_right = shifted(edge_left, "group", -1)
    corners = call(corner_kernel, [(3 if count == 1 else 5, *tile)] * 2, [y_outer, y_inner])
    c_left = shifted(corners[1], "group", 1)
    c_right = shifted(corners[0], "group", -1)
    return own, x_left, x_right, y_outer, y_inner, c_left, c_right


def put_first(window, to, red, black, from_left, from_right):
    wide = red.shape[0]
    upper = iota(red.shape, 0) < wide // 2
    window[0][to, :wide] = red
    window[0][to, wide:] = jnp.where(upper, from_right, from_left)
    window[1][to, :wide] = black
    window[1][to, wide:] = roll(jnp.where(upper, from_left, from_right), wide // 2, 0)


def assemble_own(window, at, own, y_outer, y_inner):
    pairs, wide, columns = own.shape[2:]
    row = iota((wide, columns), 0)
    kept, riders = kept_pairs(pairs)
    core = my_core()

    def beside(place):
        return sides(core, y_outer[place], y_inner[place])

    for pair in range(pairs):
        if at == 0:
            left, right = beside(pair)
        elif pair in kept:
            left, right = beside(pairs + (at - 1) * (pairs // 2) + kept.index(pair))
        elif at == 1:
            left, right = beside(2 * pairs + riders.index(pair))
        else:
            (left, right), other = beside(pairs + riders.index(pair)), beside(pairs + pairs // 2 + riders.index(pair))
            left, right = rider_from_left(row, left, other[0]), rider_from_right(row, right, other[1])
        put_first(window, pair, own[at, 0, pair], own[at, 1, pair], left, right)


def assemble_edges(window, at, places, x_left, x_right, c_left, c_right):
    for side, x_side, corner in ((0, x_left, c_left), (1, x_right, c_right)):
        for k in range(2):
            if at == 0:
                near = k != side
                left, right = (corner[0], corner[1]) if near else (corner[2], corner[2])
            else:
                left = right = corner[2 + at]
            put_first(window, places[2 * side + k], x_side[at, 0, k], x_side[at, 1, k], left, right)


def inner_sweeps(count, field, mass, source):
    pairs = field[0].shape[0]

    def half(colour, less):
        whole = (pairs - 2 * less) // 4 * 4
        half_sweep(field, mass, source, colour, less, less + whole, 4)
        if whole < pairs - 2 * less:
            half_sweep(field, mass, source, colour, less + whole, pairs - less, 4)

    half(0, 1)
    half(1, 2)

    @pl.when(count >= 2)
    def _():
        half(0, 3)
        half(1, 4)


def edge_sweeps(count, field, mass_of, source_of):
    limit, rows, columns = field[0].shape
    is_odd = odd((rows, columns))

    def some(colour, positions):
        mine, other = field[colour], field[1 - colour]
        fresh = []
        for w in positions:
            first, second = other[max(w - 1, 0)], other[min(w + 1, limit - 1)]
            if colour == 1:
                first, second = second, first
            value = other[w]
            around = value + jnp.where(is_odd, second, first) + both_ways(value, 0) + both_ways(value, 1)
            fresh.append(newton(around, mine[w], mass_of(colour, w), source_of(colour, w)))
        for w, value in zip(positions, fresh):
            mine[w] = value

    def half(colour, low, high):
        some(colour, range(low, high))
        some(colour, range(limit - high, limit - low))

    half(0, 0, 3)
    half(1, 1, 4)

    @pl.when(count >= 2)
    def _():
        half(0, 1, 5)
        half(1, 2, 6)


def first_inner_kernel(counts, own, y_outer, y_inner, *windows):
    field, mass, source = windows[:2], windows[2:4], windows[4:]
    for at, window in enumerate((field, mass, source)):
        assemble_own(window, at, own, y_outer, y_inner)
    inner_sweeps(count_of(counts, 0), field, mass, source)


def first_inner_again_kernel(counts, own, y_outer, y_inner, *windows):
    mass, source, field = windows[:2], windows[2:4], windows[4:]
    assemble_own(field, 0, own, y_outer, y_inner)
    inner_sweeps(count_of(counts, 0) - 2, field, mass, source)


def first_outer(count, halo, inner, mass, source, edges, field):
    pairs = inner[0].shape[0]
    for colour in range(2):
        for pair in range(pairs):
            field[colour][pair + 2] = inner[colour][pair]
    assemble_edges(field, 0, (0, 1, pairs + 2, pairs + 3), *halo)

    def of(whole, beyond):
        def at(colour, w):
            if 2 <= w < pairs + 2:
                return whole[colour][w - 2]
            return beyond[colour][w if w < 2 else w - pairs]

        return at

    edge_sweeps(count, field, of(mass, edges[:2]), of(source, edges[2:]))


def first_kernel(counts, *refs):
    halo, inner, mass, source, refs = refs[:4], refs[4:6], refs[6:8], refs[8:10], refs[10:]
    outs, again, edges, field, rest = refs[:4], refs[4:9], refs[9:13], refs[13:15], refs[15:]
    for at, window in ((1, edges[:2]), (2, edges[2:])):
        assemble_edges(window, at, range(4), *halo)
    count = count_of(counts, 0)
    first_outer(count, halo, inner, mass, source, edges, field)
    first_finish(count, field, mass, source, outs, again, *rest)


def first_again_kernel(counts, *refs):
    halo, inner, mass, source, edges, refs = refs[:4], refs[4:6], refs[6:8], refs[8:10], refs[10:14], refs[14:]
    outs, field, rest = refs[:4], refs[4:6], refs[6:]
    count = count_of(counts, 0) - 2
    first_outer(count, halo, inner, mass, source, edges, field)
    first_finish(count, field, mass, source, outs, None, *rest)


def first_finish(count, field, mass, source, outs, again, tall, held, sent):
    fine, nxt, edge_left, edge_right = outs
    limit, rows, columns = field[0].shape
    pairs, wide = limit - 4, rows // 2
    is_odd = odd((wide, columns))
    row = iota((wide, columns), 0)
    top, bottom = row == 0, row == wide - 1
    copy = pltpu.make_async_copy(held, fine, sent)

    if again is not None:

        @pl.when(count > 2)
        def _():
            own, outer, inner, *edges = again
            upper = row < wide // 2
            for pair in range(pairs):
                red, black = field[0][pair + 2, :wide], field[1][pair + 2, :wide]
                own[0, 0, pair] = red
                own[0, 1, pair] = black
                turned = roll(black, wide // 2, 0)
                outer[pair], inner[pair] = sides(
                    my_core(), jnp.where(upper, red, turned), jnp.where(upper, turned, red)
                )
                for edge, first in zip(edges, (0, pairs - 2)):
                    if first <= pair < first + 2:
                        edge[0, 0, pair - first] = red
                        edge[0, 1, pair - first] = black

    def keep(index, value):
        for c in range(columns // LANES):
            tall[c, index] = value[:, c * LANES : (c + 1) * LANES]

    @pl.when(count <= 2)
    def _():
        for pair in range(pairs):
            red, black = field[0][pair + 2, :wide], field[1][pair + 2, :wide]
            held[2 * pair] = jnp.where(is_odd, black, red)
            held[2 * pair + 1] = jnp.where(is_odd, red, black)
        copy.start()

        def step(pair, carry):
            total = jnp.zeros((wide, columns), jnp.float32)
            for colour in range(2):
                other = field[1 - colour][pair + 2, :wide]
                first = jnp.where(pair == 0, 0.0, field[1 - colour][pair + 1, :wide])
                second = jnp.where(pair == pairs - 1, 0.0, field[1 - colour][pair + 3, :wide])
                if colour == 1:
                    first, second = second, first
                around = other + jnp.where(is_odd, second, first) + both_ways(other, 1)
                around = around + jnp.where(bottom, 0.0, roll(other, -1, 0))
                around = around + jnp.where(top, 0.0, roll(other, 1, 0))
                at, own = (pair + 2, slice(0, wide)), (pair, slice(0, wide))
                total = total + residual(around, field[colour][at], mass[colour][own], source[colour][own])
            keep(pair, field[0][at] + field[1][at])
            keep(pairs + pair, total)
            keep(2 * pairs + pair, mass[0][own] + mass[1][own])
            return carry

        lax.fori_loop(0, pairs, step, 0, unroll=2)
        low = jnp.where(is_odd, field[1][2, :wide], field[0][2, :wide])
        high = jnp.where(is_odd, field[0][pairs + 1, :wide], field[1][pairs + 1, :wide])
        half, tiles, quarter = columns // 2, pairs // 2, wide // 2
        keep(3 * pairs, high)
        keep(3 * pairs + 1, low)
        lines = (3 * pairs + 2) * wide // 2
        flat = tall.reshape(columns // LANES, 2 * lines, LANES)

        def every_other(start):
            parts = [flat[c, pl.ds(start, lines, stride=2)] for c in range(columns // LANES)]
            return jnp.concatenate(parts, 1)

        firsts, seconds = every_other(0), every_other(1)
        whole = (iota((wide, columns), 0)) % quarter
        y_faces = []
        for t in range(tiles):
            last, head = seconds[t * wide : (t + 1) * wide], firsts[t * wide : (t + 1) * wide]
            y_faces.append(
                jnp.where(
                    whole == 0,
                    roll(last, quarter + 1, 0),
                    jnp.where(whole == quarter - 1, roll(head, quarter - 1, 0), 0.0),
                )
            )
        narrow = pooled(jnp.concatenate([firsts + seconds] + y_faces, 0), pool_matrix(columns, half))
        is_odd_half = odd((wide, half), quarter)
        is_even = same_member((wide, half), quarter)

        def packed(index, factor):
            tile = narrow[index * wide : (index + 1) * wide] * factor
            return jnp.where(is_odd_half, roll(tile, quarter, 0), tile)

        face_x = packed(3 * tiles, 0.5)
        for t in range(tiles):
            values = [
                packed(t, 0.125),
                packed(tiles + t, 0.5),
                packed(2 * tiles + t, 0.5),
                packed(3 * tiles + 1 + t, 0.5),
            ]
            for at, value in enumerate(values):
                nxt[at, t] = value
                if t < 2:
                    if at == 1 and t == 1:
                        value = jnp.where(is_even, value, face_x)
                    edge_left[at, t] = value
                if t >= tiles - 2:
                    if at == 1 and t == tiles - 2:
                        value = jnp.where(is_even, face_x, value)
                    edge_right[at, t - tiles + 2] = value
        nxt[4, 0] = face_x
        for t in range(1, tiles):
            nxt[4, t] = jnp.zeros((wide, half), jnp.float32)
        copy.wait()


def first_level(field, mass, source, sweeps):
    rows, wide, columns = field.shape
    pairs = rows // 2
    half, tiles = columns // 2, pairs // 2
    window = (pairs + 4, 2 * wide, columns)
    outs = [
        (rows, wide, columns),
        (5, tiles, wide, half),
        (4, 2, wide, half),
        (4, 2, wide, half),
    ]

    inner, edge = (pairs, 2 * wide, columns), (4, 2 * wide, columns)
    scratch = [window, window, (columns // LANES, 3 * pairs + 2, wide, LANES)]
    *packed, counts, first, second, third = packed_blocks(sweeps, [field, mass, source])
    ahead = [first, second, third]
    own, x_left, x_right, y_outer, y_inner, c_left, c_right = first_exchange(*packed)
    windows = call(first_inner_kernel, [inner] * 6, [counts, own, y_outer, y_inner])
    every = outs + pack_shapes(1, pairs, (wide, columns)) + [edge] * 4
    args = [counts, x_left, x_right, c_left, c_right, *windows]
    results = call(first_kernel, every, args, scratch, 1, 20 * MIB)
    once, more, edges = results[:4], results[4:9], results[9:]

    def again(given):
        own, x_left, x_right, y_outer, y_inner, c_left, c_right = first_exchange(*more)
        fixed = windows[2:]
        field = call(first_inner_again_kernel, [inner] * 2, [counts, own, y_outer, y_inner, *fixed])
        args = [counts, x_left, x_right, c_left, c_right, *field, *fixed, *edges]
        return list(call(first_again_kernel, outs, args, scratch, 1, 20 * MIB))

    return counts, ahead, lax.cond(ahead[0][0] > 2, again, lambda given: given, list(once))


def sent_place(at, t, limit):
    return at * limit + t if at < 2 else 2 * limit + min(max(t - 1, 0), limit - 3)


def second_prepare_kernel(own, x_left, x_right, extended, outer, inner, faces):
    tiles, wide, columns = own.shape[1:]
    quarter = wide // 2
    row_of = iota((wide, columns), 0) % quarter
    is_even = same_member((wide, columns), quarter)
    face_x = own[4, 0]
    for t in range(tiles + 4):
        if t < 2:
            source, k = x_left, t
        elif t < tiles + 2:
            source, k = own, t - 2
        else:
            source, k = x_right, t - tiles - 2
        defect = source[1, k]
        if t == 1:
            defect = defect + jnp.where(is_even, 0.0, face_x)
        if t == 2:
            defect = defect + jnp.where(is_even, x_left[1, 0], 0.0)
        if t == tiles + 1:
            defect = defect + jnp.where(is_even, 0.0, x_right[1, 1])
        if t == tiles + 2:
            defect = defect + jnp.where(is_even, face_x, 0.0)
        face_y = source[3, k]
        faces[t] = face_y
        for at in range(3):
            value = defect if at == 1 else source[at, k]
            extended[at, t] = value
            left = jnp.where(row_of == quarter - 1, face_y, value) if at == 1 else value
            right = jnp.where(row_of == 0, face_y, value) if at == 1 else value
            if at == 0:
                outer[t] = inner[t] = value
            elif at == 1 or 0 < t < tiles + 3:
                place = sent_place(at, t, tiles + 4)
                outer[place], inner[place] = sides(my_core(), left, right)


def assemble_second(window, to, tile, left, right):
    wide = tile.shape[0]
    quarter = wide // 2
    upper = iota(tile.shape, 0) < quarter
    window[0][to, :wide] = jnp.where(upper, tile, roll(right, quarter, 0))
    window[0][to, wide:] = roll(left, quarter, 0)
    window[1][to, :wide] = jnp.where(upper, roll(tile, quarter, 0), right)
    window[1][to, wide:] = left


def second_finish(count, field, mass, source, middle, packed, nxt, tall, held, sent):
    limit, rows, columns = field[0].shape
    pairs = limit - 4
    wide = rows // 2
    quarter = wide // 2
    two_sweeps(count, field, mass, source, 6)
    is_odd = odd((wide, columns), quarter)
    row = iota((wide, columns), 0)
    upper = row < quarter
    top, bottom = row == 0, row == quarter - 1
    for pair in range(pairs):
        red, black = field[0][pair + 2, :wide], field[1][pair + 2, :wide]
        tile = jnp.where(upper, red, roll(black, quarter, 0))
        packed[pair] = tile
        plain = jnp.where(is_odd, roll(tile, quarter, 0), tile)
        held[2 * pair] = plain[:quarter]
        held[2 * pair + 1] = plain[quarter:]
    copy = pltpu.make_async_copy(held, middle, sent)

    @pl.when(count <= 2)
    def _():
        copy.start()
        for pair in range(pairs):
            total = jnp.zeros((wide, columns), jnp.float32)
            for colour in range(2):
                other = field[1 - colour][pair + 2, :wide]
                around = other + both_ways(other, 1)
                around = around + jnp.where(bottom, 0.0, roll(other, -1, 0))
                around = around + jnp.where(top, 0.0, roll(other, 1, 0))
                first = field[1 - colour][pair + 1, :wide] if pair else 0.0
                second = field[1 - colour][pair + 3, :wide] if pair < pairs - 1 else 0.0
                if colour == 1:
                    first, second = second, first
                around = around + jnp.where(is_odd, second, first)
                at = (pair + 2, slice(0, wide))
                total = total + residual(around, field[colour][at], mass[colour][at], source[colour][at])
            values = [field[0][at] + field[1][at], total, mass[0][at] + mass[1][at]]
            for at, value in enumerate(values):
                for r in range(quarter):
                    tall[at, r, pair : pair + 1] = value[r : r + 1]
        low = jnp.where(is_odd, field[1][2, :wide], field[0][2, :wide])
        high = jnp.where(is_odd, field[0][pairs + 1, :wide], field[1][pairs + 1, :wide])
        pieces = []
        for at in range(3):
            for r in range(0, quarter, 2):
                pieces.append((tall[at, r] + tall[at, r + 1]) * (0.125 if at == 0 else 0.5))
        pieces.append(tall[0, 0] * 0.5)
        pieces.append(tall[0, quarter - 1] * 0.5)
        face = jnp.where(upper, high, roll(low, quarter, 0))
        pieces.append((face + roll(face, -1, 0)) * 0.5)
        wide_rows = jnp.concatenate(pieces, 0)
        nxt[...] = pooled(wide_rows, pool_matrix(columns, columns // 2)).reshape(nxt.shape)
        copy.wait()


def second_kernel(counts, extended, outer, inner, faces, middle, packed, nxt, *rest):
    mass, source, field, rest = rest[0:2], rest[2:4], rest[4:6], rest[6:]
    limit, wide, columns = extended.shape[1:]
    quarter = wide // 2
    row_of = iota((wide, columns), 0) % quarter
    top, bottom = row_of == 0, row_of == quarter - 1
    core = my_core()
    for t in range(limit):
        places = [sent_place(at, t, limit) for at in range(3)]
        beside = [sides(core, outer[place], inner[place]) for place in places]
        assemble_second(field, t, extended[0, t], *beside[0])
        assemble_second(mass, t, extended[2, t], *beside[2])
        (one, two), face = beside[1], faces[t]
        tile = extended[1, t] + jnp.where(top, one, 0.0) + jnp.where(bottom, two, 0.0)
        one = one + jnp.where(bottom, face, 0.0)
        two = two + jnp.where(top, face, 0.0)
        assemble_second(source, t, tile, one, two)
    source_from_defect(field, mass, source)
    second_finish(count_of(counts, 1), field, mass, source, middle, packed, nxt, *rest)


def second_again_kernel(counts, extended, outer, inner, *rest):
    mass, source = rest[0:2], rest[2:4]
    middle, packed, nxt, *rest = rest[4:]
    field, rest = rest[:2], rest[2:]
    core = my_core()
    for t in range(extended.shape[0]):
        assemble_second(field, t, extended[t], *sides(core, outer[t], inner[t]))
    second_finish(count_of(counts, 1) - 2, field, mass, source, middle, packed, nxt, *rest)


def second_level(parts, edge_left, edge_right, count, counts):
    tiles, wide, columns = parts.shape[1:]
    limit = tiles + 4
    x_left = shifted(edge_right, "group", 1)
    x_right = shifted(edge_left, "group", -1)
    three = (3, limit, wide, columns)
    message = (3 * limit - 2, wide, columns)
    shapes = [three, message, message, (limit, wide, columns)]
    extended, outer, inner, faces = call(second_prepare_kernel, shapes, [parts, x_left, x_right])
    window = (limit, 2 * wide, columns)
    outs = [(2 * tiles, wide // 2, columns), (tiles, wide, columns), (9, tiles, columns // 2)]
    scratch = [window, window, (3, wide // 2, tiles, columns)]
    args = [counts, extended, *both_swapped(inner, outer), faces]
    middle, packed, nxt, *fixed = call(second_kernel, outs + [window] * 4, args, scratch, 1)

    def again(given):
        packed = given[1]
        x_left = shifted(packed[-2:], "group", 1)
        x_right = shifted(packed[:2], "group", -1)
        extended = jnp.concatenate([x_left, packed, x_right], 0)
        args = [counts, extended, *both_swapped(extended, extended), *fixed]
        return list(call(second_again_kernel, outs, args, scratch, 1))

    done = lax.cond(count > 2, again, lambda given: given, [middle, packed, nxt])
    return done[0], done[2]


def third_prepare_kernel(*refs):
    blocks, out = refs[:-1], refs[-1]
    count = len(blocks)
    rows, columns = blocks[0].shape[1:]
    row = iota((rows, columns), 0)
    for b in range(count):
        span = pl.ds(pl.multiple_of(((lax.axis_index("group") + b) % count) * rows, rows), rows)
        before, after = blocks[b - 1][8], blocks[(b + 1) % count][8]
        for at in range(8):
            value = blocks[b][at]
            if at in (2, 3):
                high = before[2 * (at - 2) : 2 * (at - 2) + 1]
                low = after[rows // 2 + 2 * (at - 2) : rows // 2 + 2 * (at - 2) + 1]
                value = value + jnp.where(row == 0, high, 0.0) + jnp.where(row == rows - 1, low, 0.0)
            out[at, span] = value


FIELD, DEFECT, MASS, FACE = 0, 4, 7, 10


def third_chip_kernel(own, other, chip, rest):
    edge = my_core()
    for at, start in enumerate((FIELD, DEFECT, MASS)):
        values = [own[2 * at + edge], own[2 * at + 1 - edge], other[2 * at + edge], other[2 * at + 1 - edge]]
        if at == 1:
            values[1] = values[1] + other[6 + edge]
            values[2] = values[2] + own[7 - edge]
        for k in range(4 if at == 0 else 3):
            chip[start + k] = values[k]
        if at > 0:
            rest[at - 1] = values[3]
    chip[FACE] = own[6 + edge]
    rest[2] = other[7 - edge]


def third_finish(count, field, mass, source, coarse, packed, message, tall, held, sent):
    rows, columns = field[0].shape[1:]
    core = my_core()
    is_odd = odd((rows, columns), plus=core)
    two_sweeps(count, field, mass, source, 6, core)
    red, black = field[0][2], field[1][2]
    one, two = jnp.where(is_odd, black, red), jnp.where(is_odd, red, black)
    for colour in range(2):
        for k in range(2):
            packed[2 * colour + k] = field[colour][2 + k]
    tall[:rows] = jnp.where(core == 0, one, two)
    tall[rows : 2 * rows] = jnp.where(core == 0, two, one)
    for r in range(rows):
        held[2 * r : 2 * r + 1] = tall[r : r + 1]
        held[2 * r + 1 : 2 * r + 2] = tall[rows + r : rows + r + 1]
    copy = pltpu.make_async_copy(held, coarse, sent)

    @pl.when(count <= 2)
    def _():
        copy.start()
        totals = []
        for q in (2, 3):
            total = jnp.zeros((rows, columns), jnp.float32)
            for colour in range(2):
                other = field[1 - colour]
                beyond = inner_only(is_odd, other[5 - q], q, colour)
                around = other[q] + beyond + both_ways(other[q], 0) + both_ways(other[q], 1)
                total = total + residual(around, field[colour][q], mass[colour][q], source[colour][q])
            totals.append(total * 0.5)
        red, black = field[0][3], field[1][3]
        last = jnp.where(is_odd, red, black)
        pieces = [(field[0][q] + field[1][q]) * 0.125 for q in (2, 3)] + totals
        pieces += [(mass[0][q] + mass[1][q]) * 0.5 for q in (2, 3)] + [one * 0.5, last * 0.5]
        tall[...] = pooled(jnp.concatenate(pieces, 0), pool_matrix(columns, columns))
        half = rows // 2
        narrow = tall[pl.ds(0, 8 * half, stride=2)] + tall[pl.ds(1, 8 * half, stride=2)]
        lane = iota((half, columns), 1) // (columns // 2)
        lower = lane == core
        is_odd_half = odd((half, columns))
        even_row = same_row((half, columns))

        def narrow_of(k):
            return narrow[k * half : (k + 1) * half]

        tiles = []
        for at in range(3):
            tile = jnp.where(lower, narrow_of(2 * at), narrow_of(2 * at + 1))
            tiles.append(jnp.where(is_odd_half, roll(tile, columns // 2, 1), tile))
        low_face = jnp.where(core == 0, narrow_of(6), narrow_of(7))
        high_face = jnp.where(core == 0, narrow_of(7), narrow_of(6))
        tiles.append(jnp.where(even_row, high_face, low_face))
        for at in range(2):
            tile = jnp.where(core == 0, tiles[at], tiles[2 + at])
            tile = jnp.where(lax.axis_index("brick") < message.shape[0], tile, roll(tile, columns // 2, 1))
            for c in range(message.shape[0]):
                message[c, at] = tile
        copy.wait()


def same_row(shape):
    half = shape[1] // 2
    lane = iota(shape, 1)
    return ((iota(shape, 0) + lane + lane // half) & 1) == 0


def inner_only(is_odd, inner, q, colour):
    above = is_odd if colour == 0 else jnp.logical_not(is_odd)
    return jnp.where(above, inner, 0.0) if q == 2 else jnp.where(above, 0.0, inner)


def pack_pair(window, at, even, next_one, is_odd):
    window[0][at] = jnp.where(is_odd, next_one, even)
    window[1][at] = jnp.where(is_odd, even, next_one)


def third_kernel(counts, chip, inner, near, far, coarse, packed, message, *rest):
    mass, source, field, rest = rest[0:2], rest[2:4], rest[4:6], rest[6:]
    rows, columns = chip.shape[1:]
    is_odd = odd((rows, columns), plus=my_core())
    for at, (window, start) in enumerate(((field, FIELD), (source, DEFECT), (mass, MASS))):
        side, own, beyond = ([part[start + min(k, 3 if at == 0 else 2)] for k in range(4)] for part in (near, chip, far))
        if at > 0:
            own[3] = inner[at - 1]
        if at == 1:
            side[0] = side[0] + chip[FACE]
            own[0] = own[0] + near[FACE]
            own[3] = own[3] + far[FACE]
            beyond[0] = beyond[0] + inner[2]
        line = side[::-1] + own + beyond
        for q in range(6):
            pack_pair(window, q, line[2 * q], line[2 * q + 1], is_odd)
    source_from_defect(field, mass, source, plus=my_core())
    third_finish(count_of(counts, 2), field, mass, source, coarse, packed, message, *rest)


def third_again_kernel(counts, chip, near, far, *rest):
    mass, source = rest[0:2], rest[2:4]
    coarse, packed, message, *rest = rest[4:]
    field, rest = rest[:2], rest[2:]
    for colour in range(2):
        for k in range(2):
            field[colour][1 - k] = near[2 * colour + k]
            field[colour][2 + k] = chip[2 * colour + k]
            field[colour][4 + k] = far[2 * colour + k]
    third_finish(count_of(counts, 2) - 2, field, mass, source, coarse, packed, message, *rest)


def third_level(part, count, counts):
    groups, chips = lax.axis_size("group"), lax.axis_size("brick") // 2
    tile_rows, columns = part.shape[1:]
    rows = groups * tile_rows
    blocks = [part] + [shifted(part, "group", -d) for d in range(1, groups)]
    (own,) = call(third_prepare_kernel, [(8, rows, columns)], blocks)
    shapes = [(11, rows, columns), (3, rows, columns)]
    chip, inner = call(third_chip_kernel, shapes, [own, swapped_cores(own)])
    near = swapped_chips(chip)
    far = swapped_cores(near)
    window = (6, rows, columns)
    outs = [(2 * rows, columns), (4, rows, columns), (chips, 2, rows // 2, columns)]
    scratch = [window, window, (8 * rows, columns)]
    args = [counts, chip, inner, near, far]
    coarse, packed, message, *fixed = call(third_kernel, outs + [window] * 4, args, scratch, 1)

    def again(given):
        packed = given[1]
        near = swapped_chips(packed)
        args = [counts, packed, near, swapped_cores(near), *fixed]
        return list(call(third_again_kernel, outs, args, scratch, 1))

    done = lax.cond(count > 2, again, lambda given: given, [coarse, packed, message])
    return done[0].reshape(rows, 2, columns), done[2]


def fourth_kernel(counts, own, other, out, *windows):
    field, mass, source, (held, sent) = windows[0:2], windows[2:4], windows[4:6], windows[6:]
    chips, _, rows, columns = own.shape
    tiles, half = chips // 2, columns // 2
    lane = iota((rows, columns), 1)
    low = lane < half
    is_odd = odd((rows, columns))
    first, last = lane % half == 0, lane % half == half - 1

    def turned(value):
        return roll(value, half, 1)

    def beside(value):
        after = jnp.where(last, roll(value, half - 1, 1), roll(value, -1, 1))
        return after + jnp.where(first, roll(value, 1 - half, 1), roll(value, 1, 1))

    def put(window, t, one, two):
        window[0][t + 1] = jnp.where(low, one, two)
        window[1][t + 1] = turned(jnp.where(low, two, one))

    def repeat(window, colour):
        window[colour][0] = turned(window[colour][tiles])
        window[colour][tiles + 1] = turned(window[colour][1])

    def load(one, two):
        even_row = same_row((rows, columns))

        def defect(t):
            before, after = two[(t - 1) % chips, 1], two[(t + 1) % chips, 1]
            before = turned(before) if t in (0, tiles) else before
            after = turned(after) if t in (tiles - 1, chips - 1) else after
            if t < tiles:
                return one[t, 1] + jnp.where(even_row, before, after)
            return one[t, 1] + jnp.where(even_row, after, before)

        for t in range(tiles):
            put(field, t, one[t, 0], one[t + tiles, 0])
            put(mass, t, two[t, 0], two[t + tiles, 0])
            put(source, t, defect(t), defect(t + tiles))

    @pl.when(my_core() == 0)
    def _():
        load(own, other)

    @pl.when(my_core() == 1)
    def _():
        load(other, own)

    for colour in range(2):
        repeat(field, colour)
    source_from_defect(field, mass, source, beside, range(1, tiles + 1))

    def one_sweep(step, carry):
        for colour in range(2):
            half_sweep(field, mass, source, colour, 1, tiles + 1, 16, beside)
            repeat(field, colour)
        return carry

    lax.fori_loop(0, count_of(counts, 3), one_sweep, 0)
    for t in range(tiles):
        red, black = field[0][t + 1], field[1][t + 1]
        red_too, black_too = turned(red), turned(black)
        one = jnp.where(low, jnp.where(is_odd, black, red), jnp.where(is_odd, red_too, black_too))
        two = jnp.where(low, jnp.where(is_odd, black_too, red_too), jnp.where(is_odd, red, black))
        for at, value in ((t, one), (t + tiles, two)):
            held[:, at * columns : (at + 1) * columns] = value
    copy = pltpu.make_async_copy(held, out, sent)
    copy.start()
    copy.wait()


def fourth_level(message, counts):
    chips, _, rows, columns = message.shape
    cores = [[2 * chip + c for chip in range(chips)] for c in range(2)]
    own = lax.all_to_all(message, "brick", 0, 0, axis_index_groups=cores)
    other = swapped_cores(own)
    scratch = [(chips // 2 + 2, rows, columns)] * 6
    (out,) = call(fourth_kernel, [(rows, chips * columns)], [counts, own, other], scratch, 1)
    return out


def on_device(initial_field, mass, source, sweeps):
    counts, ahead, (fine, parts, edge_left, edge_right) = first_level(initial_field, mass, source, sweeps)
    middle, part = second_level(parts, edge_left, edge_right, ahead[1][0], counts)
    coarse, message = third_level(part, ahead[2][0], counts)
    coarsest = fourth_level(message, counts)
    return fine, middle, coarse, coarsest


def solution(mesh):
    return jax.shard_map(
        on_device,
        mesh=mesh,
        in_specs=(
            P("group", "brick", None),
            P("group", "brick", None),
            P("group", "brick", None),
            P(),
        ),
        out_specs=(
            P("group", "brick", None),
            P("group", "brick", None),
            P(None, "brick", None),
            P(),
        ),
        check_vma=False,
    )
```

```python
import functools

import jax
import jax.numpy as jnp
from jax import lax
from jax.experimental import pallas as pl
from jax.experimental.pallas import tpu as pltpu
from jax.sharding import PartitionSpec as P


INTERPRET = False
MIB = 1024 * 1024
LANES = 128


def call(kernel, out_shapes, args, scratch=(), results=0, limit=12 * MIB):
    spec = pl.BlockSpec(memory_space=pltpu.VMEM)
    return pl.pallas_call(
        kernel,
        out_shape=[
            (pltpu.HBM if at < results else pltpu.VMEM)(shape, jnp.float32) for at, shape in enumerate(out_shapes)
        ],
        in_specs=[spec] * len(args),
        out_specs=[pl.BlockSpec(memory_space=pltpu.HBM)] * results + [spec] * (len(out_shapes) - results),
        scratch_shapes=[pltpu.VMEM(shape, jnp.float32) for shape in [*scratch, *out_shapes[:results]]]
        + [pltpu.SemaphoreType.DMA] * results,
        compiler_params=pltpu.CompilerParams(vmem_limit_bytes=limit),
        interpret=INTERPRET,
    )(*args)


def iota(shape, axis):
    return lax.broadcasted_iota(jnp.int32, shape, axis)


def odd(shape, period=None, plus=0):
    rows = iota(shape, 0)
    if period is not None:
        rows = rows % period
    return ((rows + iota(shape, 1) + plus) & 1) == 1


def same_member(shape, quarter):
    rows = iota(shape, 0)
    return ((rows % quarter + rows // quarter + iota(shape, 1)) & 1) == 0


def roll(value, shift, axis):
    return pltpu.roll(value, shift % value.shape[axis], axis)


def both_ways(value, axis):
    return roll(value, 1, axis) + roll(value, -1, axis)


def newton(around, value, mass, source):
    curve = mass * (value * value)
    over = (around + source) + 2.0 * (curve * value)
    under = (6.0 + mass) + 3.0 * curve
    guess = pl.reciprocal(under, approx=True)
    guess = guess * (2.0 - under * guess)
    return over * guess


def residual(around, value, mass, source):
    return (around - 6.0 * value) - mass * (value * value * value + value) + source


def pooled(rows, pool):
    high = rows.astype(jnp.bfloat16)
    rest = rows - high.astype(jnp.float32)
    middle = rest.astype(jnp.bfloat16)
    low = (rest - middle.astype(jnp.float32)).astype(jnp.bfloat16)
    dot = functools.partial(jnp.dot, preferred_element_type=jnp.float32)
    return dot(high, pool) + (dot(middle, pool) + dot(low, pool))


def pool_matrix(width, columns):
    half = width // 2
    shape = (width, columns)
    return jnp.where(iota(shape, 0) // 2 == iota(shape, 1) % half, 1.0, 0.0).astype(jnp.bfloat16)


def beside_matrix(width):
    shape = (width, width // 2)
    place = (iota(shape, 0) - 2 * iota(shape, 1) + 1 + width) % width
    return jnp.where(place < 4, 1.0, 0.0).astype(jnp.bfloat16)


def half_sweep(field, mass, source, colour, low, high, most, beside=None, plus=0):
    mine, other = field[colour], field[1 - colour]
    limit, rows, columns = mine.shape
    is_odd = odd((rows, columns), plus=plus)
    beside = beside or (lambda value: both_ways(value, 1))
    together = max(k for k in range(1, most + 1) if (high - low) % k == 0)

    def step(turn, carry):
        start = low + turn * together
        near = [other[jnp.clip(start + k, 0, limit - 1)] for k in range(-1, together + 1)]
        fresh = []
        for k in range(together):
            first, second = (near[k], near[k + 2]) if colour == 0 else (near[k + 2], near[k])
            around = near[k + 1] + jnp.where(is_odd, second, first)
            around = around + both_ways(near[k + 1], 0) + beside(near[k + 1])
            fresh.append(newton(around, mine[start + k], mass[colour][start + k], source[colour][start + k]))
        for k in range(together):
            mine[start + k] = fresh[k]
        return carry

    turns = (high - low) // together
    if turns == 1:
        step(0, 0)
    else:
        lax.fori_loop(0, turns, step, 0)


def two_sweeps(count, field, mass, source, most, plus=0):
    limit = field[0].shape[0]
    half_sweep(field, mass, source, 0, 0, limit, most, plus=plus)
    half_sweep(field, mass, source, 1, 1, limit - 1, most, plus=plus)

    @pl.when(count >= 2)
    def _():
        half_sweep(field, mass, source, 0, 1, limit - 1, most, plus=plus)
        half_sweep(field, mass, source, 1, 2, limit - 2, most, plus=plus)


def source_from_defect(field, mass, source, beside=None, inner=None, plus=0):
    limit, rows, columns = field[0].shape
    is_odd = odd((rows, columns), plus=plus)
    beside = beside or (lambda value: both_ways(value, 1))
    for index in inner or range(limit):
        for colour in range(2):
            other = field[1 - colour]
            first, second = other[max(index - 1, 0)], other[min(index + 1, limit - 1)]
            if colour == 1:
                first, second = second, first
            around = other[index] + jnp.where(is_odd, second, first)
            around = around + both_ways(other[index], 0) + beside(other[index])
            source[colour][index] = source[colour][index] - residual(
                around, field[colour][index], mass[colour][index], 0.0
            )


def shifted(value, axis, by):
    count = lax.axis_size(axis)
    return lax.ppermute(value, axis, [(i, (i + by) % count) for i in range(count)])


def swapped_cores(value):
    count = lax.axis_size("brick")
    return lax.ppermute(value, "brick", [(i, i ^ 1) for i in range(count)])


def swapped_chips(value):
    count = lax.axis_size("brick")
    return lax.ppermute(value, "brick", [(i, (i + 1 if i % 2 else i - 1) % count) for i in range(count)])


def both_swapped(inner, outer):
    far = swapped_chips(outer)
    return far, swapped_cores(inner)


def sides(core, outer, inner):
    on_first = jnp.broadcast_to(core, outer.shape) == 0
    return jnp.where(on_first, outer, inner), jnp.where(on_first, inner, outer)


def my_core():
    return lax.axis_index("brick") & 1


def count_of(counts, level):
    return jnp.max(counts[level])


def kept_pairs(pairs):
    quarter = pairs // 4
    kept = list(range(quarter)) + list(range(pairs - quarter, pairs))
    return kept, list(range(quarter, pairs - quarter))


def ride_right(row, mass, source, rider):
    mass = jnp.where(row < 2, roll(rider, -2, 0), jnp.where(row == 4, roll(rider, -1, 0), mass))
    return mass, jnp.where(row < 2, roll(rider, 2, 0), source)


def ride_left(row, mass, source, rider):
    mass = jnp.where(row > 5, roll(rider, 2, 0), jnp.where(row == 3, roll(rider, 1, 0), mass))
    return mass, jnp.where(row > 5, roll(rider, -2, 0), source)


def rider_from_left(row, mass, source):
    return jnp.where(row < 4, roll(mass, 2, 0), jnp.where(row == 5, roll(mass, 1, 0), roll(source, -2, 0)))


def rider_from_right(row, mass, source):
    return jnp.where(row < 2, roll(source, 2, 0), jnp.where(row == 2, roll(mass, -1, 0), roll(mass, -2, 0)))


def pack_kernel(*refs):
    sweeps, *blocks = refs[:4]
    own, outer, inner, edge_left, edge_right, counts, *ahead = refs[4:13]
    held, arrived, few, few_arrived, sent, *singles = refs[13:]
    count = len(blocks)
    core = my_core()
    pairs = own.shape[2]
    rows, columns = own.shape[3:]
    is_odd = odd((rows, columns))
    row = iota((rows, columns), 0)
    upper = row < rows // 2
    parts = arrived.shape[1]
    some = 2 * pairs // parts

    def part_of(at, part):
        span = pl.ds(some * part, some)
        return pltpu.make_async_copy(blocks[at].at[span], held.at[at, span], arrived.at[at, part])

    def packed(at, pair):
        even, next_one = held[at, 2 * pair], held[at, 2 * pair + 1]
        red = jnp.where(is_odd, next_one, even)
        black = jnp.where(is_odd, even, next_one)
        own[at, 0, pair] = red
        own[at, 1, pair] = black
        if pair < 2:
            edge_left[at, 0, pair] = red
            edge_left[at, 1, pair] = black
        if pair >= pairs - 2:
            edge_right[at, 0, pair - pairs + 2] = red
            edge_right[at, 1, pair - pairs + 2] = black
        turned = roll(black, rows // 2, 0)
        return jnp.where(upper, red, turned), jnp.where(upper, turned, red)

    for at in range(count):
        for part in range(parts):
            part_of(at, part).start()
    copy = pltpu.make_async_copy(sweeps, few, few_arrived)
    copy.start()
    copy.wait()
    alone = []
    for level, (single, out) in enumerate(zip(singles, ahead)):
        single[0] = few[level]
        alone.append(pltpu.make_async_copy(single, out, sent.at[level]))
        alone[-1].start()
    for level in range(4):
        counts[level] = jnp.full(counts.shape[1:], few[level])
    for part in range(parts):
        part_of(0, part).wait()
        for pair in range(some // 2 * part, some // 2 * (part + 1)):
            outer[pair], inner[pair] = sides(core, *packed(0, pair))
    for at in (1, 2):
        for part in range(parts):
            part_of(at, part).wait()
    kept, riders = kept_pairs(pairs)
    half = pairs // 2
    for k, (pair, other) in enumerate(zip(kept, riders)):
        mass, source = packed(1, pair), packed(2, pair)
        other_mass, rider = packed(1, other), packed(2, other)
        left = ride_left(row, mass[0], source[0], rider[0])
        right = ride_right(row, mass[1], source[1], rider[1])
        places = (pairs + k, pairs + half + k, 2 * pairs + k)
        for place, one, two in zip(places, (*left, other_mass[0]), (*right, other_mass[1])):
            outer[place], inner[place] = sides(core, one, two)
    for copy in alone:
        copy.wait()


def corner_kernel(y_outer, y_inner, to_left, to_right):
    core = my_core()
    tiles, rows, columns = y_outer.shape
    pairs = tiles if to_left.shape[0] == 3 else tiles * 2 // 5
    from_right = iota((rows, columns), 0) % (rows // 2) < rows // 4
    for out, near, far, kept in ((to_left, 0, 1, 0), (to_right, pairs - 1, pairs - 2, pairs // 2 - 1)):
        out[0], out[1] = sides(core, y_outer[near], y_inner[near])
        both = [far] if out.shape[0] == 3 else [far, pairs + kept, pairs + pairs // 2 + kept]
        for k, at in enumerate(both):
            left, right = sides(core, y_outer[at], y_inner[at])
            out[2 + k] = jnp.where(from_right, right, left)


def pack_shapes(count, pairs, tile):
    shapes = [(count, 2, pairs, *tile)] + [(pairs if count == 1 else pairs * 5 // 2, *tile)] * 2
    return shapes + [(count, 2, 2, *tile)] * 2


def packed_blocks(sweeps, blocks):
    count = len(blocks)
    rows, *tile = blocks[0].shape
    shapes = pack_shapes(count, rows // 2, tile)
    return pl.pallas_call(
        pack_kernel,
        out_shape=[pltpu.VMEM(shape, jnp.float32) for shape in shapes] + [pltpu.VMEM((4, 8, LANES), jnp.int32)]
        + [pltpu.HBM((1,), jnp.int32)] * 3,
        in_specs=[pl.BlockSpec(memory_space=pltpu.HBM)] * (1 + count),
        out_specs=[pl.BlockSpec(memory_space=pltpu.VMEM)] * (len(shapes) + 1)
        + [pl.BlockSpec(memory_space=pltpu.HBM)] * 3,
        scratch_shapes=[
            pltpu.VMEM((count, rows, *tile), jnp.float32),
            pltpu.SemaphoreType.DMA((count, 4)),
            pltpu.SMEM((4,), jnp.int32),
            pltpu.SemaphoreType.DMA,
            pltpu.SemaphoreType.DMA((3,)),
            *[pltpu.SMEM((1,), jnp.int32)] * 3,
        ],
        compiler_params=pltpu.CompilerParams(vmem_limit_bytes=12 * MIB),
    )(*[pltpu.with_memory_space_constraint(value, pltpu.HBM) for value in (sweeps, *blocks)])


def first_exchange(own, outer, inner, edge_left, edge_right):
    count, tile = own.shape[0], own.shape[3:]
    y_outer, y_inner = both_swapped(inner, outer)
    x_left = shifted(edge_right, "group", 1)
    x_right = shifted(edge_left, "group", -1)
    corners = call(corner_kernel, [(3 if count == 1 else 5, *tile)] * 2, [y_outer, y_inner])
    c_left = shifted(corners[1], "group", 1)
    c_right = shifted(corners[0], "group", -1)
    return own, x_left, x_right, y_outer, y_inner, c_left, c_right


def put_first(window, to, red, black, from_left, from_right):
    wide = red.shape[0]
    upper = iota(red.shape, 0) < wide // 2
    window[0][to, :wide] = red
    window[0][to, wide:] = jnp.where(upper, from_right, from_left)
    window[1][to, :wide] = black
    window[1][to, wide:] = roll(jnp.where(upper, from_left, from_right), wide // 2, 0)


def assemble_own(window, at, own, y_outer, y_inner):
    pairs, wide, columns = own.shape[2:]
    row = iota((wide, columns), 0)
    kept, riders = kept_pairs(pairs)
    core = my_core()

    def beside(place):
        return sides(core, y_outer[place], y_inner[place])

    for pair in range(pairs):
        if at == 0:
            left, right = beside(pair)
        elif pair in kept:
            left, right = beside(pairs + (at - 1) * (pairs // 2) + kept.index(pair))
        elif at == 1:
            left, right = beside(2 * pairs + riders.index(pair))
        else:
            (left, right), other = beside(pairs + riders.index(pair)), beside(pairs + pairs // 2 + riders.index(pair))
            left, right = rider_from_left(row, left, other[0]), rider_from_right(row, right, other[1])
        put_first(window, pair, own[at, 0, pair], own[at, 1, pair], left, right)


def assemble_edges(window, at, places, x_left, x_right, c_left, c_right):
    for side, x_side, corner in ((0, x_left, c_left), (1, x_right, c_right)):
        for k in range(2):
            if at == 0:
                near = k != side
                left, right = (corner[0], corner[1]) if near else (corner[2], corner[2])
            else:
                left = right = corner[2 + at]
            put_first(window, places[2 * side + k], x_side[at, 0, k], x_side[at, 1, k], left, right)


def inner_sweeps(count, field, mass, source):
    pairs = field[0].shape[0]

    def half(colour, less):
        whole = (pairs - 2 * less) // 4 * 4
        half_sweep(field, mass, source, colour, less, less + whole, 4)
        if whole < pairs - 2 * less:
            half_sweep(field, mass, source, colour, less + whole, pairs - less, 4)

    half(0, 1)
    half(1, 2)

    @pl.when(count >= 2)
    def _():
        half(0, 3)
        half(1, 4)


def edge_sweeps(count, field, mass_of, source_of):
    limit, rows, columns = field[0].shape
    is_odd = odd((rows, columns))

    def some(colour, positions):
        mine, other = field[colour], field[1 - colour]
        fresh = []
        for w in positions:
            first, second = other[max(w - 1, 0)], other[min(w + 1, limit - 1)]
            if colour == 1:
                first, second = second, first
            value = other[w]
            around = value + jnp.where(is_odd, second, first) + both_ways(value, 0) + both_ways(value, 1)
            fresh.append(newton(around, mine[w], mass_of(colour, w), source_of(colour, w)))
        for w, value in zip(positions, fresh):
            mine[w] = value

    def half(colour, low, high):
        some(colour, range(low, high))
        some(colour, range(limit - high, limit - low))

    half(0, 0, 3)
    half(1, 1, 4)

    @pl.when(count >= 2)
    def _():
        half(0, 1, 5)
        half(1, 2, 6)


def first_inner_kernel(counts, own, y_outer, y_inner, *windows):
    field, mass, source = windows[:2], windows[2:4], windows[4:]
    for at, window in enumerate((field, mass, source)):
        assemble_own(window, at, own, y_outer, y_inner)
    inner_sweeps(count_of(counts, 0), field, mass, source)


def first_inner_again_kernel(counts, own, y_outer, y_inner, *windows):
    mass, source, field = windows[:2], windows[2:4], windows[4:]
    assemble_own(field, 0, own, y_outer, y_inner)
    inner_sweeps(count_of(counts, 0) - 2, field, mass, source)


def first_outer(count, halo, inner, mass, source, edges, field):
    pairs = inner[0].shape[0]
    for colour in range(2):
        for pair in range(pairs):
            field[colour][pair + 2] = inner[colour][pair]
    assemble_edges(field, 0, (0, 1, pairs + 2, pairs + 3), *halo)

    def of(whole, beyond):
        def at(colour, w):
            if 2 <= w < pairs + 2:
                return whole[colour][w - 2]
            return beyond[colour][w if w < 2 else w - pairs]

        return at

    edge_sweeps(count, field, of(mass, edges[:2]), of(source, edges[2:]))


def first_kernel(counts, *refs):
    halo, inner, mass, source, refs = refs[:4], refs[4:6], refs[6:8], refs[8:10], refs[10:]
    outs, again, edges, field, rest = refs[:4], refs[4:9], refs[9:13], refs[13:15], refs[15:]
    for at, window in ((1, edges[:2]), (2, edges[2:])):
        assemble_edges(window, at, range(4), *halo)
    count = count_of(counts, 0)
    first_outer(count, halo, inner, mass, source, edges, field)
    first_finish(count, field, mass, source, outs, again, *rest)


def first_again_kernel(counts, *refs):
    halo, inner, mass, source, edges, refs = refs[:4], refs[4:6], refs[6:8], refs[8:10], refs[10:14], refs[14:]
    outs, field, rest = refs[:4], refs[4:6], refs[6:]
    count = count_of(counts, 0) - 2
    first_outer(count, halo, inner, mass, source, edges, field)
    first_finish(count, field, mass, source, outs, None, *rest)


def first_finish(count, field, mass, source, outs, again, tall, held, sent):
    fine, nxt, edge_left, edge_right = outs
    limit, rows, columns = field[0].shape
    pairs, wide = limit - 4, rows // 2
    is_odd = odd((wide, columns))
    row = iota((wide, columns), 0)
    top, bottom = row == 0, row == wide - 1
    copy = pltpu.make_async_copy(held, fine, sent)

    if again is not None:

        @pl.when(count > 2)
        def _():
            own, outer, inner, *edges = again
            upper = row < wide // 2
            for pair in range(pairs):
                red, black = field[0][pair + 2, :wide], field[1][pair + 2, :wide]
                own[0, 0, pair] = red
                own[0, 1, pair] = black
                turned = roll(black, wide // 2, 0)
                outer[pair], inner[pair] = sides(
                    my_core(), jnp.where(upper, red, turned), jnp.where(upper, turned, red)
                )
                for edge, first in zip(edges, (0, pairs - 2)):
                    if first <= pair < first + 2:
                        edge[0, 0, pair - first] = red
                        edge[0, 1, pair - first] = black

    def keep(index, value):
        for c in range(columns // LANES):
            tall[c, index] = value[:, c * LANES : (c + 1) * LANES]

    @pl.when(count <= 2)
    def _():
        for pair in range(pairs):
            red, black = field[0][pair + 2, :wide], field[1][pair + 2, :wide]
            held[2 * pair] = jnp.where(is_odd, black, red)
            held[2 * pair + 1] = jnp.where(is_odd, red, black)
        copy.start()

        def step(pair, carry):
            total = jnp.zeros((wide, columns), jnp.float32)
            for colour in range(2):
                other = field[1 - colour][pair + 2, :wide]
                first = jnp.where(pair == 0, 0.0, field[1 - colour][pair + 1, :wide])
                second = jnp.where(pair == pairs - 1, 0.0, field[1 - colour][pair + 3, :wide])
                if colour == 1:
                    first, second = second, first
                around = other + jnp.where(is_odd, second, first)
                around = around + jnp.where(bottom, 0.0, roll(other, -1, 0))
                around = around + jnp.where(top, 0.0, roll(other, 1, 0))
                at, own = (pair + 2, slice(0, wide)), (pair, slice(0, wide))
                total = total + residual(around, field[colour][at], mass[colour][own], source[colour][own])
            keep(pair, field[0][at] + field[1][at])
            keep(pairs + pair, total)
            keep(2 * pairs + pair, mass[0][own] + mass[1][own])
            return carry

        lax.fori_loop(0, pairs, step, 0, unroll=2)
        low = jnp.where(is_odd, field[1][2, :wide], field[0][2, :wide])
        high = jnp.where(is_odd, field[0][pairs + 1, :wide], field[1][pairs + 1, :wide])
        half, tiles, quarter = columns // 2, pairs // 2, wide // 2
        keep(3 * pairs, high)
        keep(3 * pairs + 1, low)
        lines = (3 * pairs + 2) * wide // 2
        flat = tall.reshape(columns // LANES, 2 * lines, LANES)

        def every_other(start):
            parts = [flat[c, pl.ds(start, lines, stride=2)] for c in range(columns // LANES)]
            return jnp.concatenate(parts, 1)

        firsts, seconds = every_other(0), every_other(1)
        whole = (iota((wide, columns), 0)) % quarter
        y_faces = []
        for t in range(tiles):
            last, head = seconds[t * wide : (t + 1) * wide], firsts[t * wide : (t + 1) * wide]
            y_faces.append(
                jnp.where(
                    whole == 0,
                    roll(last, quarter + 1, 0),
                    jnp.where(whole == quarter - 1, roll(head, quarter - 1, 0), 0.0),
                )
            )
        narrow = pooled(jnp.concatenate([firsts + seconds] + y_faces, 0), pool_matrix(columns, half))
        along = pooled((firsts + seconds)[: tiles * wide], beside_matrix(columns))
        is_odd_half = odd((wide, half), quarter)
        is_even = same_member((wide, half), quarter)

        def packed(index, factor):
            tile = narrow[index * wide : (index + 1) * wide]
            if tiles <= index < 2 * tiles:
                tile = tile + along[(index - tiles) * wide : (index - tiles + 1) * wide]
            tile = tile * factor
            return jnp.where(is_odd_half, roll(tile, quarter, 0), tile)

        face_x = packed(3 * tiles, 0.5)
        for t in range(tiles):
            values = [
                packed(t, 0.125),
                packed(tiles + t, 0.5),
                packed(2 * tiles + t, 0.5),
                packed(3 * tiles + 1 + t, 0.5),
            ]
            for at, value in enumerate(values):
                nxt[at, t] = value
                if t < 2:
                    if at == 1 and t == 1:
                        value = jnp.where(is_even, value, face_x)
                    edge_left[at, t] = value
                if t >= tiles - 2:
                    if at == 1 and t == tiles - 2:
                        value = jnp.where(is_even, face_x, value)
                    edge_right[at, t - tiles + 2] = value
        nxt[4, 0] = face_x
        for t in range(1, tiles):
            nxt[4, t] = jnp.zeros((wide, half), jnp.float32)
        copy.wait()


def first_level(field, mass, source, sweeps):
    rows, wide, columns = field.shape
    pairs = rows // 2
    half, tiles = columns // 2, pairs // 2
    window = (pairs + 4, 2 * wide, columns)
    outs = [
        (rows, wide, columns),
        (5, tiles, wide, half),
        (4, 2, wide, half),
        (4, 2, wide, half),
    ]

    inner, edge = (pairs, 2 * wide, columns), (4, 2 * wide, columns)
    scratch = [window, window, (columns // LANES, 3 * pairs + 2, wide, LANES)]
    *packed, counts, first, second, third = packed_blocks(sweeps, [field, mass, source])
    ahead = [first, second, third]
    own, x_left, x_right, y_outer, y_inner, c_left, c_right = first_exchange(*packed)
    windows = call(first_inner_kernel, [inner] * 6, [counts, own, y_outer, y_inner])
    every = outs + pack_shapes(1, pairs, (wide, columns)) + [edge] * 4
    args = [counts, x_left, x_right, c_left, c_right, *windows]
    results = call(first_kernel, every, args, scratch, 1, 20 * MIB)
    once, more, edges = results[:4], results[4:9], results[9:]

    def again(given):
        own, x_left, x_right, y_outer, y_inner, c_left, c_right = first_exchange(*more)
        fixed = windows[2:]
        field = call(first_inner_again_kernel, [inner] * 2, [counts, own, y_outer, y_inner, *fixed])
        args = [counts, x_left, x_right, c_left, c_right, *field, *fixed, *edges]
        return list(call(first_again_kernel, outs, args, scratch, 1, 20 * MIB))

    return counts, ahead, lax.cond(ahead[0][0] > 2, again, lambda given: given, list(once))


def sent_place(at, t, limit):
    return at * limit + t if at < 2 else 2 * limit + min(max(t - 1, 0), limit - 3)


def second_prepare_kernel(own, x_left, x_right, extended, outer, inner, faces):
    tiles, wide, columns = own.shape[1:]
    quarter = wide // 2
    row_of = iota((wide, columns), 0) % quarter
    is_even = same_member((wide, columns), quarter)
    face_x = own[4, 0]
    for t in range(tiles + 4):
        if t < 2:
            source, k = x_left, t
        elif t < tiles + 2:
            source, k = own, t - 2
        else:
            source, k = x_right, t - tiles - 2
        defect = source[1, k]
        if t == 1:
            defect = defect + jnp.where(is_even, 0.0, face_x)
        if t == 2:
            defect = defect + jnp.where(is_even, x_left[1, 0], 0.0)
        if t == tiles + 1:
            defect = defect + jnp.where(is_even, 0.0, x_right[1, 1])
        if t == tiles + 2:
            defect = defect + jnp.where(is_even, face_x, 0.0)
        face_y = source[3, k]
        faces[t] = face_y
        for at in range(3):
            value = defect if at == 1 else source[at, k]
            extended[at, t] = value
            left = jnp.where(row_of == quarter - 1, face_y, value) if at == 1 else value
            right = jnp.where(row_of == 0, face_y, value) if at == 1 else value
            if at == 0:
                outer[t] = inner[t] = value
            elif at == 1 or 0 < t < tiles + 3:
                place = sent_place(at, t, tiles + 4)
                outer[place], inner[place] = sides(my_core(), left, right)


def assemble_second(window, to, tile, left, right):
    wide = tile.shape[0]
    quarter = wide // 2
    upper = iota(tile.shape, 0) < quarter
    window[0][to, :wide] = jnp.where(upper, tile, roll(right, quarter, 0))
    window[0][to, wide:] = roll(left, quarter, 0)
    window[1][to, :wide] = jnp.where(upper, roll(tile, quarter, 0), right)
    window[1][to, wide:] = left


def second_finish(count, field, mass, source, middle, packed, nxt, tall, held, sent):
    limit, rows, columns = field[0].shape
    pairs = limit - 4
    wide = rows // 2
    quarter = wide // 2
    two_sweeps(count, field, mass, source, 6)
    is_odd = odd((wide, columns), quarter)
    row = iota((wide, columns), 0)
    upper = row < quarter
    top, bottom = row == 0, row == quarter - 1
    for pair in range(pairs):
        red, black = field[0][pair + 2, :wide], field[1][pair + 2, :wide]
        tile = jnp.where(upper, red, roll(black, quarter, 0))
        packed[pair] = tile
        plain = jnp.where(is_odd, roll(tile, quarter, 0), tile)
        held[2 * pair] = plain[:quarter]
        held[2 * pair + 1] = plain[quarter:]
    copy = pltpu.make_async_copy(held, middle, sent)

    @pl.when(count <= 2)
    def _():
        copy.start()
        for pair in range(pairs):
            total = jnp.zeros((wide, columns), jnp.float32)
            for colour in range(2):
                other = field[1 - colour][pair + 2, :wide]
                around = other + both_ways(other, 1)
                around = around + jnp.where(bottom, 0.0, roll(other, -1, 0))
                around = around + jnp.where(top, 0.0, roll(other, 1, 0))
                first = field[1 - colour][pair + 1, :wide] if pair else 0.0
                second = field[1 - colour][pair + 3, :wide] if pair < pairs - 1 else 0.0
                if colour == 1:
                    first, second = second, first
                around = around + jnp.where(is_odd, second, first)
                at = (pair + 2, slice(0, wide))
                total = total + residual(around, field[colour][at], mass[colour][at], source[colour][at])
            values = [field[0][at] + field[1][at], total, mass[0][at] + mass[1][at]]
            for at, value in enumerate(values):
                for r in range(quarter):
                    tall[at, r, pair : pair + 1] = value[r : r + 1]
        low = jnp.where(is_odd, field[1][2, :wide], field[0][2, :wide])
        high = jnp.where(is_odd, field[0][pairs + 1, :wide], field[1][pairs + 1, :wide])
        pieces = []
        for at in range(3):
            for r in range(0, quarter, 2):
                pieces.append((tall[at, r] + tall[at, r + 1]) * (0.125 if at == 0 else 0.5))
        pieces.append(tall[0, 0] * 0.5)
        pieces.append(tall[0, quarter - 1] * 0.5)
        face = jnp.where(upper, high, roll(low, quarter, 0))
        pieces.append((face + roll(face, -1, 0)) * 0.5)
        wide_rows = jnp.concatenate(pieces, 0)
        nxt[...] = pooled(wide_rows, pool_matrix(columns, columns // 2)).reshape(nxt.shape)
        copy.wait()


def second_kernel(counts, extended, outer, inner, faces, middle, packed, nxt, *rest):
    mass, source, field, rest = rest[0:2], rest[2:4], rest[4:6], rest[6:]
    limit, wide, columns = extended.shape[1:]
    quarter = wide // 2
    row_of = iota((wide, columns), 0) % quarter
    top, bottom = row_of == 0, row_of == quarter - 1
    core = my_core()
    for t in range(limit):
        places = [sent_place(at, t, limit) for at in range(3)]
        beside = [sides(core, outer[place], inner[place]) for place in places]
        assemble_second(field, t, extended[0, t], *beside[0])
        assemble_second(mass, t, extended[2, t], *beside[2])
        (one, two), face = beside[1], faces[t]
        tile = extended[1, t] + jnp.where(top, one, 0.0) + jnp.where(bottom, two, 0.0)
        one = one + jnp.where(bottom, face, 0.0)
        two = two + jnp.where(top, face, 0.0)
        assemble_second(source, t, tile, one, two)
    source_from_defect(field, mass, source)
    second_finish(count_of(counts, 1), field, mass, source, middle, packed, nxt, *rest)


def second_again_kernel(counts, extended, outer, inner, *rest):
    mass, source = rest[0:2], rest[2:4]
    middle, packed, nxt, *rest = rest[4:]
    field, rest = rest[:2], rest[2:]
    core = my_core()
    for t in range(extended.shape[0]):
        assemble_second(field, t, extended[t], *sides(core, outer[t], inner[t]))
    second_finish(count_of(counts, 1) - 2, field, mass, source, middle, packed, nxt, *rest)


def second_level(parts, edge_left, edge_right, count, counts):
    tiles, wide, columns = parts.shape[1:]
    limit = tiles + 4
    x_left = shifted(edge_right, "group", 1)
    x_right = shifted(edge_left, "group", -1)
    three = (3, limit, wide, columns)
    message = (3 * limit - 2, wide, columns)
    shapes = [three, message, message, (limit, wide, columns)]
    extended, outer, inner, faces = call(second_prepare_kernel, shapes, [parts, x_left, x_right])
    window = (limit, 2 * wide, columns)
    outs = [(2 * tiles, wide // 2, columns), (tiles, wide, columns), (9, tiles, columns // 2)]
    scratch = [window, window, (3, wide // 2, tiles, columns)]
    args = [counts, extended, *both_swapped(inner, outer), faces]
    middle, packed, nxt, *fixed = call(second_kernel, outs + [window] * 4, args, scratch, 1)

    def again(given):
        packed = given[1]
        x_left = shifted(packed[-2:], "group", 1)
        x_right = shifted(packed[:2], "group", -1)
        extended = jnp.concatenate([x_left, packed, x_right], 0)
        args = [counts, extended, *both_swapped(extended, extended), *fixed]
        return list(call(second_again_kernel, outs, args, scratch, 1))

    done = lax.cond(count > 2, again, lambda given: given, [middle, packed, nxt])
    return done[0], done[2]


def third_prepare_kernel(*refs):
    blocks, out = refs[:-1], refs[-1]
    count = len(blocks)
    rows, columns = blocks[0].shape[1:]
    row = iota((rows, columns), 0)
    for b in range(count):
        span = pl.ds(pl.multiple_of(((lax.axis_index("group") + b) % count) * rows, rows), rows)
        before, after = blocks[b - 1][8], blocks[(b + 1) % count][8]
        for at in range(8):
            value = blocks[b][at]
            if at in (2, 3):
                high = before[2 * (at - 2) : 2 * (at - 2) + 1]
                low = after[rows // 2 + 2 * (at - 2) : rows // 2 + 2 * (at - 2) + 1]
                value = value + jnp.where(row == 0, high, 0.0) + jnp.where(row == rows - 1, low, 0.0)
            out[at, span] = value


FIELD, DEFECT, MASS, FACE = 0, 4, 7, 10


def third_chip_kernel(own, other, chip, rest):
    edge = my_core()
    for at, start in enumerate((FIELD, DEFECT, MASS)):
        values = [own[2 * at + edge], own[2 * at + 1 - edge], other[2 * at + edge], other[2 * at + 1 - edge]]
        if at == 1:
            values[1] = values[1] + other[6 + edge]
            values[2] = values[2] + own[7 - edge]
        for k in range(4 if at == 0 else 3):
            chip[start + k] = values[k]
        if at > 0:
            rest[at - 1] = values[3]
    chip[FACE] = own[6 + edge]
    rest[2] = other[7 - edge]


def third_finish(count, field, mass, source, coarse, packed, message, tall, held, sent):
    rows, columns = field[0].shape[1:]
    core = my_core()
    is_odd = odd((rows, columns), plus=core)
    two_sweeps(count, field, mass, source, 6, core)
    red, black = field[0][2], field[1][2]
    one, two = jnp.where(is_odd, black, red), jnp.where(is_odd, red, black)
    for colour in range(2):
        for k in range(2):
            packed[2 * colour + k] = field[colour][2 + k]
    tall[:rows] = jnp.where(core == 0, one, two)
    tall[rows : 2 * rows] = jnp.where(core == 0, two, one)
    for r in range(rows):
        held[2 * r : 2 * r + 1] = tall[r : r + 1]
        held[2 * r + 1 : 2 * r + 2] = tall[rows + r : rows + r + 1]
    copy = pltpu.make_async_copy(held, coarse, sent)

    @pl.when(count <= 2)
    def _():
        copy.start()
        totals = []
        for q in (2, 3):
            total = jnp.zeros((rows, columns), jnp.float32)
            for colour in range(2):
                other = field[1 - colour]
                beyond = inner_only(is_odd, other[5 - q], q, colour)
                around = other[q] + beyond + both_ways(other[q], 0) + both_ways(other[q], 1)
                total = total + residual(around, field[colour][q], mass[colour][q], source[colour][q])
            totals.append(total * 0.5)
        red, black = field[0][3], field[1][3]
        last = jnp.where(is_odd, red, black)
        pieces = [(field[0][q] + field[1][q]) * 0.125 for q in (2, 3)] + totals
        pieces += [(mass[0][q] + mass[1][q]) * 0.5 for q in (2, 3)] + [one * 0.5, last * 0.5]
        tall[...] = pooled(jnp.concatenate(pieces, 0), pool_matrix(columns, columns))
        half = rows // 2
        narrow = tall[pl.ds(0, 8 * half, stride=2)] + tall[pl.ds(1, 8 * half, stride=2)]
        lane = iota((half, columns), 1) // (columns // 2)
        lower = lane == core
        is_odd_half = odd((half, columns))
        even_row = same_row((half, columns))

        def narrow_of(k):
            return narrow[k * half : (k + 1) * half]

        tiles = []
        for at in range(3):
            tile = jnp.where(lower, narrow_of(2 * at), narrow_of(2 * at + 1))
            tiles.append(jnp.where(is_odd_half, roll(tile, columns // 2, 1), tile))
        low_face = jnp.where(core == 0, narrow_of(6), narrow_of(7))
        high_face = jnp.where(core == 0, narrow_of(7), narrow_of(6))
        tiles.append(jnp.where(even_row, high_face, low_face))
        for at in range(2):
            tile = jnp.where(core == 0, tiles[at], tiles[2 + at])
            tile = jnp.where(lax.axis_index("brick") < message.shape[0], tile, roll(tile, columns // 2, 1))
            for c in range(message.shape[0]):
                message[c, at] = tile
        copy.wait()


def same_row(shape):
    half = shape[1] // 2
    lane = iota(shape, 1)
    return ((iota(shape, 0) + lane + lane // half) & 1) == 0


def inner_only(is_odd, inner, q, colour):
    above = is_odd if colour == 0 else jnp.logical_not(is_odd)
    return jnp.where(above, inner, 0.0) if q == 2 else jnp.where(above, 0.0, inner)


def pack_pair(window, at, even, next_one, is_odd):
    window[0][at] = jnp.where(is_odd, next_one, even)
    window[1][at] = jnp.where(is_odd, even, next_one)


def third_kernel(counts, chip, inner, near, far, coarse, packed, message, *rest):
    mass, source, field, rest = rest[0:2], rest[2:4], rest[4:6], rest[6:]
    rows, columns = chip.shape[1:]
    is_odd = odd((rows, columns), plus=my_core())
    for at, (window, start) in enumerate(((field, FIELD), (source, DEFECT), (mass, MASS))):
        side, own, beyond = ([part[start + min(k, 3 if at == 0 else 2)] for k in range(4)] for part in (near, chip, far))
        if at > 0:
            own[3] = inner[at - 1]
        if at == 1:
            side[0] = side[0] + chip[FACE]
            own[0] = own[0] + near[FACE]
            own[3] = own[3] + far[FACE]
            beyond[0] = beyond[0] + inner[2]
        line = side[::-1] + own + beyond
        for q in range(6):
            pack_pair(window, q, line[2 * q], line[2 * q + 1], is_odd)
    source_from_defect(field, mass, source, plus=my_core())
    third_finish(count_of(counts, 2), field, mass, source, coarse, packed, message, *rest)


def third_again_kernel(counts, chip, near, far, *rest):
    mass, source = rest[0:2], rest[2:4]
    coarse, packed, message, *rest = rest[4:]
    field, rest = rest[:2], rest[2:]
    for colour in range(2):
        for k in range(2):
            field[colour][1 - k] = near[2 * colour + k]
            field[colour][2 + k] = chip[2 * colour + k]
            field[colour][4 + k] = far[2 * colour + k]
    third_finish(count_of(counts, 2) - 2, field, mass, source, coarse, packed, message, *rest)


def third_level(part, count, counts):
    groups, chips = lax.axis_size("group"), lax.axis_size("brick") // 2
    tile_rows, columns = part.shape[1:]
    rows = groups * tile_rows
    blocks = [part] + [shifted(part, "group", -d) for d in range(1, groups)]
    (own,) = call(third_prepare_kernel, [(8, rows, columns)], blocks)
    shapes = [(11, rows, columns), (3, rows, columns)]
    chip, inner = call(third_chip_kernel, shapes, [own, swapped_cores(own)])
    near = swapped_chips(chip)
    far = swapped_cores(near)
    window = (6, rows, columns)
    outs = [(2 * rows, columns), (4, rows, columns), (chips, 2, rows // 2, columns)]
    scratch = [window, window, (8 * rows, columns)]
    args = [counts, chip, inner, near, far]
    coarse, packed, message, *fixed = call(third_kernel, outs + [window] * 4, args, scratch, 1)

    def again(given):
        packed = given[1]
        near = swapped_chips(packed)
        args = [counts, packed, near, swapped_cores(near), *fixed]
        return list(call(third_again_kernel, outs, args, scratch, 1))

    done = lax.cond(count > 2, again, lambda given: given, [coarse, packed, message])
    return done[0].reshape(rows, 2, columns), done[2]


def fourth_kernel(counts, own, other, out, *windows):
    field, mass, source, (held, sent) = windows[0:2], windows[2:4], windows[4:6], windows[6:]
    chips, _, rows, columns = own.shape
    tiles, half = chips // 2, columns // 2
    lane = iota((rows, columns), 1)
    low = lane < half
    is_odd = odd((rows, columns))
    first, last = lane % half == 0, lane % half == half - 1

    def turned(value):
        return roll(value, half, 1)

    def beside(value):
        after = jnp.where(last, roll(value, half - 1, 1), roll(value, -1, 1))
        return after + jnp.where(first, roll(value, 1 - half, 1), roll(value, 1, 1))

    def put(window, t, one, two):
        window[0][t + 1] = jnp.where(low, one, two)
        window[1][t + 1] = turned(jnp.where(low, two, one))

    def repeat(window, colour):
        window[colour][0] = turned(window[colour][tiles])
        window[colour][tiles + 1] = turned(window[colour][1])

    def load(one, two):
        even_row = same_row((rows, columns))

        def defect(t):
            before, after = two[(t - 1) % chips, 1], two[(t + 1) % chips, 1]
            before = turned(before) if t in (0, tiles) else before
            after = turned(after) if t in (tiles - 1, chips - 1) else after
            if t < tiles:
                return one[t, 1] + jnp.where(even_row, before, after)
            return one[t, 1] + jnp.where(even_row, after, before)

        for t in range(tiles):
            put(field, t, one[t, 0], one[t + tiles, 0])
            put(mass, t, two[t, 0], two[t + tiles, 0])
            put(source, t, defect(t), defect(t + tiles))

    @pl.when(my_core() == 0)
    def _():
        load(own, other)

    @pl.when(my_core() == 1)
    def _():
        load(other, own)

    for colour in range(2):
        repeat(field, colour)
    source_from_defect(field, mass, source, beside, range(1, tiles + 1))

    def one_sweep(step, carry):
        for colour in range(2):
            half_sweep(field, mass, source, colour, 1, tiles + 1, 16, beside)
            repeat(field, colour)
        return carry

    lax.fori_loop(0, count_of(counts, 3), one_sweep, 0)
    for t in range(tiles):
        red, black = field[0][t + 1], field[1][t + 1]
        red_too, black_too = turned(red), turned(black)
        one = jnp.where(low, jnp.where(is_odd, black, red), jnp.where(is_odd, red_too, black_too))
        two = jnp.where(low, jnp.where(is_odd, black_too, red_too), jnp.where(is_odd, red, black))
        for at, value in ((t, one), (t + tiles, two)):
            held[:, at * columns : (at + 1) * columns] = value
    copy = pltpu.make_async_copy(held, out, sent)
    copy.start()
    copy.wait()


def fourth_level(message, counts):
    chips, _, rows, columns = message.shape
    cores = [[2 * chip + c for chip in range(chips)] for c in range(2)]
    own = lax.all_to_all(message, "brick", 0, 0, axis_index_groups=cores)
    other = swapped_cores(own)
    scratch = [(chips // 2 + 2, rows, columns)] * 6
    (out,) = call(fourth_kernel, [(rows, chips * columns)], [counts, own, other], scratch, 1)
    return out


def on_device(initial_field, mass, source, sweeps):
    counts, ahead, (fine, parts, edge_left, edge_right) = first_level(initial_field, mass, source, sweeps)
    middle, part = second_level(parts, edge_left, edge_right, ahead[1][0], counts)
    coarse, message = third_level(part, ahead[2][0], counts)
    coarsest = fourth_level(message, counts)
    return fine, middle, coarse, coarsest


def solution(mesh):
    return jax.shard_map(
        on_device,
        mesh=mesh,
        in_specs=(
            P("group", "brick", None),
            P("group", "brick", None),
            P("group", "brick", None),
            P(),
        ),
        out_specs=(
            P("group", "brick", None),
            P("group", "brick", None),
            P(None, "brick", None),
            P(),
        ),
        check_vma=False,
    )
```
